32 devices in a mesh: dp: 4 (over x, core), section: 2 (over y), mp: 4 (over z).
Axes of the slice: x: 2, y: 2, z: 4, core: 2. Of those that a mesh axis runs over, the one named last changes fastest.
Arguments:
- inputs: bfloat16 [2, 2048, 1024], P(None, ('dp', 'mp')), may hold values from -6 to 6
- cotangent: bfloat16 [2, 2048, 1024], P(None, ('dp', 'mp')), may hold values from -6 to 6
- doc_ids: int32 [2, 4, 512], P(None, 'dp'), may hold values from 0 to 7, never falling along the last dimension, each value on 1 to 256 neighbouring positions
- w_query: bfloat16 [2, 1024, 1024], P('section', None, 'mp'), may hold values from -0.1875 to 0.1875
- b_query: bfloat16 [2, 1024], P('section', 'mp'), may hold values from -3 to 3
- w_key: bfloat16 [2, 1024, 1024], P('section', None, 'mp'), may hold values from -0.1875 to 0.1875
- w_value: bfloat16 [2, 1024, 1024], P('section', None, 'mp'), may hold values from -0.1875 to 0.1875
- b_value: bfloat16 [2, 1024], P('section', 'mp'), may hold values from -3 to 3
- w_out: bfloat16 [2, 1024, 1024], P('section', 'mp'), may hold values from -0.5 to 0.5
- b_out: bfloat16 [2, 1024], P('section'), may hold values from -2 to 2
- gain_one: bfloat16 [2, 1024], P('section'), may hold values from 0.5 to 1.5
- shift_one: bfloat16 [2, 1024], P('section'), may hold values from -2 to 2
- w_up: bfloat16 [2, 1024, 4096], P('section', None, 'mp'), may hold values from -0.1875 to 0.1875
- b_up: bfloat16 [2, 4096], P('section', 'mp'), may hold values from -3 to 3
- w_down: bfloat16 [2, 4096, 1024], P('section', 'mp'), may hold values from -0.09375 to 0.09375
- b_down: bfloat16 [2, 1024], P('section'), may hold values from -2 to 2
- gain_two: bfloat16 [2, 1024], P('section'), may hold values from 0.5 to 1.5
- shift_two: bfloat16 [2, 1024], P('section'), may hold values from -2 to 2
Outputs:
- section_outputs: bfloat16 [2, 2, 2048, 1024], P('section', None, ('dp', 'mp'))
- section_input_grads: float32 [2, 2, 2048, 1024], P('section', None, ('dp', 'mp'))
- grad_w_query: float32 [2, 1024, 1024], P('section', None, 'mp')
- grad_b_query: float32 [2, 1024], P('section', 'mp')
- grad_w_key: float32 [2, 1024, 1024], P('section', None, 'mp')
- grad_w_value: float32 [2, 1024, 1024], P('section', None, 'mp')
- grad_b_value: float32 [2, 1024], P('section', 'mp')
- grad_w_out: float32 [2, 1024, 1024], P('section', 'mp')
- grad_b_out: float32 [2, 1024], P('section')
- grad_gain_one: float32 [2, 1024], P('section')
- grad_shift_one: float32 [2, 1024], P('section')
- grad_w_up: float32 [2, 1024, 4096], P('section', None, 'mp')
- grad_b_up: float32 [2, 4096], P('section', 'mp')
- grad_w_down: float32 [2, 4096, 1024], P('section', 'mp')
- grad_b_down: float32 [2, 1024], P('section')
- grad_gain_two: float32 [2, 1024], P('section')
- grad_shift_two: float32 [2, 1024], P('section')
The draws below stay inside these ranges and needn't reach their ends.
Inputs may be any that keep to these rules, and one draw needn't show every extreme that they name: `doc_ids`: within each row of 512 tokens the ids never fall.
All inputs are finite; a program needn't handle non-finite values.
Results may differ from the reference program's by a relative error of at most 0.03.
Values may be sent and summed in bfloat16 or wider, within the bound.
No kernel may reach another device: no remote copies, remote signals or barrier semaphores. Data moves between devices by JAX's collectives and lax.ppermute only.
A program may use at most 128 MiB of HBM per device.

```python
import math
import jax
import jax.numpy as jnp
import numpy as np
from jax import lax

D = 1024
H = 16
HD = 64
FF = 4096
SEQ = 512
MICRO = 2
ROWS_MB = 1
ROWS_ALL = 4
TOKMB = 2048
N_DP = 4


def strengthened(array, own_key, source, target, blocks, factor):
    def block_of(position):
        return (jnp.arange(array.shape[position]) // (array.shape[position] // blocks)).reshape((-1,) + (1,) * (array.ndim - 1 - position))

    one_side = jax.random.permutation(own_key, blocks)[block_of(target)]
    second = (block_of(target) + blocks // 2) % blocks
    return jnp.where((block_of(source) == one_side) | (block_of(source) == second), factor * array, array)


def level_of(rng, dims, pieces, smallest, top_value):
    factor_of, own = 1.0, jax.random.fold_in(rng, 6)
    for dim, shards_of in pieces:
        steps = jnp.exp(jax.random.uniform(jax.random.fold_in(own, dim), (shards_of,), jnp.float32, smallest / len(pieces), top_value / len(pieces)))
        factor_of = factor_of * jnp.repeat(steps, dims[dim] // shards_of).reshape([-1 if axis == dim else 1 for axis in range(len(dims))])
    return factor_of


def length_profile(amount, total, most, skew):
    portions = [(1 << 20) // math.isqrt(standing ** skew) + 1 for standing in range(2, amount + 1)]
    rest, holding = total - most - (amount - 1), [1] * (amount - 1)
    while rest > 0:
        free = [i for i in range(amount - 1) if holding[i] < most]
        whole, left = sum([portions[i] for i in free]), rest
        for i in free:
            more = min(most - holding[i], max(1, left * portions[i] // whole), rest)
            holding[i] = holding[i] + more
            rest = rest - more
    return np.array([most] + holding)


def uneven(stream_key, amount, total, bound, lean):
    if amount == 2:
        one = jax.random.randint(stream_key, (), max(1, total - bound), min(bound, total - 1) + 1)
        return jnp.stack([one, total - one])
    sizes = jnp.asarray(length_profile(amount, total, bound, lean), jnp.int32)
    couples = (amount - 1) // 2
    source_of, receiver = sizes[1:1 + 2 * couples:2], sizes[2:2 + 2 * couples:2]
    slack = jnp.minimum(source_of - 1, bound - receiver)
    passed = jax.random.randint(jax.random.fold_in(stream_key, 1), (couples,), 0, 1 << 20) % (slack + 1)
    sizes = sizes.at[1:1 + 2 * couples:2].set(source_of - passed).at[2:2 + 2 * couples:2].set(receiver + passed)
    return sizes[jax.random.permutation(jax.random.fold_in(stream_key, 2), amount)]


def noise(own_key, extent, deviation, reach, pieces=(), dtype=jnp.bfloat16):
    array = deviation * jax.random.normal(own_key, extent, jnp.float32)
    if pieces:
        array = array * level_of(own_key, extent, pieces, -0.22, 0.18)
    return jnp.clip(array, -reach, reach).astype(dtype)


def heavy_noise(rng, extent, deviation, reach, cuts, heavy, dtype=jnp.bfloat16):
    result = deviation * jax.random.normal(rng, extent, jnp.float32)
    if cuts:
        result = result * level_of(rng, extent, cuts, -0.22, 0.18)
    return jnp.clip(strengthened(result, jax.random.fold_in(rng, 3), *heavy), -reach, reach).astype(dtype)


def setup_inputs(seed: int = 0) -> dict:
    streams_of = jax.random.split(jax.random.key(seed), 19)
    inputs = noise(streams_of[0], (MICRO, TOKMB, D), 1.0, 6.0, ((1, 16),))
    cotangent = heavy_noise(streams_of[1], (MICRO, TOKMB, D), 1.0, 6.0, ((1, 16),), (1, 2, 16, 2.0))
    doc_ids = jax.vmap(lambda own: jnp.searchsorted(jnp.cumsum(uneven(own, max(SEQ // 64, 4), SEQ, SEQ // 2, 0)), jnp.arange(SEQ), side="right"))(jax.random.split(streams_of[2], MICRO * ROWS_ALL)).reshape((MICRO, ROWS_ALL, SEQ)).astype(jnp.int32)
    w_query = noise(streams_of[3], (2, D, H * HD), D ** -0.5, 0.1875, ((0, 2), (2, 4)))
    b_query = noise(streams_of[4], (2, H * HD), 0.5, 3.0, ((0, 2), (1, 4)))
    w_key = noise(streams_of[5], (2, D, H * HD), D ** -0.5, 0.1875, ((0, 2), (2, 4)))
    w_value = noise(streams_of[6], (2, D, H * HD), D ** -0.5, 0.1875, ((0, 2), (2, 4)))
    b_value = noise(streams_of[7], (2, H * HD), 0.5, 3.0, ((0, 2), (1, 4)))
    w_out = noise(streams_of[8], (2, H * HD, D), (H * HD // 8) ** -0.5, 0.5, ((0, 2), (1, 4)))
    b_out = noise(streams_of[9], (2, D), 0.3, 2.0, ((0, 2),))
    gain_one = jnp.clip(1.0 + 0.1 * jax.random.normal(streams_of[10], (2, D), jnp.float32), 0.5, 1.5).astype(jnp.bfloat16)
    shift_one = noise(streams_of[11], (2, D), 0.3, 2.0, ((0, 2),))
    w_up = noise(streams_of[12], (2, D, FF), D ** -0.5, 0.1875, ((0, 2), (2, 4)))
    b_up = noise(streams_of[13], (2, FF), 0.5, 3.0, ((0, 2), (1, 4)))
    w_down = noise(streams_of[14], (2, FF, D), FF ** -0.5, 0.09375, ((0, 2), (1, 4)))
    b_down = noise(streams_of[15], (2, D), 0.3, 2.0, ((0, 2),))
    gain_two = jnp.clip(1.0 + 0.1 * jax.random.normal(streams_of[16], (2, D), jnp.float32), 0.5, 1.5).astype(jnp.bfloat16)
    shift_two = noise(streams_of[17], (2, D), 0.3, 2.0, ((0, 2),))
    return dict(inputs=inputs, cotangent=cotangent, doc_ids=doc_ids, w_query=w_query, b_query=b_query, w_key=w_key, w_value=w_value, b_value=b_value, w_out=w_out, b_out=b_out, gain_one=gain_one, shift_one=shift_one, w_up=w_up, b_up=b_up, w_down=w_down, b_down=b_down, gain_two=gain_two, shift_two=shift_two)


EPSILON = 1e-05
NEGATIVE = -1e+30

@jax.custom_vjp
def low(v):
    return lax.optimization_barrier(v.astype(jnp.bfloat16)).astype(jnp.float32)

@jax.custom_vjp
def low_back(v):
    return v

def low_keep(v):
    return (low(v), None)

def low_pass(kept, grad):
    return (grad,)

def back_keep(v):
    return (v, None)

def back_low(kept, grad):
    return (low(grad),)
low.defvjp(low_keep, low_pass)
low_back.defvjp(back_keep, back_low)

def both_round(values):
    return low_back(low(values))

def project(left, right):
    return jnp.einsum('rsd,de->rse', left, right, precision=lax.Precision.HIGHEST)

def normalize(hidden, gain, offset):
    centre = lax.optimization_barrier(jnp.mean(hidden, -1, keepdims=True))
    centred = hidden - centre
    variance = lax.optimization_barrier(jnp.mean(centred * centred, -1, keepdims=True))
    return centred * lax.rsqrt(variance + EPSILON) * gain + offset

def layer_apply(layer_input, weights, allowed):
    w_query, b_query, w_key, w_value, b_value, w_out, b_out, gain_one, shift_one, w_up, b_up, w_down, b_down, gain_two, shift_two = weights
    batch_rows = layer_input.shape[0]
    input_low = low(layer_input)
    query_rows = both_round(project(input_low, w_query) + b_query).reshape(batch_rows, SEQ, H, HD)
    key_rows = both_round(project(input_low, w_key)).reshape(batch_rows, SEQ, H, HD)
    value_rows = both_round(project(input_low, w_value) + b_value).reshape(batch_rows, SEQ, H, HD)
    scores = jnp.einsum('rqhd,rkhd->rhqk', query_rows, key_rows, precision=lax.Precision.HIGHEST) * HD ** (-0.5)
    scores = low_back(scores)
    scores = jnp.where(allowed[:, None], scores, NEGATIVE)
    probs_low = low(jax.nn.softmax(scores, axis=-1))
    mixed = jnp.einsum('rhqk,rkhd->rqhd', probs_low, value_rows, precision=lax.Precision.HIGHEST)
    mixed = both_round(mixed.reshape(batch_rows, SEQ, H * HD))
    attended = low_back(project(mixed, w_out) + b_out)
    middle = normalize(layer_input + attended, gain_one, shift_one)
    hidden_up = low_back(project(low(middle), w_up) + b_up)
    activated = low(jax.nn.gelu(hidden_up, approximate=False))
    lowered = low_back(project(activated, w_down) + b_down)
    return normalize(middle + lowered, gain_two, shift_two)

def reference(inputs, cotangent, doc_ids, w_query, b_query, w_key, w_value, b_value, w_out, b_out, gain_one, shift_one, w_up, b_up, w_down, b_down, gain_two, shift_two):
    rows_total = MICRO * ROWS_MB * N_DP
    group = math.gcd(rows_total, max(1, 4096 // SEQ))
    params = tuple((w.astype(jnp.float32) for w in (w_query, b_query, w_key, w_value, b_value, w_out, b_out, gain_one, shift_one, w_up, b_up, w_down, b_down, gain_two, shift_two)))
    rows_in = inputs.astype(jnp.float32).reshape(rows_total // group, group, SEQ, D)
    rows_grad = cotangent.astype(jnp.float32).reshape(rows_total // group, group, SEQ, D)
    rows_ids = doc_ids.reshape(rows_total // group, group, SEQ)
    zero_grads = tuple((jnp.zeros(p.shape, jnp.float32) for p in params))

    def group_step(totals, item):
        group_in, group_grad, group_ids = item
        allowed = group_ids[:, :, None] == group_ids[:, None, :]
        probe = jnp.zeros(group_in.shape, jnp.float32)

        def forward(weights, layer_input, added):
            first_out = layer_apply(layer_input, tuple((w[0] for w in weights)), allowed)
            between = low_back(low(first_out)) + added
            second_out = layer_apply(between, tuple((w[1] for w in weights)), allowed)
            return (first_out, second_out)
        (first_out, second_out), pull = jax.vjp(forward, params, group_in, probe)
        grad_params, grad_input, grad_probe = pull((jnp.zeros(first_out.shape, jnp.float32), group_grad))
        totals = jax.tree.map(jnp.add, totals, grad_params)
        return (totals, (first_out.astype(jnp.bfloat16), second_out.astype(jnp.bfloat16), grad_input, grad_probe))
    totals, (firsts, seconds, grads_first, grads_second) = lax.scan(group_step, zero_grads, (rows_in, rows_grad, rows_ids))
    layout = (MICRO, ROWS_MB * SEQ * N_DP, D)
    section_outputs = jnp.stack([firsts.reshape(layout), seconds.reshape(layout)])
    section_input_grads = jnp.stack([grads_first.reshape(layout), grads_second.reshape(layout)])
    return (section_outputs, section_input_grads, totals[0], totals[1], totals[2], totals[3], totals[4], totals[5], totals[6], totals[7], totals[8], totals[9], totals[10], totals[11], totals[12], totals[13], totals[14])
```

```python
from functools import partial

import jax
import jax.numpy as jnp
from jax import lax
from jax.sharding import PartitionSpec as P

HD = 64
SEQ = 512
SHARE = 128
AXES = ("dp", "section", "mp")
EPSILON = 1e-05
NEGATIVE = -1e30
F32 = jnp.float32
BF16 = jnp.bfloat16


def dot_nt(left, right):
    return lax.dot_general(left, right, (((1,), (1,)), ((), ())), preferred_element_type=F32)


def dot_nn(left, right):
    return lax.dot_general(left, right, (((1,), (0,)), ((), ())), preferred_element_type=F32)


def dot_tn(left, right):
    return lax.dot_general(left, right, (((0,), (0,)), ((), ())), preferred_element_type=F32)


def mover(sizes, target, takes=None):
    replicas, sections, shards = sizes
    pairs = []
    for d in range(replicas):
        for s in range(sections):
            for z in range(shards):
                if takes is None or takes(d, s, z):
                    nd, ns, nz = target(d, s, z)
                    pairs.append(
                        ((d * sections + s) * shards + z, (nd * sections + ns) * shards + nz)
                    )

    def move(values):
        return lax.ppermute(values, AXES, pairs)

    return move


def norm_forward(hidden, gain, offset):
    centre = jnp.mean(hidden, -1, keepdims=True)
    centred = hidden - centre
    variance = jnp.mean(centred * centred, -1, keepdims=True)
    inverse = lax.rsqrt(variance + EPSILON)
    normed = centred * inverse
    return (normed * gain + offset, normed, inverse)


def norm_backward(upstream, normed, inverse, gain):
    scaled = upstream * gain
    return inverse * (
        scaled
        - jnp.mean(scaled, -1, keepdims=True)
        - normed * jnp.mean(scaled * normed, -1, keepdims=True)
    )


def layer_forward(share, weights, allowed, gather, scatter):
    wide = share.astype(F32)
    low = share.astype(BF16)
    whole = gather(low)
    rows = jnp.einsum("td,zaed->azte", whole, weights["qkv"], preferred_element_type=F32)
    rows = (rows + weights["b_qkv"][:, :, None, :]).astype(BF16)
    query, key, value = rows[0], rows[1], rows[2]
    scores = jnp.einsum("zqe,zke->zqk", query, key, preferred_element_type=F32) * HD ** (-0.5)
    scores = jnp.where(allowed[None], scores, NEGATIVE)
    exponent = jnp.exp(scores - jnp.max(scores, -1, keepdims=True))
    probs = exponent / jnp.sum(exponent, -1, keepdims=True)
    probs_low = probs.astype(BF16)
    mixed = jnp.einsum("zqk,zke->zqe", probs_low, value, preferred_element_type=F32).astype(BF16)
    attended = scatter(
        jnp.einsum("zte,zed->td", mixed, weights["out"], preferred_element_type=F32)
    )
    middle, normed_one, inverse_one = norm_forward(
        wide + attended + weights["b_out"], weights["gain_one"], weights["shift_one"]
    )
    spread = gather(middle.astype(BF16))
    hidden = [dot_nt(spread, up) + bias for up, bias in zip(weights["up"], weights["b_up"])]
    active = [jax.nn.gelu(h, approximate=False).astype(BF16) for h in hidden]
    lowered = scatter(
        dot_nn(active[0], weights["down"][0]) + dot_nn(active[1], weights["down"][1])
    )
    result, normed_two, inverse_two = norm_forward(
        middle + lowered + weights["b_down"], weights["gain_two"], weights["shift_two"]
    )
    kept = (
        whole,
        query,
        key,
        value,
        probs,
        mixed,
        normed_one,
        inverse_one,
        spread,
        hidden,
        active,
        normed_two,
        inverse_two,
    )
    return (result, kept)


def layer_backward(upstream, weights, kept, gather, scatter):
    (
        whole,
        query,
        key,
        value,
        probs,
        mixed,
        normed_one,
        inverse_one,
        spread,
        hidden,
        active,
        normed_two,
        inverse_two,
    ) = kept
    d_gain_two = jnp.sum(upstream * normed_two, 0)
    d_shift_two = jnp.sum(upstream, 0)
    d_sum_two = norm_backward(upstream, normed_two, inverse_two, weights["gain_two"])
    low_two = d_sum_two.astype(BF16)
    d_b_down = jnp.sum(low_two.astype(F32), 0)
    d_lowered = gather(low_two)
    d_hidden, d_down, d_up, d_b_up = [], [], [], []
    for h in range(2):
        d_active = dot_nt(d_lowered, weights["down"][h])
        pull = jax.vjp(partial(jax.nn.gelu, approximate=False), hidden[h])[1]
        d_hidden.append(pull(d_active)[0].astype(BF16))
        d_down.append(dot_tn(active[h], d_lowered))
        d_up.append(dot_tn(d_hidden[h], spread))
        d_b_up.append(jnp.sum(d_hidden[h].astype(F32), 0))
    d_middle = d_sum_two + scatter(
        dot_nn(d_hidden[0], weights["up"][0]) + dot_nn(d_hidden[1], weights["up"][1])
    )
    d_gain_one = jnp.sum(d_middle * normed_one, 0)
    d_shift_one = jnp.sum(d_middle, 0)
    d_sum_one = norm_backward(d_middle, normed_one, inverse_one, weights["gain_one"])
    low_one = d_sum_one.astype(BF16)
    d_b_out = jnp.sum(low_one.astype(F32), 0)
    d_attended = gather(low_one)
    d_out = jnp.einsum("zte,td->zed", mixed, d_attended, preferred_element_type=F32)
    d_mixed = jnp.einsum(
        "td,zed->zte", d_attended, weights["out"], preferred_element_type=F32
    ).astype(BF16)
    d_probs = jnp.einsum("zqe,zke->zqk", d_mixed, value, preferred_element_type=F32)
    d_scores = (probs * (d_probs - jnp.sum(probs * d_probs, -1, keepdims=True))).astype(BF16)
    scale = HD ** (-0.5)
    d_query = jnp.einsum("zqk,zke->zqe", d_scores, key, preferred_element_type=F32) * scale
    d_key = jnp.einsum("zqk,zqe->zke", d_scores, query, preferred_element_type=F32) * scale
    d_value = jnp.einsum(
        "zqk,zqe->zke", probs.astype(BF16), d_mixed, preferred_element_type=F32
    )
    d_rows = jnp.stack([d_query, d_key, d_value]).astype(BF16)
    d_qkv = jnp.einsum("azte,td->zaed", d_rows, whole, preferred_element_type=F32)
    d_b_qkv = jnp.sum(d_rows.astype(F32), 2)
    d_input = d_sum_one + scatter(
        jnp.einsum("azte,zaed->td", d_rows, weights["qkv"], preferred_element_type=F32)
    )
    vectors = jnp.stack([d_b_out, d_gain_one, d_shift_one, d_b_down, d_gain_two, d_shift_two])
    return (d_input, d_qkv, d_b_qkv, d_out, d_up, d_b_up, d_down, vectors)


def solution(mesh):
    replicas, sections, shards = (mesh.shape[name] for name in AXES)
    sizes = (replicas, sections, shards)

    def quarter_of(d, s):
        return 2 * ((d >> 1) & 1) + s

    swap_y = mover(sizes, lambda d, s, z: (d, s ^ 1, z))
    swap_x = mover(sizes, lambda d, s, z: (d ^ 2, s, z))
    swap_xy = mover(sizes, lambda d, s, z: (d ^ 2, s ^ 1, z))
    swap_core = mover(sizes, lambda d, s, z: (d ^ 1, s, z))
    swap_z = [mover(sizes, lambda d, s, z, r=r: (d, s, z ^ r)) for r in range(1, 4)]
    place_in = mover(
        sizes,
        lambda d, s, z: (
            (d & ~2) | ((z >> 1) << 1),
            z & 1,
            2 * (s ^ (z & 1)) + ((d >> 1) & 1),
        ),
    )
    place_out = [
        mover(
            sizes,
            lambda d, s, z, r=r: (
                (d & ~2) | ((z & 1) << 1),
                (z >> 1) ^ r,
                quarter_of(d, s),
            ),
        )
        for r in range(2)
    ]

    def gather(share):
        return jnp.concatenate([share, swap_y(share), swap_x(share), swap_xy(share)])

    def scatter(part):
        low = part.astype(BF16).reshape(4, SHARE, -1)
        own = part[:SHARE]
        return (
            own
            + swap_y(low[1]).astype(F32)
            + swap_x(low[2]).astype(F32)
            + swap_xy(low[3]).astype(F32)
        )

    def gather_z(piece):
        return jnp.stack([piece] + [move(piece) for move in swap_z])

    def scatter_z(pieces):
        total = pieces[0].astype(F32)
        for r in range(1, 4):
            total = total + swap_z[r - 1](pieces[r]).astype(F32)
        return total

    def to_layers(first, second, section):
        pick = (lax.axis_index("mp") >> 1) == 0
        moved_a = place_out[0](jnp.where(pick, first, second))
        moved_b = place_out[1](jnp.where(pick, second, first))
        is_first = section == 0
        return jnp.stack(
            [jnp.where(is_first, moved_a, moved_b), jnp.where(is_first, moved_b, moved_a)]
        )

    def per_device(
        inputs,
        cotangent,
        doc_ids,
        w_query,
        b_query,
        w_key,
        w_value,
        b_value,
        w_out,
        b_out,
        gain_one,
        shift_one,
        w_up,
        b_up,
        w_down,
        b_down,
        gain_two,
        shift_two,
    ):
        replica = lax.axis_index("dp")
        section = lax.axis_index("section")
        shard = lax.axis_index("mp")
        core = replica & 1
        quarter = quarter_of(replica, section)

        which = (section ^ shard) & 1
        share_in = place_in(lax.dynamic_index_in_dim(inputs, which, 0, False))
        share_grad = place_in(lax.dynamic_index_in_dim(cotangent, which, 0, False))
        other_ids = swap_x(doc_ids)
        mine = ((replica >> 1) & 1) == (shard & 1)
        ids = jnp.where(mine, doc_ids, other_ids)
        ids = lax.dynamic_index_in_dim(ids, shard >> 1, 0, False).reshape(4, SHARE)
        ids = jnp.concatenate(
            [lax.dynamic_index_in_dim(ids, quarter ^ r, 0, False) for r in range(4)]
        )
        allowed = ids[:, None] == ids[None, :]

        layer_vectors = jnp.concatenate(
            [b_out, gain_one, shift_one, b_down, gain_two, shift_two]
        )

        def attn_pack(block):
            head = block * HD + core * 32
            columns = [
                lax.dynamic_slice_in_dim(w[0], head, 32, 1).T for w in (w_query, w_key, w_value)
            ]
            small = jnp.concatenate(
                [
                    lax.dynamic_slice_in_dim(b_query[0], head, 32),
                    lax.dynamic_slice_in_dim(b_value[0], head, 32),
                    lax.dynamic_slice_in_dim(b_up[0], block * 256 + core * 128, 128),
                    jnp.zeros((1024 - 192,), BF16),
                ]
            )[None]
            return jnp.concatenate(
                columns
                + [
                    lax.dynamic_slice_in_dim(w_out[0], head, 32, 0),
                    small,
                    layer_vectors,
                    jnp.zeros((9, 1024), BF16),
                ]
            )

        def ffn_pack(block):
            unit = block * 256 + core * 128
            return jnp.concatenate(
                [
                    lax.dynamic_slice_in_dim(w_up[0], unit, 128, 1).T,
                    lax.dynamic_slice_in_dim(w_down[0], unit, 128, 0),
                ]
            )

        packs = []
        for make in (attn_pack, ffn_pack):
            own = make(quarter)
            received = swap_y(make(quarter ^ 1))
            packs.append((own, received))
        layers = []
        for layer in range(2):
            attn, ffn = (jnp.where(section == layer, own, other) for own, other in packs)
            vectors = attn[129:135].astype(F32)
            attn_own = gather_z(attn[:144])
            attn_other = swap_core(attn_own)
            ffn_own = gather_z(ffn)
            ffn_other = swap_core(ffn_own)
            heads = jnp.concatenate(
                [attn_own[:, :128].reshape(4, 4, 32, 1024), attn_other[:, :128].reshape(4, 4, 32, 1024)],
                2,
            )
            biases = [a[:, 128].astype(F32) for a in (attn_own, attn_other)]
            zero = jnp.zeros((4, HD), F32)
            layers.append(
                dict(
                    qkv=heads[:, :3],
                    out=heads[:, 3],
                    b_qkv=jnp.stack(
                        [
                            jnp.concatenate([b[:, :32] for b in biases], 1),
                            zero,
                            jnp.concatenate([b[:, 32:64] for b in biases], 1),
                        ]
                    ),
                    up=[f[:, :128].reshape(512, 1024) for f in (ffn_own, ffn_other)],
                    down=[f[:, 128:].reshape(512, 1024) for f in (ffn_own, ffn_other)],
                    b_up=[b[:, 64:192].reshape(512) for b in biases],
                    b_out=vectors[0],
                    gain_one=vectors[1],
                    shift_one=vectors[2],
                    b_down=vectors[3],
                    gain_two=vectors[4],
                    shift_two=vectors[5],
                )
            )

        first, kept_first = layer_forward(share_in, layers[0], allowed, gather, scatter)
        first = first.astype(BF16)
        second, kept_second = layer_forward(first, layers[1], allowed, gather, scatter)
        second = second.astype(BF16)
        section_outputs = to_layers(first, second, section)[None]

        upstream = share_grad.astype(F32)
        reduced = [None, None]
        all_vectors = [None, None]
        grads_in = [None, None]
        for layer, kept in ((1, kept_second), (0, kept_first)):
            d_input, d_qkv, d_b_qkv, d_out, d_up, d_b_up, d_down, vectors = layer_backward(
                upstream, layers[layer], kept, gather, scatter
            )
            grads_in[layer] = d_input.astype(BF16)
            upstream = grads_in[layer].astype(F32)
            all_vectors[layer] = vectors
            heads = jnp.concatenate([d_qkv, d_out[:, None]], 1).reshape(4, 4, 2, 32, 1024)
            halves = []
            for half in range(2):
                small = jnp.concatenate(
                    [
                        d_b_qkv[0][:, 32 * half : 32 * half + 32],
                        d_b_qkv[2][:, 32 * half : 32 * half + 32],
                        d_b_up[half].reshape(4, 128),
                        jnp.zeros((4, 1024 - 192), F32),
                    ],
                    1,
                )[:, None]
                halves.append(
                    jnp.concatenate(
                        [
                            heads[:, :, half].reshape(4, 128, 1024),
                            small,
                            jnp.zeros((4, 15, 1024), F32),
                            d_up[half].reshape(4, 128, 1024),
                            d_down[half].reshape(4, 128, 1024),
                        ],
                        1,
                    )
                )
            half_sum = (halves[0] + swap_core(halves[1].astype(BF16)).astype(F32)).astype(BF16)
            reduced[layer] = scatter_z(half_sum).astype(BF16)

        if replicas > 4:
            groups = [[low + 4 * high for high in range(replicas // 4)] for low in range(4)]
            reduced = [
                lax.psum(part, "dp", axis_index_groups=groups).astype(BF16) for part in reduced
            ]
        mine = jnp.where(section == 0, reduced[0], reduced[1])
        theirs = jnp.where(section == 0, reduced[1], reduced[0])
        pieces = jnp.stack([mine, swap_y(theirs), swap_x(mine), swap_xy(theirs)])
        pieces = jnp.stack([pieces, swap_core(pieces)])
        pieces = lax.dynamic_index_in_dim(
            jnp.stack([pieces, pieces[::-1]]), core, 0, False
        )
        ordered = jnp.stack(
            [lax.dynamic_index_in_dim(pieces, quarter ^ r, 1, False) for r in range(4)]
        ).astype(F32)
        heads = ordered[:, :, :128].reshape(4, 2, 4, 32, 1024).transpose(2, 0, 1, 3, 4)
        heads = heads.reshape(4, 256, 1024)
        small = ordered[:, :, 128]
        g_up = ordered[:, :, 144:272].reshape(1024, 1024).T
        g_down = ordered[:, :, 272:400].reshape(1024, 1024)
        vectors = lax.psum(jnp.stack(all_vectors), AXES)
        vectors = lax.dynamic_index_in_dim(vectors, section, 0, True)
        section_input_grads = to_layers(grads_in[0], grads_in[1], section)[None].astype(F32)
        return (
            section_outputs,
            section_input_grads,
            heads[0].T[None],
            small[:, :, :32].reshape(1, 256),
            heads[1].T[None],
            heads[2].T[None],
            small[:, :, 32:64].reshape(1, 256),
            heads[3][None],
            vectors[:, 0],
            vectors[:, 1],
            vectors[:, 2],
            g_up[None],
            small[:, :, 64:192].reshape(1, 1024),
            g_down[None],
            vectors[:, 3],
            vectors[:, 4],
            vectors[:, 5],
        )

    vector = P("section", None)
    columns = P("section", None, "mp")
    rows = P("section", "mp", None)
    spread = P("section", "mp")
    tokens = P(None, ("dp", "mp"), None)
    layer_tokens = P("section", None, ("dp", "mp"), None)
    return jax.shard_map(
        per_device,
        mesh=mesh,
        in_specs=(
            tokens,
            tokens,
            P(None, "dp", None),
            columns,
            spread,
            columns,
            columns,
            spread,
            rows,
            vector,
            vector,
            vector,
            columns,
            spread,
            rows,
            vector,
            vector,
            vector,
        ),
        out_specs=(
            layer_tokens,
            layer_tokens,
            columns,
            spread,
            columns,
            columns,
            spread,
            rows,
            vector,
            vector,
            vector,
            columns,
            spread,
            rows,
            vector,
            vector,
            vector,
        ),
        check_vma=False,
    )
```

```python
from functools import partial

import jax
import jax.numpy as jnp
from jax import lax
from jax.experimental import pallas as pl
from jax.experimental.pallas import tpu as pltpu
from jax.sharding import PartitionSpec as P

HD = 64
SEQ = 512
SHARE = 128
WIDE = 1024
HEADS = 4
HALF = 32
ATTN = 144
FEED = 272
AXES = ("dp", "section", "mp")
EPSILON = 1e-05
NEGATIVE = -1e30
F32 = jnp.float32
BF16 = jnp.bfloat16
VMEM = pl.BlockSpec(memory_space=pltpu.VMEM)
ANY = pl.BlockSpec(memory_space=pl.ANY)
SMEM = pl.BlockSpec(memory_space=pltpu.SMEM)


def dot_nt(left, right):
    return lax.dot_general(left, right, (((1,), (1,)), ((), ())), preferred_element_type=F32)


def dot_nn(left, right):
    return lax.dot_general(left, right, (((1,), (0,)), ((), ())), preferred_element_type=F32)


def dot_tn(left, right):
    return lax.dot_general(left, right, (((0,), (0,)), ((), ())), preferred_element_type=F32)


def shape(dims, dtype=BF16):
    return jax.ShapeDtypeStruct(dims, dtype)


def call(kernel, name, ins, outs, scratch=(), flops=0, moved=0, limit=40):
    return pl.pallas_call(
        kernel,
        name=name,
        in_specs=ins,
        out_specs=tuple(VMEM for _ in outs),
        out_shape=tuple(outs),
        scratch_shapes=list(scratch),
        compiler_params=pltpu.CompilerParams(vmem_limit_bytes=limit << 20),
        cost_estimate=pl.CostEstimate(flops=flops, bytes_accessed=moved, transcendentals=0),
    )


def at_rows(rows, values):
    place = lax.broadcasted_iota(jnp.int32, (rows, values[0].shape[1]), 0)
    block = jnp.zeros((rows, values[0].shape[1]), F32)
    for i, value in enumerate(values):
        block = jnp.where(place == i, value, block)
    return block


def columns(i, width=256):
    return pl.ds(pl.multiple_of(i * width, width), width)


def prep_attn_kernel(place, wq, wk, wv, wo, bq, bv, v0, v1, v2, v3, v4, v5, own, peer, turned):
    core, quarter = place[0], place[1]
    for a, w in enumerate((wq, wk, wv)):
        turned[a] = w[0].T
    layer_rows = [v[...].astype(F32) for v in (v0, v1, v2, v3, v4, v5)]
    source = lax.broadcasted_iota(jnp.int32, (256, 128), 0)
    lane = lax.broadcasted_iota(jnp.int32, (256, 128), 1)
    for out, block in ((own, quarter), (peer, quarter ^ 1)):
        head = pl.multiple_of(block * HD + core * HALF, HALF)
        for a in range(3):
            out[HALF * a : HALF * a + HALF] = turned[a, pl.ds(head, HALF)]
        out[3 * HALF : 4 * HALF] = wo[0, pl.ds(head, HALF)]
        inner = lane & 63
        wanted = block * HD + (inner ^ (core * HALF))
        hit = source == wanted
        zero = jnp.zeros((256, 128), F32)
        one = jnp.ones((256, 128), F32)
        first = jnp.where(hit & (lane < 64), one, zero).astype(BF16)
        second = jnp.where(hit & (lane >= 64), one, zero).astype(BF16)
        bias = dot_nn(jnp.broadcast_to(bq[...], (16, 256)), first) + dot_nn(
            jnp.broadcast_to(bv[...], (16, 256)), second
        )
        rows = lax.broadcasted_iota(jnp.int32, (16, WIDE), 0)
        block_rows = jnp.zeros((16, WIDE), F32)
        for i, row in enumerate(layer_rows):
            block_rows = jnp.where(rows == i + 1, row, block_rows)
        out[128:144] = block_rows.astype(BF16)
        first_row = lax.broadcasted_iota(jnp.int32, (16, 128), 0) == 0
        out[128:144, 0:128] = jnp.where(first_row, bias, block_rows[:, 0:128]).astype(BF16)


def prep_feed_kernel(place, up, down, bu, own, peer, column, sems):
    core, quarter = place[0], place[1]
    copies = []
    for i, block in enumerate((quarter, quarter ^ 1)):
        unit = pl.multiple_of(block * 256 + core * 128, 128)
        copy = pltpu.make_async_copy(up.at[0, :, pl.ds(unit, 128)], column.at[i], sems.at[2 * i])
        copy.start()
        out = (own, peer)[i]
        other = pltpu.make_async_copy(
            down.at[0, pl.ds(unit, 128)], out.at[128:256], sems.at[2 * i + 1]
        )
        other.start()
        copies.append((copy, other))
    row = lax.broadcasted_iota(jnp.int32, (16, 128), 0) == 0
    for i, block in enumerate((quarter, quarter ^ 1)):
        out = (own, peer)[i]
        out[256:272] = jnp.zeros((16, WIDE), BF16)
        for h in range(2):
            unit = pl.multiple_of(block * 256 + (core ^ h) * 128, 128)
            piece = bu[:, pl.ds(unit, 128)].astype(F32)
            out[256:272, 128 * h : 128 * h + 128] = jnp.where(row, piece, 0.0).astype(BF16)
        copies[i][0].wait()
        out[0:128] = column[i].T
        copies[i][1].wait()


def layer_rows(ref, *which):
    block = ref[...].astype(F32)
    return [block[i : i + 1] for i in which]


def norm_forward(hidden, gain, offset):
    centre = jnp.mean(hidden, -1, keepdims=True)
    centred = hidden - centre
    variance = jnp.mean(centred * centred, -1, keepdims=True)
    inverse = lax.rsqrt(variance + EPSILON)
    normed = centred * inverse
    return (normed * gain + offset, normed, inverse)


def norm_backward(upstream, normed, inverse, gain):
    scaled = upstream * gain
    return inverse * (
        scaled
        - jnp.mean(scaled, -1, keepdims=True)
        - normed * jnp.mean(scaled * normed, -1, keepdims=True)
    )


def norm_kernel(first, own, r1, r2, r3, residual, vec, result, low, normed, inverse):
    bias, gain, offset = layer_rows(vec, *((1, 2, 3) if first else (4, 5, 6)))
    hidden = residual[...].astype(F32) + (
        own[...] + r1[...].astype(F32) + r2[...].astype(F32) + r3[...].astype(F32)
    ) + bias
    value, normed[...], inverse[...] = norm_forward(hidden, gain, offset)
    result[...] = value
    low[...] = value.astype(BF16)


def sums(*values):
    return at_rows(8, [jnp.sum(v, 0, keepdims=True) for v in values])


def norm_two_back_kernel(upstream, normed, inverse, vec, total, low, vectors):
    grad = upstream[...].astype(F32)
    (gain,) = layer_rows(vec, 5)
    value = norm_backward(grad, normed[...], inverse[...], gain)
    rounded = value.astype(BF16)
    total[...] = value
    low[...] = rounded
    vectors[...] = sums(rounded.astype(F32), grad * normed[...], grad)


def norm_two_back_sum_kernel(
    before, own, r1, r2, r3, normed, inverse, vec, total, low, vectors, given
):
    given[...] = (
        before[...]
        + own[...]
        + r1[...].astype(F32)
        + r2[...].astype(F32)
        + r3[...].astype(F32)
    ).astype(BF16)
    norm_two_back_kernel(given, normed, inverse, vec, total, low, vectors)


def norm_one_back_kernel(before, own, r1, r2, r3, normed, inverse, vec, total, low, vectors):
    grad = (
        before[...]
        + own[...]
        + r1[...].astype(F32)
        + r2[...].astype(F32)
        + r3[...].astype(F32)
    )
    (gain,) = layer_rows(vec, 2)
    value = norm_backward(grad, normed[...], inverse[...], gain)
    rounded = value.astype(BF16)
    total[...] = value
    low[...] = rounded
    vectors[...] = sums(rounded.astype(F32), grad * normed[...], grad)


def load_attn(own, other, weight, sems):
    copies = []
    for half, ref in enumerate((own, other)):
        for a in range(4):
            copies.append(
                pltpu.make_async_copy(
                    ref.at[:, HALF * a : HALF * a + HALF],
                    weight.at[a, :, half],
                    sems.at[half * 4 + a],
                )
            )
    return copies


def join(target, pieces):
    for i, piece in enumerate(pieces):
        target[SHARE * i : SHARE * i + SHARE] = piece[...]


def spread_out(value, where, own, parts):
    own[:, where] = value[0:SHARE]
    for i, part in enumerate(parts):
        part[:, where] = value[SHARE * (i + 1) : SHARE * (i + 2)].astype(BF16)


def attn_kernel(
    x0, x1, x2, x3, a_own, a_other, id_column, id_row,
    own, p1, p2, p3, qkv, probs, mixed,
    weight, small, x_all, sems,
):
    copies = load_attn(a_own, a_other, weight, sems)
    copies.append(pltpu.make_async_copy(a_own.at[:, 128:144], small, sems.at[8]))
    for copy in copies:
        copy.start()
    join(x_all, (x0, x1, x2, x3))
    for copy in copies:
        copy.wait()
    biases = [small[z].astype(F32)[0:1] for z in range(4)]
    bias_of = (
        jnp.concatenate([b[:, 0:64] for b in biases], 1),
        None,
        jnp.concatenate([b[:, 64:128] for b in biases], 1),
    )
    x = x_all[...]
    for a in range(3):
        rows = dot_nt(x, weight[a].reshape(256, WIDE))
        if bias_of[a] is not None:
            rows = rows + bias_of[a]
        qkv[:, 256 * a : 256 * a + 256] = rows.astype(BF16)
    for c in range(2):
        q_rows = slice(256 * c, 256 * c + 256)
        allowed = id_column[q_rows] == id_row[...]
        for h in range(HEADS):
            query = qkv[q_rows, HD * h : HD * h + HD]
            key = qkv[:, 256 + HD * h : 256 + HD * h + HD]
            value = qkv[:, 512 + HD * h : 512 + HD * h + HD]
            scores = jnp.where(allowed, dot_nt(query, key) * HD ** (-0.5), NEGATIVE)
            exponent = jnp.exp(scores - jnp.max(scores, -1, keepdims=True))
            low = (exponent / jnp.sum(exponent, -1, keepdims=True)).astype(BF16)
            probs[h, q_rows] = low
            mixed[q_rows, HD * h : HD * h + HD] = dot_nn(low, value).astype(BF16)
    out = weight[3].reshape(256, WIDE)
    for n in range(4):
        where = slice(256 * n, 256 * n + 256)
        spread_out(dot_nn(mixed[...], out[:, where]), where, own, (p1, p2, p3))


def attn_back_kernel(
    g0, g1, g2, g3, a_own, a_other, qkv, probs,
    own, p1, p2, p3, d_rows,
    weight, g_all, sems,
):
    copies = load_attn(a_own, a_other, weight, sems)
    for copy in copies:
        copy.start()
    join(g_all, (g0, g1, g2, g3))
    for copy in copies:
        copy.wait()
    d_mixed = dot_nt(g_all[...], weight[3].reshape(256, WIDE)).astype(BF16)
    scale = HD ** (-0.5)
    for h in range(HEADS):
        query = qkv[:, HD * h : HD * h + HD]
        key = qkv[:, 256 + HD * h : 256 + HD * h + HD]
        value = qkv[:, 512 + HD * h : 512 + HD * h + HD]
        grad = d_mixed[:, HD * h : HD * h + HD]
        d_key = jnp.zeros((SEQ, HD), F32)
        d_value = jnp.zeros((SEQ, HD), F32)
        for c in range(2):
            q_rows = slice(256 * c, 256 * c + 256)
            low = probs[h, q_rows]
            p = low.astype(F32)
            d_probs = dot_nt(grad[q_rows], value)
            inner = jnp.sum(p * d_probs, -1, keepdims=True)
            d_scores = (p * (d_probs - inner)).astype(BF16)
            d_rows[q_rows, HD * h : HD * h + HD] = (dot_nn(d_scores, key) * scale).astype(BF16)
            d_key = d_key + dot_tn(d_scores, query[q_rows])
            d_value = d_value + dot_tn(low, grad[q_rows])
        d_rows[:, 256 + HD * h : 256 + HD * h + HD] = (d_key * scale).astype(BF16)
        d_rows[:, 512 + HD * h : 512 + HD * h + HD] = d_value.astype(BF16)
    rows = d_rows[...]
    for n in range(4):
        where = slice(256 * n, 256 * n + 256)
        w = weight[0:3, :, :, :, where].reshape(768, 256)
        spread_out(dot_nn(rows, w), where, own, (p1, p2, p3))


def attn_weights_kernel(
    d_rows, mixed, x0, x1, x2, x3, g0, g1, g2, g3, vec_one, vec_two, own, other, x_all, g_all
):
    join(x_all, (x0, x1, x2, x3))
    join(g_all, (g0, g1, g2, g3))
    for a in range(4):
        if a < 3:
            value = dot_tn(d_rows[:, 256 * a : 256 * a + 256], x_all[...])
        else:
            value = dot_tn(mixed[...], g_all[...])
        value = value.astype(BF16).reshape(4, 2, HALF, WIDE)
        own[:, HALF * a : HALF * a + HALF] = value[:, 0]
        other[:, HALF * a : HALF * a + HALF] = value[:, 1]
    total = jnp.sum(d_rows[...].astype(F32), 0, keepdims=True)
    one, two = vec_one[...], vec_two[...]
    vectors = [one[i : i + 1] for i in range(3)] + [two[i : i + 1] for i in range(3)]
    block = at_rows(16, [jnp.zeros((1, WIDE), F32)] + vectors)
    first_row = lax.broadcasted_iota(jnp.int32, (16, 128), 0) == 0
    for half, out in enumerate((own, other)):
        for z in range(4):
            start = HD * z + HALF * half
            bias = jnp.concatenate(
                [
                    total[:, start : start + HALF],
                    total[:, 512 + start : 512 + start + HALF],
                    jnp.zeros((1, 64), F32),
                ],
                1,
            )
            out[z, 128:144] = block.astype(BF16)
            out[z, 128:144, 0:128] = jnp.where(first_row, bias, block[:, 0:128]).astype(BF16)


def load_feed(own, other, up, down, sems):
    ups, downs = [], []
    for half, ref in enumerate((own, other)):
        ups.append(
            pltpu.make_async_copy(
                ref.at[:, 0:128], up.at[4 * half : 4 * half + 4], sems.at[2 * half]
            )
        )
        downs.append(
            pltpu.make_async_copy(
                ref.at[:, 128:256], down.at[4 * half : 4 * half + 4], sems.at[2 * half + 1]
            )
        )
    return ups, downs


def feed_kernel(
    x0, x1, x2, x3, f_own, f_other,
    own, p1, p2, p3, active, slope,
    up, down, small, bias, x_all, sems,
):
    ups, downs = load_feed(f_own, f_other, up, down, sems)
    copies = [pltpu.make_async_copy(f_own.at[:, 256:272], small, sems.at[4])] + ups
    for copy in copies + downs:
        copy.start()
    join(x_all, (x0, x1, x2, x3))
    for copy in copies:
        copy.wait()
    for half in range(2):
        for z in range(4):
            unit = 512 * half + 128 * z
            bias[0:8, unit : unit + 128] = jnp.broadcast_to(
                small[z, :, 128 * half : 128 * half + 128].astype(F32)[0:1], (8, 128)
            )

    def units(i, carry):
        block = up[pl.ds(2 * i, 2)].reshape(256, WIDE)
        hidden = dot_nt(x_all[...], block) + bias[0:1, columns(i)]
        share = 0.5 * (1.0 + lax.erf(hidden * (0.5 ** 0.5)))
        density = jnp.exp(-0.5 * hidden * hidden) * 0.3989422804014327
        active[:, columns(i)] = (hidden * share).astype(BF16)
        slope[:, columns(i)] = (share + hidden * density).astype(BF16)
        return carry

    lax.fori_loop(0, 4, units, 0)
    for copy in downs:
        copy.wait()

    def features(n, carry):
        block = down[:, :, columns(n)].reshape(WIDE, 256)
        spread_out(dot_nn(active[...], block), columns(n), own, (p1, p2, p3))
        return carry

    lax.fori_loop(0, 4, features, 0)


def feed_back_kernel(
    g0, g1, g2, g3, f_own, f_other, slope,
    own, p1, p2, p3, d_hidden,
    up, down, g_all, sems,
):
    ups, downs = load_feed(f_own, f_other, up, down, sems)
    for copy in downs + ups:
        copy.start()
    join(g_all, (g0, g1, g2, g3))
    for copy in downs:
        copy.wait()

    def units(i, carry):
        block = down[pl.ds(2 * i, 2)].reshape(256, WIDE)
        value = dot_nt(g_all[...], block) * slope[:, columns(i)].astype(F32)
        d_hidden[:, columns(i)] = value.astype(BF16)
        return carry

    lax.fori_loop(0, 4, units, 0)
    for copy in ups:
        copy.wait()

    def features(n, carry):
        block = up[:, :, columns(n)].reshape(WIDE, 256)
        spread_out(dot_nn(d_hidden[...], block), columns(n), own, (p1, p2, p3))
        return carry

    lax.fori_loop(0, 4, features, 0)


def feed_weights_kernel(
    d_hidden, active, x0, x1, x2, x3, g0, g1, g2, g3, own, other, x_all, g_all
):
    join(x_all, (x0, x1, x2, x3))
    join(g_all, (g0, g1, g2, g3))
    row = lax.broadcasted_iota(jnp.int32, (16, 128), 0) == 0
    for half, out in enumerate((own, other)):

        def pair(i, carry, half=half, out=out):
            where = columns(2 * half + i)
            value = dot_tn(d_hidden[:, where], x_all[...]).astype(BF16)
            out[pl.ds(2 * i, 2), 0:128] = value.reshape(2, 128, WIDE)
            value = dot_tn(active[:, where], g_all[...]).astype(BF16)
            out[pl.ds(2 * i, 2), 128:256] = value.reshape(2, 128, WIDE)
            return carry

        lax.fori_loop(0, 2, pair, 0)
        total = jnp.sum(d_hidden[:, 512 * half : 512 * half + 512].astype(F32), 0, keepdims=True)
        for z in range(4):
            out[z, 256:272] = jnp.zeros((16, WIDE), BF16)
            out[z, 256:272, 0:128] = jnp.where(row, total[:, 128 * z : 128 * z + 128], 0.0).astype(
                BF16
            )


def finish_attn_kernel(place, pieces, gq, gk, gv, go, small, turned, extra, sems):
    copies = []
    for j in range(4):
        for h in range(2):
            index = place[2 * j + h]
            i = 2 * j + h
            copies.append(
                pltpu.make_async_copy(pieces.at[index, 128:144], extra.at[i], sems.at[4, i])
            )
            for a in range(4):
                copies.append(
                    pltpu.make_async_copy(
                        pieces.at[index, HALF * a : HALF * a + HALF],
                        turned.at[a, j, h],
                        sems.at[a, i],
                    )
                )
    for copy in copies:
        copy.start()
    for copy in copies:
        copy.wait()
    for a, out in enumerate((gq, gk, gv)):
        out[0] = turned[a].reshape(256, WIDE).astype(F32).T
    go[0] = turned[3].reshape(256, WIDE).astype(F32)
    small[...] = extra[...]


def finish_feed_kernel(place, pieces, gu, gd, small, block, sems):
    copies = []
    for i in range(8):
        index = place[i]
        copy = pltpu.make_async_copy(pieces.at[index], block.at[i], sems.at[i])
        copy.start()
        copies.append(copy)
    for i in range(8):
        copies[i].wait()
        gu[0, :, 128 * i : 128 * i + 128] = block[i, 0:128].astype(F32).T
        gd[0, 128 * i : 128 * i + 128] = block[i, 128:256].astype(F32)
        small[i] = block[i, 256:272]


MAC_FEED = 2 * SEQ * WIDE * WIDE
TOKEN = [VMEM] * 4
PARTS = [shape((SHARE, WIDE), F32)] + [shape((SHARE, WIDE))] * 3
DMA = pltpu.SemaphoreType.DMA


def scratch(dims, dtype=BF16):
    return pltpu.VMEM(dims, dtype)


prep_attn = call(
    prep_attn_kernel,
    "pack_attention",
    [SMEM] + [VMEM] * 12,
    [shape((ATTN, WIDE))] * 2,
    [scratch((3, 256, WIDE))],
    moved=4 << 20,
)
prep_feed = call(
    prep_feed_kernel,
    "pack_feed",
    [SMEM, ANY, ANY, VMEM],
    [shape((FEED, WIDE))] * 2,
    [scratch((2, WIDE, 128)), DMA((4,))],
    moved=2 << 20,
)
VEC = VMEM
NORMS = [
    shape((SHARE, WIDE), F32),
    shape((SHARE, WIDE)),
    shape((SHARE, WIDE), F32),
    shape((SHARE, 1), F32),
]
norm_one, norm_two = (
    call(partial(norm_kernel, first), name, [VMEM] * 5 + [VEC], NORMS, moved=3 << 20)
    for first, name in ((True, "norm_one"), (False, "norm_two"))
)
BACKS = [shape((SHARE, WIDE), F32), shape((SHARE, WIDE)), shape((8, WIDE), F32)]
norm_two_back = call(
    norm_two_back_kernel, "norm_two_back", [VMEM] * 3 + [VEC], BACKS, moved=3 << 20
)
norm_two_back_sum = call(
    norm_two_back_sum_kernel,
    "norm_two_back_sum",
    [VMEM] * 7 + [VEC],
    BACKS + [shape((SHARE, WIDE))],
    moved=3 << 20,
)
norm_one_back = call(
    norm_one_back_kernel, "norm_one_back", [VMEM] * 7 + [VEC], BACKS, moved=3 << 20
)
attn_forward = call(
    attn_kernel,
    "attention",
    TOKEN + [ANY, ANY, VMEM, VMEM],
    PARTS + [shape((SEQ, 768)), shape((HEADS, SEQ, SEQ)), shape((SEQ, 256))],
    [
        scratch((4, 4, 2, HALF, WIDE)),
        scratch((4, 16, WIDE)),
        scratch((SEQ, WIDE)),
        DMA((9,)),
    ],
    flops=2 * MAC_FEED,
    moved=8 << 20,
)
attn_backward = call(
    attn_back_kernel,
    "attention_back",
    TOKEN + [ANY, ANY, VMEM, VMEM],
    PARTS + [shape((SEQ, 768))],
    [scratch((4, 4, 2, HALF, WIDE)), scratch((SEQ, WIDE)), DMA((8,))],
    flops=3 * MAC_FEED,
    moved=8 << 20,
)
attn_weights = call(
    attn_weights_kernel,
    "attention_weights",
    [VMEM] * 12,
    [shape((4, ATTN, WIDE))] * 2,
    [scratch((SEQ, WIDE)), scratch((SEQ, WIDE))],
    flops=MAC_FEED,
    moved=6 << 20,
)
FEED_SCRATCH = [scratch((8, 128, WIDE)), scratch((8, 128, WIDE))]
feed_forward = call(
    feed_kernel,
    "feed",
    TOKEN + [ANY, ANY],
    PARTS + [shape((SEQ, WIDE))] * 2,
    FEED_SCRATCH
    + [scratch((4, 16, WIDE)), scratch((8, WIDE), F32), scratch((SEQ, WIDE)), DMA((5,))],
    flops=2 * MAC_FEED,
    moved=9 << 20,
)
feed_backward = call(
    feed_back_kernel,
    "feed_back",
    TOKEN + [ANY, ANY, VMEM],
    PARTS + [shape((SEQ, WIDE))],
    FEED_SCRATCH + [scratch((SEQ, WIDE)), DMA((4,))],
    flops=2 * MAC_FEED,
    moved=9 << 20,
)
feed_weights = call(
    feed_weights_kernel,
    "feed_weights",
    [VMEM] * 10,
    [shape((4, FEED, WIDE))] * 2,
    [scratch((SEQ, WIDE)), scratch((SEQ, WIDE))],
    flops=2 * MAC_FEED,
    moved=9 << 20,
)
finish_attn = call(
    finish_attn_kernel,
    "finish_attention",
    [SMEM, ANY],
    [shape((1, WIDE, 256), F32)] * 3 + [shape((1, 256, WIDE), F32), shape((8, 16, WIDE))],
    [scratch((4, 4, 2, HALF, WIDE)), scratch((8, 16, WIDE)), DMA((5, 8))],
    moved=6 << 20,
)
finish_feed = call(
    finish_feed_kernel,
    "finish_feed",
    [SMEM, ANY],
    [shape((1, WIDE, WIDE), F32)] * 2 + [shape((8, 16, WIDE))],
    [scratch((8, FEED, WIDE)), DMA((8,))],
    moved=12 << 20,
)


def mover(sizes, target, takes=None):
    replicas, sections, shards = sizes
    pairs = []
    for d in range(replicas):
        for s in range(sections):
            for z in range(shards):
                if takes is None or takes(d, s, z):
                    nd, ns, nz = target(d, s, z)
                    pairs.append(
                        ((d * sections + s) * shards + z, (nd * sections + ns) * shards + nz)
                    )

    def move(values):
        return lax.ppermute(values, AXES, pairs)

    return move


def solution(mesh):
    replicas, sections, shards = (mesh.shape[name] for name in AXES)
    sizes = (replicas, sections, shards)

    def quarter_of(d, s):
        return 2 * ((d >> 1) & 1) + s

    swap_y = mover(sizes, lambda d, s, z: (d, s ^ 1, z))
    swap_x = mover(sizes, lambda d, s, z: (d ^ 2, s, z))
    swap_xy = mover(sizes, lambda d, s, z: (d ^ 2, s ^ 1, z))
    swap_core = mover(sizes, lambda d, s, z: (d ^ 1, s, z))
    swap_z = [mover(sizes, lambda d, s, z, r=r: (d, s, z ^ r)) for r in range(1, 4)]
    place_in = mover(
        sizes,
        lambda d, s, z: (
            (d & ~2) | ((z >> 1) << 1),
            z & 1,
            2 * (s ^ (z & 1)) + ((d >> 1) & 1),
        ),
    )
    place_out = [
        mover(
            sizes,
            lambda d, s, z, r=r: (
                (d & ~2) | ((z & 1) << 1),
                (z >> 1) ^ r,
                quarter_of(d, s),
            ),
        )
        for r in range(2)
    ]

    def gather(share):
        return (share, swap_y(share), swap_x(share), swap_xy(share))

    def scatter(parts):
        own, p1, p2, p3 = parts
        return (own, swap_y(p1), swap_x(p2), swap_xy(p3))

    def gather_direct(piece):
        return jnp.stack([piece] + [move(piece) for move in swap_z])

    def scatter_direct(pieces):
        total = pieces[0].astype(F32)
        for r in range(1, 4):
            total = total + swap_z[r - 1](pieces[r]).astype(F32)
        return total.astype(BF16)

    def gather_mp(piece):
        return lax.all_gather(piece, "mp", axis=0)

    def scatter_mp(pieces):
        return lax.psum_scatter(pieces, "mp", scatter_dimension=0)

    def to_layers(first, second, section):
        pick = (lax.axis_index("mp") >> 1) == 0
        moved_a = place_out[0](jnp.where(pick, first, second))
        moved_b = place_out[1](jnp.where(pick, second, first))
        is_first = section == 0
        return jnp.stack(
            [jnp.where(is_first, moved_a, moved_b), jnp.where(is_first, moved_b, moved_a)]
        )

    def per_device(
        inputs,
        cotangent,
        doc_ids,
        w_query,
        b_query,
        w_key,
        w_value,
        b_value,
        w_out,
        b_out,
        gain_one,
        shift_one,
        w_up,
        b_up,
        w_down,
        b_down,
        gain_two,
        shift_two,
    ):
        replica = lax.axis_index("dp")
        section = lax.axis_index("section")
        shard = lax.axis_index("mp")
        core = replica & 1
        quarter = quarter_of(replica, section)
        place = jnp.stack([core, quarter]).astype(jnp.int32)

        attn_packs = prep_attn(
            place,
            w_query,
            w_key,
            w_value,
            w_out,
            b_query,
            b_value,
            b_out,
            gain_one,
            shift_one,
            b_down,
            gain_two,
            shift_two,
        )
        feed_packs = prep_feed(place, w_up, w_down, b_up)
        packs = [(own, swap_y(peer)) for own, peer in (attn_packs, feed_packs)]

        which = (section ^ shard) & 1
        share_in = place_in(lax.dynamic_index_in_dim(inputs, which, 0, False))
        share_grad = place_in(lax.dynamic_index_in_dim(cotangent, which, 0, False))
        other_ids = swap_x(doc_ids)
        mine = ((replica >> 1) & 1) == (shard & 1)
        ids = jnp.where(mine, doc_ids, other_ids)
        ids = lax.dynamic_index_in_dim(ids, shard >> 1, 0, False).reshape(4, SHARE)
        ids = jnp.concatenate(
            [lax.dynamic_index_in_dim(ids, quarter ^ r, 0, False) for r in range(4)]
        )
        id_column, id_row = ids[:, None], ids[None, :]

        layers = []
        for layer in range(2):
            attn, feed = (jnp.where(section == layer, own, other) for own, other in packs)
            attn = gather_direct(attn) if layer == 0 else gather_mp(attn)
            feed = gather_mp(feed)
            layers.append((attn, swap_core(attn), feed, swap_core(feed), attn[0, 128:144]))

        def forward(share, weights):
            attn, attn_other, feed, feed_other, vec = weights
            whole = gather(share)
            *parts, qkv, probs, mixed = attn_forward(
                *whole, attn, attn_other, id_column, id_row
            )
            middle, low, normed_one, inverse_one = norm_one(*scatter(parts), share, vec)
            spread = gather(low)
            *parts, active, slope = feed_forward(*spread, feed, feed_other)
            _, result, normed_two, inverse_two = norm_two(*scatter(parts), middle, vec)
            kept = (
                whole,
                qkv,
                probs,
                mixed,
                normed_one,
                inverse_one,
                spread,
                active,
                slope,
                normed_two,
                inverse_two,
            )
            return result, kept

        def backward(given, weights, kept, last):
            attn, attn_other, feed, feed_other, vec = weights
            (
                whole,
                qkv,
                probs,
                mixed,
                normed_one,
                inverse_one,
                spread,
                active,
                slope,
                normed_two,
                inverse_two,
            ) = kept
            grad = None
            if last:
                total, low, vec_two = norm_two_back(given, normed_two, inverse_two, vec)
            else:
                total, low, vec_two, grad = norm_two_back_sum(
                    *given, normed_two, inverse_two, vec
                )
            grads = gather(low)
            *parts, d_hidden = feed_backward(*grads, feed, feed_other, slope)
            feed_grad = feed_weights(d_hidden, active, *spread, *grads)
            total, low, vec_one = norm_one_back(
                total, *scatter(parts), normed_one, inverse_one, vec
            )
            grads = gather(low)
            *parts, d_rows = attn_backward(*grads, attn, attn_other, qkv, probs)
            attn_grad = attn_weights(d_rows, mixed, *whole, *grads, vec_one, vec_two)
            return (total, *scatter(parts)), grad, attn_grad, feed_grad

        def core_sum(halves):
            own, other = halves
            return (own.astype(F32) + swap_core(other).astype(F32)).astype(BF16)

        first, kept_first = forward(share_in, layers[0])
        second, kept_second = forward(first, layers[1])
        section_outputs = to_layers(first, second, section)[None]

        given, _, attn_one, feed_one = backward(share_grad, layers[1], kept_second, True)
        feed_one = scatter_mp(core_sum(feed_one))
        attn_one = scatter_mp(core_sum(attn_one))
        given, grad_one, attn_zero, feed_zero = backward(given, layers[0], kept_first, False)
        grad_zero = sum(part.astype(F32) for part in given).astype(BF16)
        feed_zero = scatter_mp(core_sum(feed_zero))
        attn_zero = scatter_direct(core_sum(attn_zero))

        def exchange(zero, one):
            if replicas > 4:
                groups = [[low + 4 * high for high in range(replicas // 4)] for low in range(4)]
                zero, one = lax.psum((zero, one), "dp", axis_index_groups=groups)
            mine = jnp.where(section == 0, zero, one)
            theirs = jnp.where(section == 0, one, zero)
            pieces = jnp.stack([mine, swap_y(theirs), swap_x(mine), swap_xy(theirs)])
            return jnp.concatenate([pieces, swap_core(pieces)])

        feeds = exchange(feed_zero, feed_one)
        attns = exchange(attn_zero, attn_one)
        order = jnp.stack(
            [(h ^ core) * 4 + (j ^ quarter) for j in range(4) for h in range(2)]
        ).astype(jnp.int32)
        g_up, g_down, feed_small = finish_feed(order, feeds)
        g_query, g_key, g_value, g_out, attn_small = finish_attn(order, attns)
        vectors = jnp.sum(attns[0:4, 128:144].astype(F32), 0)
        bias = attn_small[:, 0].astype(F32)
        g_b_up = feed_small[:, 0, 0:128].astype(F32).reshape(1, WIDE)
        section_input_grads = to_layers(grad_zero, grad_one, section)[None].astype(F32)
        return (
            section_outputs,
            section_input_grads,
            g_query,
            bias[:, 0:HALF].reshape(1, 256),
            g_key,
            g_value,
            bias[:, HALF : 2 * HALF].reshape(1, 256),
            g_out,
            vectors[1:2],
            vectors[2:3],
            vectors[3:4],
            g_up,
            g_b_up,
            g_down,
            vectors[4:5],
            vectors[5:6],
            vectors[6:7],
        )

    vector = P("section", None)
    by_column = P("section", None, "mp")
    by_row = P("section", "mp", None)
    spread = P("section", "mp")
    tokens = P(None, ("dp", "mp"), None)
    layer_tokens = P("section", None, ("dp", "mp"), None)
    return jax.shard_map(
        per_device,
        mesh=mesh,
        in_specs=(
            tokens,
            tokens,
            P(None, "dp", None),
            by_column,
            spread,
            by_column,
            by_column,
            spread,
            by_row,
            vector,
            vector,
            vector,
            by_column,
            spread,
            by_row,
            vector,
            vector,
            vector,
        ),
        out_specs=(
            layer_tokens,
            layer_tokens,
            by_column,
            spread,
            by_column,
            by_column,
            spread,
            by_row,
            vector,
            vector,
            vector,
            by_column,
            spread,
            by_row,
            vector,
            vector,
            vector,
        ),
        check_vma=False,
    )
```

```python
from functools import partial

import jax
import jax.numpy as jnp
from jax import lax
from jax.experimental import pallas as pl
from jax.experimental.pallas import tpu as pltpu
from jax.sharding import PartitionSpec as P

HD = 64
SEQ = 512
SHARE = 128
WIDE = 1024
HEADS = 4
HALF = 32
ATTN = 144
UP = 144
DOWN = 128
FEED = UP + DOWN
AXES = ("dp", "section", "mp")
EPSILON = 1e-05
NEGATIVE = -1e30
F32 = jnp.float32
BF16 = jnp.bfloat16
VMEM = pl.BlockSpec(memory_space=pltpu.VMEM)
ANY = pl.BlockSpec(memory_space=pl.ANY)
HBM = pl.BlockSpec(memory_space=pltpu.HBM)
SMEM = pl.BlockSpec(memory_space=pltpu.SMEM)


def dot_nt(left, right):
    return lax.dot_general(left, right, (((1,), (1,)), ((), ())), preferred_element_type=F32)


def dot_nn(left, right):
    return lax.dot_general(left, right, (((1,), (0,)), ((), ())), preferred_element_type=F32)


def dot_tn(left, right):
    return lax.dot_general(left, right, (((0,), (0,)), ((), ())), preferred_element_type=F32)


def shape(dims, dtype=BF16):
    return jax.ShapeDtypeStruct(dims, dtype)


DMA = pltpu.SemaphoreType.DMA


def scratch(dims, dtype=BF16):
    return pltpu.VMEM(dims, dtype)


def in_hbm(value):
    return pltpu.with_memory_space_constraint(value, pltpu.HBM)


class Arriving:
    def __init__(self, copies, target):
        self.copies, self.target = copies, target
        for copy in copies:
            copy.start()

    def get(self):
        for copy in self.copies:
            copy.wait()
        self.copies = []
        return self.target


class Leaving:
    def __init__(self, copies, buffer):
        self.copies, self.buffer, self.sent = copies, buffer, False

    def __setitem__(self, where, value):
        self.buffer[where] = value

    def __getitem__(self, where):
        return self.buffer[where]

    def send(self):
        for copy in self.copies:
            copy.start()
        self.sent = True


class Chunks:
    def __init__(self, rows):
        self.buffer = shape((4, rows, WIDE))
        cut = 80 if rows == ATTN else 64
        self.parts = [(z, start, end) for z in range(4) for start, end in ((0, cut), (cut, rows))]
        self.shapes = [shape((end - start, WIDE)) for _, start, end in self.parts]

    def views(self, buffer):
        return [buffer.at[z, start:end] for z, start, end in self.parts]


def call(kernel, name, ins, outs, scratches=(), limit=32):
    def arrays(item):
        return item.shapes if isinstance(item, Chunks) else [item]

    def buffer_of(item):
        held = item.buffer if isinstance(item, Chunks) else item
        return scratch(held.shape, held.dtype)

    loads = [i for i in ins if not isinstance(i, str)]
    stores = [o for where, o in outs if where == "h"]
    specs = {"v": VMEM, "s": SMEM, "r": HBM, "h": HBM, "a": ANY}
    in_specs, pinned = [], []
    for i in ins:
        count = 1 if isinstance(i, str) else len(arrays(i))
        in_specs += [specs[i] if isinstance(i, str) else HBM] * count
        pinned += [i == "r" or not isinstance(i, str)] * count
    out_specs, out_shapes = [], []
    for where, o in outs:
        for one in arrays(o):
            out_specs.append(specs[where])
            out_shapes.append(pltpu.HBM(one.shape, one.dtype) if where == "h" else one)
    n_loads = sum(len(arrays(i)) for i in loads)
    n_stores = sum(len(arrays(o)) for o in stores)

    def views(item, buffer):
        return item.views(buffer) if isinstance(item, Chunks) else [buffer]

    def body(after, *refs):
        refs = list(refs)
        in_refs = [refs.pop(0) for _ in in_specs]
        del refs[:after]
        out_refs = [refs.pop(0) for _ in out_specs]
        load_bufs = [refs.pop(0) for _ in loads]
        store_bufs = [refs.pop(0) for _ in stores]
        load_sems = refs.pop(0) if loads else None
        store_sems = refs.pop(0) if stores else None
        operands, results, n = [], [], 0
        for kind in ins:
            if isinstance(kind, str):
                operands.append(in_refs.pop(0))
                continue
            target, copies = load_bufs.pop(0), []
            for view in views(kind, target):
                copies.append(pltpu.make_async_copy(in_refs.pop(0), view, load_sems.at[n]))
                n += 1
            operands.append(Arriving(copies, target))
        n = 0
        for where, o in outs:
            if where == "v":
                results.append(out_refs.pop(0))
                continue
            buffer, copies = store_bufs.pop(0), []
            for view in views(o, buffer):
                copies.append(pltpu.make_async_copy(view, out_refs.pop(0), store_sems.at[n]))
                n += 1
            results.append(Leaving(copies, buffer))
        kernel(*operands, *results, *refs)
        for operand in operands:
            if isinstance(operand, Arriving):
                operand.get()
        leaving = [result for result in results if isinstance(result, Leaving)]
        for result in leaving:
            if not result.sent:
                result.send()
        for result in leaving:
            for copy in result.copies:
                copy.wait()

    def run(*operands):
        after = len(operands) - len(in_specs)
        operands = [
            in_hbm(operand) if pin else operand
            for pin, operand in zip(pinned + [True] * after, operands)
        ]
        return pl.pallas_call(
            partial(body, after),
            name=name,
            in_specs=in_specs + [ANY] * after,
            out_specs=tuple(out_specs),
            out_shape=tuple(out_shapes),
            scratch_shapes=[buffer_of(item) for item in loads + stores]
            + ([DMA((n_loads,))] if loads else [])
            + ([DMA((n_stores,))] if stores else [])
            + list(scratches),
            compiler_params=pltpu.CompilerParams(vmem_limit_bytes=limit << 20),
            cost_estimate=pl.CostEstimate(flops=0, bytes_accessed=0, transcendentals=0),
        )(*operands)

    return run


def hold(value, *after):
    return pl.pallas_call(
        lambda *refs: None,
        name="hold",
        in_specs=[HBM] + [ANY] * len(after),
        out_specs=HBM,
        out_shape=pltpu.HBM(value.shape, value.dtype),
        input_output_aliases={0: 0},
    )(in_hbm(value), *after)


def stamp(*values):
    def kernel(*refs):
        refs[-1][...] = jnp.zeros((8, 128), F32)

    return pl.pallas_call(
        kernel,
        name="stamp",
        in_specs=[ANY] * len(values),
        out_specs=VMEM,
        out_shape=shape((8, 128), F32),
        compiler_params=pltpu.CompilerParams(vmem_limit_bytes=16 << 20),
        cost_estimate=pl.CostEstimate(flops=0, bytes_accessed=0, transcendentals=0),
    )(*values)


def zero_after(after):
    def kernel(after, out):
        out[0] = 0

    return pl.pallas_call(
        kernel,
        name="zero",
        in_specs=[ANY],
        out_specs=SMEM,
        out_shape=shape((1,), jnp.int32),
    )(after)[0]


def at_rows(rows, values):
    place = lax.broadcasted_iota(jnp.int32, (rows, values[0].shape[1]), 0)
    block = jnp.zeros((rows, values[0].shape[1]), F32)
    for i, value in enumerate(values):
        block = jnp.where(place == i, value, block)
    return block


def columns(i, width=256):
    return pl.ds(pl.multiple_of(i * width, width), width)


def prep_attn_kernel(place, wq, wk, wv, wo, bq, bv, v0, v1, v2, v3, v4, v5, own, peer, turned):
    core, quarter = place[0], place[1]
    for a, w in enumerate((wq, wk, wv)):
        turned[a] = w.get()[0].T
    layer_rows = [v.get()[...].astype(F32) for v in (v0, v1, v2, v3, v4, v5)]
    wo, bq, bv = wo.get(), bq.get(), bv.get()
    source = lax.broadcasted_iota(jnp.int32, (256, 128), 0)
    lane = lax.broadcasted_iota(jnp.int32, (256, 128), 1)
    for out, block in ((own, quarter), (peer, quarter ^ 1)):
        head = pl.multiple_of(block * HD + core * HALF, HALF)
        for a in range(3):
            out[HALF * a : HALF * a + HALF] = turned[a, pl.ds(head, HALF)]
        out[3 * HALF : 4 * HALF] = wo[0, pl.ds(head, HALF)]
        inner = lane & 63
        wanted = block * HD + (inner ^ (core * HALF))
        hit = source == wanted
        zero = jnp.zeros((256, 128), F32)
        one = jnp.ones((256, 128), F32)
        first = jnp.where(hit & (lane < 64), one, zero).astype(BF16)
        second = jnp.where(hit & (lane >= 64), one, zero).astype(BF16)
        bias = dot_nn(jnp.broadcast_to(bq[...], (16, 256)), first) + dot_nn(
            jnp.broadcast_to(bv[...], (16, 256)), second
        )
        rows = lax.broadcasted_iota(jnp.int32, (16, WIDE), 0)
        block_rows = jnp.zeros((16, WIDE), F32)
        for i, row in enumerate(layer_rows):
            block_rows = jnp.where(rows == i + 1, row, block_rows)
        out[128:144] = block_rows.astype(BF16)
        first_row = lax.broadcasted_iota(jnp.int32, (16, 128), 0) == 0
        out[128:144, 0:128] = jnp.where(first_row, bias, block_rows[:, 0:128]).astype(BF16)


def pick_kernel(place, own, got, out):
    own, got = own.get(), got.get()
    out[...] = jnp.where(jnp.full(own.shape, place[2]) == 0, own[...], got[...])


def prep_feed_kernel(place, up, down, bu, own, peer, column, sems):
    core, quarter = place[0], place[1]
    copies = []
    outs = ((own, quarter), (peer, quarter ^ 1))
    for i, (out, block) in enumerate(outs):
        unit = pl.multiple_of(block * 256 + core * 128, 128)
        copies.append(
            pltpu.make_async_copy(up.at[0, :, pl.ds(unit, 128)], column.at[i], sems.at[2 * i])
        )
        copies.append(
            pltpu.make_async_copy(
                down.at[0, pl.ds(unit, 128)], out.buffer.at[UP:FEED], sems.at[2 * i + 1]
            )
        )
    for copy in copies:
        copy.start()
    row = lax.broadcasted_iota(jnp.int32, (16, 128), 0) == 0
    for i, (out, block) in enumerate(outs):
        out[128:144] = jnp.zeros((16, WIDE), BF16)
        for h in range(2):
            unit = pl.multiple_of(block * 256 + (core ^ h) * 128, 128)
            piece = bu[:, pl.ds(unit, 128)].astype(F32)
            out[128:144, 128 * h : 128 * h + 128] = jnp.where(row, piece, 0.0).astype(BF16)
        copies[2 * i].wait()
        out[0:128] = column[i].T
        copies[2 * i + 1].wait()
        out.send()


def rows_of(ref, *which):
    block = ref[...].astype(F32)
    return [block[i : i + 1] for i in which]


def norm_forward(hidden, gain, offset):
    centre = jnp.mean(hidden, -1, keepdims=True)
    centred = hidden - centre
    variance = jnp.mean(centred * centred, -1, keepdims=True)
    inverse = lax.rsqrt(variance + EPSILON)
    normed = centred * inverse
    return (normed * gain + offset, normed, inverse)


def norm_backward(upstream, normed, inverse, gain):
    scaled = upstream * gain
    return inverse * (
        scaled
        - jnp.mean(scaled, -1, keepdims=True)
        - normed * jnp.mean(scaled * normed, -1, keepdims=True)
    )


def received(own, r1, r2, r3):
    return own[...] + r1[...].astype(F32) + r2[...].astype(F32) + r3[...].astype(F32)


def norm_kernel(first, own, r1, r2, r3, residual, vec, value, low, normed, inverse):
    bias, gain, offset = rows_of(vec, *((1, 2, 3) if first else (4, 5, 6)))
    hidden = residual[...].astype(F32) + received(own, r1, r2, r3) + bias
    result, flat, scale = norm_forward(hidden, gain, offset)
    low[...] = result.astype(BF16)
    value[...] = result
    normed[...] = flat.astype(BF16)
    inverse[...] = scale


def sums(*values):
    return at_rows(8, [jnp.sum(v, 0, keepdims=True) for v in values])


def norm_back(grad, gain, normed, inverse, total, low, vectors):
    flat = normed.get()[...].astype(F32)
    value = norm_backward(grad, flat, inverse.get()[...], gain)
    rounded = value.astype(BF16)
    low[...] = rounded
    total[...] = value
    total.send()
    vectors[...] = sums(rounded.astype(F32), grad * flat, grad)


def norm_two_back_kernel(upstream, vec, normed, inverse, total, low, vectors):
    (gain,) = rows_of(vec, 5)
    norm_back(upstream[...].astype(F32), gain, normed, inverse, total, low, vectors)


def norm_two_back_sum_kernel(
    own, r1, r2, r3, vec, before, normed, inverse, total, low, vectors, given
):
    (gain,) = rows_of(vec, 5)
    rounded = (before.get()[...] + received(own, r1, r2, r3)).astype(BF16)
    norm_back(rounded.astype(F32), gain, normed, inverse, total, low, vectors)
    given[...] = rounded


def norm_one_back_kernel(own, r1, r2, r3, vec, before, normed, inverse, total, low, vectors):
    (gain,) = rows_of(vec, 2)
    grad = before.get()[...] + received(own, r1, r2, r3)
    norm_back(grad, gain, normed, inverse, total, low, vectors)


def last_sum_kernel(own, r1, r2, r3, before, given):
    given[...] = (before.get()[...] + received(own, r1, r2, r3)).astype(BF16)


def load_attn(own, other, weight, sems):
    return [
        pltpu.make_async_copy(
            ref.at[:, HALF * a : HALF * a + HALF], weight.at[a, :, half], sems.at[4 * half + a]
        )
        for half, ref in enumerate((own, other))
        for a in range(4)
    ]


def join(target, pieces, sems):
    copies = [
        pltpu.make_async_copy(piece, target.at[SHARE * i : SHARE * i + SHARE], sems.at[i])
        for i, piece in enumerate(pieces)
    ]
    for copy in copies:
        copy.start()
    return copies


def arrive(copies):
    for copy in copies:
        copy.wait()


def spread_out(value, where, own, parts):
    own[:, where] = value[0:SHARE]
    for i, part in enumerate(parts):
        part[:, where] = value[SHARE * (i + 1) : SHARE * (i + 2)].astype(BF16)


def by_share(left, right, own, parts):
    for i in (3, 2, 1, 0):
        value = dot_nn(left[SHARE * i : SHARE * i + SHARE], right)
        if i:
            parts[i - 1][...] = value.astype(BF16)
        else:
            own[...] = value


def attn_kernel(
    x0, x1, x2, x3, id_row, a_own, a_other,
    own, p1, p2, p3, qkv, probs, mixed, x_out, weight_out,
    small, sems, x_sems,
):
    weight, x_all = weight_out.buffer, x_out.buffer
    copies = load_attn(a_own, a_other, weight, sems)
    copies.append(pltpu.make_async_copy(a_own.at[:, 128:144], small, sems.at[8]))
    for copy in copies:
        copy.start()
    arrive(join(x_all, (x0, x1, x2, x3), x_sems))
    x_out.send()
    arrive(copies)
    weight_out.send()
    ids = id_row[...]
    id_column = jnp.broadcast_to(ids, (128, SEQ)).T[:, 0:1]
    biases = [small[z].astype(F32)[0:1] for z in range(4)]
    bias_of = (
        jnp.concatenate([b[:, 0:64] for b in biases], 1),
        None,
        jnp.concatenate([b[:, 64:128] for b in biases], 1),
    )
    x = x_all[...]
    for a in range(3):
        rows = dot_nt(x, weight[a].reshape(256, WIDE))
        if bias_of[a] is not None:
            rows = rows + bias_of[a]
        qkv[:, 256 * a : 256 * a + 256] = rows.astype(BF16)
    qkv.send()
    for c in range(2):
        q_rows = slice(256 * c, 256 * c + 256)
        allowed = id_column[q_rows] == ids
        for h in range(HEADS):
            query = qkv[q_rows, HD * h : HD * h + HD]
            key = qkv[:, 256 + HD * h : 256 + HD * h + HD]
            value = qkv[:, 512 + HD * h : 512 + HD * h + HD]
            scores = jnp.where(allowed, dot_nt(query, key) * HD ** (-0.5), NEGATIVE)
            exponent = jnp.exp(scores - jnp.max(scores, -1, keepdims=True))
            low = (exponent / jnp.sum(exponent, -1, keepdims=True)).astype(BF16)
            probs[h, q_rows] = low
            mixed[q_rows, HD * h : HD * h + HD] = dot_nn(low, value).astype(BF16)
    probs.send()
    mixed.send()
    by_share(mixed, weight[3].reshape(256, WIDE), own, (p1, p2, p3))


def attn_back_kernel(
    g0, g1, g2, g3, weight, qkv, probs, own, p1, p2, p3, d_rows, g_out, x_sems
):
    g_all = g_out.buffer
    arrive(join(g_all, (g0, g1, g2, g3), x_sems))
    g_out.send()
    weight, qkv, probs = weight.get(), qkv.get(), probs.get()
    d_mixed = dot_nt(g_all[...], weight[3].reshape(256, WIDE)).astype(BF16)
    scale = HD ** (-0.5)
    for h in range(HEADS):
        query = qkv[:, HD * h : HD * h + HD]
        key = qkv[:, 256 + HD * h : 256 + HD * h + HD]
        value = qkv[:, 512 + HD * h : 512 + HD * h + HD]
        grad = d_mixed[:, HD * h : HD * h + HD]
        d_key = jnp.zeros((SEQ, HD), F32)
        d_value = jnp.zeros((SEQ, HD), F32)
        for c in range(2):
            q_rows = slice(256 * c, 256 * c + 256)
            low = probs[h, q_rows]
            p = low.astype(F32)
            d_probs = dot_nt(grad[q_rows], value)
            inner = jnp.sum(p * d_probs, -1, keepdims=True)
            d_scores = (p * (d_probs - inner)).astype(BF16)
            d_rows[q_rows, HD * h : HD * h + HD] = (dot_nn(d_scores, key) * scale).astype(BF16)
            d_key = d_key + dot_tn(d_scores, query[q_rows])
            d_value = d_value + dot_tn(low, grad[q_rows])
        d_rows[:, 256 + HD * h : 256 + HD * h + HD] = (d_key * scale).astype(BF16)
        d_rows[:, 512 + HD * h : 512 + HD * h + HD] = d_value.astype(BF16)
    d_rows.send()
    by_share(d_rows, weight[0:3].reshape(768, WIDE), own, (p1, p2, p3))


def attn_weights_kernel(
    d_rows, mixed, x_all, g_all, vec_one, vec_two, own, other
):
    operands = (d_rows, mixed, x_all, g_all, vec_one, vec_two)
    d_rows, mixed, x_all, g_all, vec_one, vec_two = (operand.get() for operand in operands)
    for a in range(4):
        if a < 3:
            value = dot_tn(d_rows[:, 256 * a : 256 * a + 256], x_all[...])
        else:
            value = dot_tn(mixed[...], g_all[...])
        value = value.astype(BF16).reshape(4, 2, HALF, WIDE)
        own[:, HALF * a : HALF * a + HALF] = value[:, 0]
        other[:, HALF * a : HALF * a + HALF] = value[:, 1]
    total = jnp.sum(d_rows[...].astype(F32), 0, keepdims=True)
    one, two = vec_one[...], vec_two[...]
    vectors = [one[i : i + 1] for i in range(3)] + [two[i : i + 1] for i in range(3)]
    block = at_rows(16, [jnp.zeros((1, WIDE), F32)] + vectors)
    first_row = lax.broadcasted_iota(jnp.int32, (16, 128), 0) == 0
    for half, out in ((1, other), (0, own)):
        for z in range(4):
            start = HD * z + HALF * half
            bias = jnp.concatenate(
                [
                    total[:, start : start + HALF],
                    total[:, 512 + start : 512 + start + HALF],
                    jnp.zeros((1, 64), F32),
                ],
                1,
            )
            out[z, 128:144] = block.astype(BF16)
            out[z, 128:144, 0:128] = jnp.where(first_row, bias, block[:, 0:128]).astype(BF16)
        out.send()


def load_feed(ups, downs, up, down, sems):
    copies = []
    for i, (refs, target) in enumerate(((ups, up), (downs, down))):
        for half in range(2):
            copies.append(
                pltpu.make_async_copy(
                    refs[half].at[:, 0:128],
                    target.at[4 * half : 4 * half + 4],
                    sems.at[2 * i + half],
                )
            )
    return copies[:2], copies[2:]


def feed_kernel(
    x0, x1, x2, x3, up_own, up_other, down_own, down_other,
    own, p1, p2, p3, active, slope, x_out, up_out, down_out,
    small, bias, sems, x_sems,
):
    x_all, up, down = x_out.buffer, up_out.buffer, down_out.buffer
    ups, downs = load_feed((up_own, up_other), (down_own, down_other), up, down, sems)
    copies = [pltpu.make_async_copy(up_own.at[:, 128:144], small, sems.at[4])] + ups
    for copy in copies + downs:
        copy.start()
    arrive(join(x_all, (x0, x1, x2, x3), x_sems))
    x_out.send()
    arrive(copies)
    up_out.send()
    for half in range(2):
        for z in range(4):
            unit = 512 * half + 128 * z
            bias[0:8, unit : unit + 128] = jnp.broadcast_to(
                small[z, :, 128 * half : 128 * half + 128].astype(F32)[0:1], (8, 128)
            )

    def units(i, carry):
        block = up[pl.ds(2 * i, 2)].reshape(256, WIDE)
        hidden = dot_nt(x_all[...], block) + bias[0:1, columns(i)]
        share = 0.5 * (1.0 + lax.erf(hidden * (0.5 ** 0.5)))
        density = jnp.exp(-0.5 * hidden * hidden) * 0.3989422804014327
        active[:, columns(i)] = (hidden * share).astype(BF16)
        slope[:, columns(i)] = (share + hidden * density).astype(BF16)
        return carry

    lax.fori_loop(0, 4, units, 0)
    active.send()
    slope.send()
    arrive(downs)
    down_out.send()

    def features(n, carry):
        block = down[:, :, columns(n)].reshape(WIDE, 256)
        spread_out(dot_nn(active[...], block), columns(n), own, (p1, p2, p3))
        return carry

    lax.fori_loop(0, 4, features, 0)


def feed_back_kernel(
    g0, g1, g2, g3, down, slope, up, own, p1, p2, p3, d_hidden, g_out, x_sems
):
    g_all = g_out.buffer
    arrive(join(g_all, (g0, g1, g2, g3), x_sems))
    g_out.send()
    down, slope = down.get(), slope.get()

    def units(i, carry):
        block = down[pl.ds(2 * i, 2)].reshape(256, WIDE)
        value = dot_nt(g_all[...], block) * slope[:, columns(i)].astype(F32)
        d_hidden[:, columns(i)] = value.astype(BF16)
        return carry

    lax.fori_loop(0, 4, units, 0)
    d_hidden.send()
    up = up.get()

    def features(n, carry):
        block = up[:, :, columns(n)].reshape(WIDE, 256)
        spread_out(dot_nn(d_hidden[...], block), columns(n), own, (p1, p2, p3))
        return carry

    lax.fori_loop(0, 4, features, 0)


def feed_weights_kernel(
    d_hidden, active, x_all, g_all, up_own, up_other, down_own, down_other
):
    d_hidden, active, x_all, g_all = (v.get() for v in (d_hidden, active, x_all, g_all))
    row = lax.broadcasted_iota(jnp.int32, (16, 128), 0) == 0
    for half, up, down in ((1, up_other, down_other), (0, up_own, down_own)):

        def pair(i, carry, half=half, up=up, down=down):
            where = columns(2 * half + i)
            value = dot_tn(d_hidden[:, where], x_all[...]).astype(BF16)
            up[pl.ds(2 * i, 2), 0:128] = value.reshape(2, 128, WIDE)
            value = dot_tn(active[:, where], g_all[...]).astype(BF16)
            down[pl.ds(2 * i, 2)] = value.reshape(2, 128, WIDE)
            return carry

        lax.fori_loop(0, 2, pair, 0)
        total = jnp.sum(d_hidden[:, 512 * half : 512 * half + 512].astype(F32), 0, keepdims=True)
        for z in range(4):
            up[z, 128:144] = jnp.zeros((16, WIDE), BF16)
            up[z, 128:144, 0:128] = jnp.where(row, total[:, 128 * z : 128 * z + 128], 0.0).astype(
                BF16
            )
        up.send()
        down.send()


def core_sum_kernel(*refs):
    count = len(refs) // 3
    for own, received, out in zip(refs[:count], refs[count : 2 * count], refs[2 * count :]):
        out[...] = (own.get()[...].astype(F32) + received[...].astype(F32)).astype(BF16)
        out.send()


def ordered(place):
    return [
        (4 * c + r, ((r ^ place[1]) * 2 + (c ^ place[0])).astype(jnp.int32))
        for c in range(2)
        for r in range(4)
    ]


def finish_attn_kernel(place, *refs):
    pieces, refs = refs[:8], refs[8:]
    gq, gk, gv, go, small, turned, sems = refs
    copies = []
    for i, to in ordered(place):
        copies.append(
            pltpu.make_async_copy(pieces[i].at[128:144], small.buffer.at[to], sems.at[4, i])
        )
        for a in range(4):
            copies.append(
                pltpu.make_async_copy(
                    pieces[i].at[HALF * a : HALF * a + HALF], turned.at[a, to], sems.at[a, i]
                )
            )
    for copy in copies:
        copy.start()
    for copy in copies:
        copy.wait()
    for a, out in enumerate((gq, gk, gv)):
        out[0] = turned[a].reshape(256, WIDE).astype(F32).T
        out.send()
    go[0] = turned[3].reshape(256, WIDE).astype(F32)


def finish_feed_kernel(place, *refs):
    pieces, refs = refs[:8], refs[8:]
    up, down, small, block, sems = refs
    copies = []
    for i, to in ordered(place):
        copies.append(pltpu.make_async_copy(pieces[i], block.at[to], sems.at[i]))
    for copy in copies:
        copy.start()
    for copy in copies:
        copy.wait()
    for i in range(8):
        down[0, 128 * i : 128 * i + 128] = block[i, UP:FEED].astype(F32)
    down.send()
    for i in range(8):
        up[0, :, 128 * i : 128 * i + 128] = block[i, 0:128].astype(F32).T
        small[i] = block[i, 128:144]


def finish_tokens_kernel(place, a, b, out):
    is_first = place[2] == 0

    @pl.when(is_first)
    def _():
        out[0, 0] = a[...].astype(out.buffer.dtype)
        out[0, 1] = b[...].astype(out.buffer.dtype)

    @pl.when(jnp.logical_not(is_first))
    def _():
        out[0, 0] = b[...].astype(out.buffer.dtype)
        out[0, 1] = a[...].astype(out.buffer.dtype)


RAW = ["a"] * 4
WHOLE = shape((SEQ, WIDE))
BLOCKS = shape((8, 128, WIDE))
HEAD_ROWS = shape((4, 4, 2, HALF, WIDE))
TOKEN = shape((SHARE, WIDE))
WIDE_TOKEN = shape((SHARE, WIDE), F32)
ONE = shape((SHARE, 1), F32)
PARTS = [("v", WIDE_TOKEN)] + [("v", TOKEN)] * 3
ROW = shape((1, WIDE))
FOUR = DMA((4,))
MASK = shape((1, SEQ), F32)
VECTORS = shape((8, WIDE), F32)

prep_attn = call(
    prep_attn_kernel,
    "pack_attention",
    ["s"]
    + [shape((1, WIDE, 256))] * 3
    + [shape((1, 256, WIDE))]
    + [shape((1, 256))] * 2
    + [ROW] * 6,
    [("h", shape((ATTN, WIDE)))] * 2,
    [scratch((3, 256, WIDE))],
)
pick = call(
    pick_kernel,
    "pick",
    ["s"] + [shape((ATTN, WIDE))] * 2,
    [("h", shape((ATTN, WIDE)))],
)
prep_feed = call(
    prep_feed_kernel,
    "pack_feed",
    ["s", "r", "r", "v"],
    [("h", shape((FEED, WIDE)))] * 2,
    [scratch((2, WIDE, 128)), DMA((4,))],
)
norm_one, norm_two = (
    call(
        partial(norm_kernel, first),
        name,
        ["v"] * 6,
        [("v", WIDE_TOKEN), ("v", TOKEN), ("h", TOKEN), ("h", ONE)],
        )
    for first, name in ((True, "norm_one"), (False, "norm_two"))
)
BACKS = [("h", WIDE_TOKEN), ("v", TOKEN), ("h", VECTORS)]
norm_two_back = call(
    norm_two_back_kernel, "norm_two_back", ["v", "v", TOKEN, ONE], BACKS
)
norm_two_back_sum = call(
    norm_two_back_sum_kernel,
    "norm_two_back_sum",
    ["v"] * 5 + [WIDE_TOKEN, TOKEN, ONE],
    BACKS + [("h", TOKEN)],
)
norm_one_back = call(
    norm_one_back_kernel,
    "norm_one_back",
    ["v"] * 5 + [WIDE_TOKEN, TOKEN, ONE],
    BACKS,
)
last_sum = call(
    last_sum_kernel, "last_sum", ["v"] * 4 + [WIDE_TOKEN], [("h", TOKEN)]
)
attn_forward = call(
    attn_kernel,
    "attention",
    RAW + ["v", "a", "a"],
    PARTS
    + [
        ("h", shape((SEQ, 768))),
        ("h", shape((HEADS, SEQ, SEQ))),
        ("h", shape((SEQ, 256))),
        ("h", WHOLE),
        ("h", HEAD_ROWS),
    ],
    [scratch((4, 16, WIDE)), DMA((9,)), FOUR],
)
attn_backward = call(
    attn_back_kernel,
    "attention_back",
    RAW + [HEAD_ROWS, shape((SEQ, 768)), shape((HEADS, SEQ, SEQ))],
    PARTS + [("h", shape((SEQ, 768))), ("h", WHOLE)],
    [FOUR],
)
attn_weights = call(
    attn_weights_kernel,
    "attention_weights",
    [shape((SEQ, 768)), shape((SEQ, 256)), WHOLE, WHOLE] + [VECTORS] * 2,
    [("h", shape((4, ATTN, WIDE)))] * 2,
)
feed_forward = call(
    feed_kernel,
    "feed",
    RAW + ["a"] * 4,
    PARTS + [("h", WHOLE)] * 3 + [("h", BLOCKS)] * 2,
    [scratch((4, 16, WIDE)), scratch((8, WIDE), F32), DMA((5,)), FOUR],
)
feed_backward = call(
    feed_back_kernel,
    "feed_back",
    RAW + [BLOCKS, WHOLE, BLOCKS],
    PARTS + [("h", WHOLE)] * 2,
    [FOUR],
)
feed_weights = call(
    feed_weights_kernel,
    "feed_weights",
    [WHOLE] * 4,
    [("h", shape((4, UP, WIDE)))] * 2 + [("h", shape((4, DOWN, WIDE)))] * 2,
)
FEED_GRADS = [shape((4, UP, WIDE)), shape((4, DOWN, WIDE))]
core_sum_feed = call(
    core_sum_kernel,
    "core_sum_feed",
    FEED_GRADS + ["v"] * 2,
    [("h", grad) for grad in FEED_GRADS],
)
core_sum_attn = call(
    core_sum_kernel,
    "core_sum_attention",
    [shape((4, ATTN, WIDE)), "v"],
    [("h", shape((4, ATTN, WIDE)))],
)
finish_attn = call(
    finish_attn_kernel,
    "finish_attention",
    ["s"] + ["r"] * 8,
    [("h", shape((1, WIDE, 256), F32))] * 3
    + [("h", shape((1, 256, WIDE), F32)), ("h", shape((8, 16, WIDE)))],
    [scratch((4, 8, HALF, WIDE)), DMA((5, 8))],
)
finish_feed = call(
    finish_feed_kernel,
    "finish_feed",
    ["s"] + ["r"] * 8,
    [("h", shape((1, WIDE, WIDE), F32))] * 2 + [("h", shape((8, 16, WIDE)))],
    [scratch((8, FEED, WIDE)), DMA((8,))],
)
finish_tokens = {
    dtype: call(
        finish_tokens_kernel,
        "finish_tokens",
        ["s", "v", "v"],
        [("h", shape((1, 2, SHARE, WIDE), dtype))],
        )
    for dtype in (F32, BF16)
}


def mover(sizes, target, takes=None):
    replicas, sections, shards = sizes
    pairs = []
    for d in range(replicas):
        for s in range(sections):
            for z in range(shards):
                if takes is None or takes(d, s, z):
                    nd, ns, nz = target(d, s, z)
                    pairs.append(
                        ((d * sections + s) * shards + z, (nd * sections + ns) * shards + nz)
                    )

    def move(values):
        return lax.ppermute(values, AXES, pairs)

    return move


def solution(mesh):
    replicas, sections, shards = (mesh.shape[name] for name in AXES)
    sizes = (replicas, sections, shards)

    def quarter_of(d, s):
        return 2 * ((d >> 1) & 1) + s

    swap_y = mover(sizes, lambda d, s, z: (d, s ^ 1, z))
    swap_x = mover(sizes, lambda d, s, z: (d ^ 2, s, z))
    swap_xy = mover(sizes, lambda d, s, z: (d ^ 2, s ^ 1, z))
    swap_core = mover(sizes, lambda d, s, z: (d ^ 1, s, z))
    place_in = mover(
        sizes,
        lambda d, s, z: (
            (d & ~2) | ((z >> 1) << 1),
            z & 1,
            2 * (s ^ (z & 1)) + ((d >> 1) & 1),
        ),
    )
    place_out = [
        mover(
            sizes,
            lambda d, s, z, r=r: (
                (d & ~2) | ((z & 1) << 1),
                (z >> 1) ^ r,
                quarter_of(d, s),
            ),
        )
        for r in range(2)
    ]

    def gather(share):
        return (share, swap_y(share), swap_x(share), swap_xy(share))

    def scatter(parts):
        own, p1, p2, p3 = parts
        return (own, swap_y(p1), swap_x(p2), swap_xy(p3))

    def gather_mp(piece):
        return lax.all_gather(piece, "mp", axis=0)

    def scatter_mp(pieces):
        return lax.psum_scatter(pieces, "mp", scatter_dimension=0)

    def to_layers(first, second):
        is_first = (lax.axis_index("mp") >> 1) == 0
        return (
            place_out[0](jnp.where(is_first, first, second)),
            place_out[1](jnp.where(is_first, second, first)),
        )

    def per_device(
        inputs,
        cotangent,
        doc_ids,
        w_query,
        b_query,
        w_key,
        w_value,
        b_value,
        w_out,
        b_out,
        gain_one,
        shift_one,
        w_up,
        b_up,
        w_down,
        b_down,
        gain_two,
        shift_two,
    ):
        replica = lax.axis_index("dp")
        section = lax.axis_index("section")
        shard = lax.axis_index("mp")
        core = replica & 1
        quarter = quarter_of(replica, section)
        place = jnp.stack([core, quarter, section, shard]).astype(jnp.int32)

        attn_own, attn_peer = prep_attn(
            place,
            w_query,
            w_key,
            w_value,
            w_out,
            b_query,
            b_value,
            b_out,
            gain_one,
            shift_one,
            b_down,
            gain_two,
            shift_two,
        )
        attn_got = swap_y(attn_peer)
        which = (section ^ shard) & 1
        share_in = place_in(lax.dynamic_index_in_dim(inputs, which, 0, False))
        other_ids = swap_x(doc_ids)
        (attn_zero,) = pick(place, attn_own, attn_got, share_in, other_ids)
        whole_in = gather(share_in)
        feed_own, feed_peer = prep_feed(
            place, w_up, w_down, b_up, attn_zero, stamp(*whole_in[1:])
        )
        feed_got = swap_y(feed_peer)

        def of_layer(layer, own, got):
            return jnp.where(section == layer, own, got)

        attn_zero = gather_mp(attn_zero)
        attn_zero = (attn_zero, swap_core(attn_zero))
        feed_packs = [of_layer(layer, feed_own, feed_got) for layer in range(2)]
        up_zero = gather_mp(feed_packs[0][:UP])
        down_zero = gather_mp(feed_packs[0][UP:])
        attn_one = gather_mp(of_layer(1, attn_own, attn_got))
        up_one = gather_mp(feed_packs[1][:UP])
        down_one = gather_mp(feed_packs[1][UP:])

        mine = ((replica >> 1) & 1) == (shard & 1)
        ids = jnp.where(mine, doc_ids, other_ids)
        ids = lax.dynamic_index_in_dim(ids, shard >> 1, 0, False).reshape(4, SHARE)
        ids = jnp.concatenate(
            [lax.dynamic_index_in_dim(ids, quarter ^ r, 0, False) for r in range(4)]
        )
        id_row = ids.astype(F32)[None, :]

        def attn_half(share, whole, weights, vec):
            *parts, qkv, probs, mixed, whole, weights = attn_forward(*whole, id_row, *weights)
            parts = scatter(parts)
            middle, low, normed, inverse = norm_one(*parts, share, vec)
            return middle, low, (whole, qkv, probs, mixed, normed, inverse, weights)

        def feed_half(middle, spread, weights, vec):
            *parts, active, slope, spread, up, down = feed_forward(*spread, *weights)
            parts = scatter(parts)
            _, result, normed, inverse = norm_two(*parts, middle, vec)
            return result, (spread, active, slope, normed, inverse, up, down)

        vec_zero = attn_zero[0][0, 128:144]
        middle, low, kept_attn_zero = attn_half(share_in, whole_in, attn_zero, vec_zero)
        spread = gather(low)
        up_zero = hold(up_zero, low)
        down_zero = hold(down_zero, stamp(*spread[1:]))
        feed_zero = (up_zero, swap_core(up_zero), down_zero, swap_core(down_zero))
        first, kept_feed_zero = feed_half(middle, spread, feed_zero, vec_zero)

        whole = gather(first)
        attn_one = hold(attn_one, first)
        vec_one = attn_one[0, 128:144]
        attn_one = (attn_one, swap_core(attn_one))
        middle, low, kept_attn_one = attn_half(first, whole, attn_one, vec_one)
        spread = gather(low)
        up_one = hold(up_one, low)
        down_one = hold(down_one, low)
        feed_one = (up_one, swap_core(up_one), down_one, swap_core(down_one))
        grad_which = which ^ zero_after(kept_attn_zero[1])
        share_grad = place_in(lax.dynamic_index_in_dim(cotangent, grad_which, 0, False))
        second, kept_feed_one = feed_half(middle, spread, feed_one, vec_one)

        def feed_half_back(low, kept, *after):
            spread, active, slope, _, _, up, down = kept
            grads = gather(low)
            *parts, d_hidden, grads = feed_backward(*grads, down, slope, up, *after)
            parts = scatter(parts)
            return parts, feed_weights(d_hidden, active, spread, grads), d_hidden

        def attn_half_back(grads, kept, *after):
            _, qkv, probs, _, _, _, weights = kept
            *parts, d_rows, grads = attn_backward(*grads, weights, qkv, probs, *after)
            return parts, d_rows, grads

        def feed_sum(halves, start):
            up, up_other, down, down_other = halves
            received = [swap_core(hold(other, start)) for other in (up_other, down_other)]
            return core_sum_feed(up, down, *received)

        total, low, vec_two = norm_two_back(
            share_grad, vec_one, kept_feed_one[3], kept_feed_one[4]
        )
        parts, halves, _ = feed_half_back(low, kept_feed_one)
        outputs = to_layers(first, second)
        total, low, vec_first = norm_one_back(
            *parts, vec_one, total, kept_attn_one[4], kept_attn_one[5], halves[0], *outputs
        )
        (section_outputs,) = finish_tokens[BF16](place, *outputs)
        grads = gather(low)
        halves = feed_sum(halves, low)
        ready = stamp(*grads[1:], in_hbm(halves[0]))
        parts, d_rows, grads = attn_half_back(grads, kept_attn_one, ready)
        parts = scatter(parts)
        feed_grad_one = [scatter_mp(hold(part, ready)) for part in halves]
        own, other = attn_weights(
            d_rows, kept_attn_one[3], kept_attn_one[0], grads, vec_first, vec_two
        )
        total, low, vec_two, grad_one = norm_two_back_sum(
            *parts, vec_zero, total, kept_feed_zero[3], kept_feed_zero[4], own
        )
        (attn_grad_one,) = core_sum_attn(own, swap_core(hold(other, low)))
        parts, halves, d_hidden = feed_half_back(
            low, kept_feed_zero, attn_grad_one, feed_grad_one[0]
        )
        attn_grad_one = hold(attn_grad_one, d_hidden)
        total, low, vec_first = norm_one_back(
            *parts,
            vec_zero,
            total,
            kept_attn_zero[4],
            kept_attn_zero[5],
            halves[0],
            feed_grad_one[1],
        )
        grads = gather(low)
        halves = feed_sum(halves, low)
        ready = stamp(*grads[1:], in_hbm(halves[0]))
        attn_grad_one = scatter_mp(attn_grad_one)
        parts, d_rows, grads = attn_half_back(grads, kept_attn_zero, ready, attn_grad_one)
        feed_grad_zero = [scatter_mp(hold(part, ready)) for part in halves]
        own, other = attn_weights(
            d_rows, kept_attn_zero[3], kept_attn_zero[0], grads, vec_first, vec_two
        )
        (attn_grad_zero,) = core_sum_attn(own, swap_core(other))
        parts = scatter(parts[:1] + [hold(part, attn_grad_zero) for part in parts[1:]])
        attn_grad_zero = scatter_mp(attn_grad_zero)
        (grad_zero,) = last_sum(*parts, total)

        def exchange(zero, one, *after):
            if replicas > 4:
                groups = [[low + 4 * high for high in range(replicas // 4)] for low in range(4)]
                zero, one = lax.psum((zero, one), "dp", axis_index_groups=groups)
            mine = jnp.where(section == 0, zero, one)
            theirs = jnp.where(section == 0, one, zero)
            if after:
                mine, theirs = hold(mine, *after), hold(theirs, *after)
            pieces = [mine, swap_y(theirs), swap_x(mine), swap_xy(theirs)]
            return pieces + [swap_core(piece) for piece in pieces]

        moved = to_layers(grad_zero, grad_one)
        (section_input_grads,) = finish_tokens[F32](place, *moved)
        feeds = exchange(
            jnp.concatenate(feed_grad_zero), jnp.concatenate(feed_grad_one), stamp(*moved)
        )
        attns = exchange(attn_grad_zero, attn_grad_one)
        g_up, g_down, up_small = finish_feed(place, *feeds)
        g_query, g_key, g_value, g_out, attn_small = finish_attn(place, *attns)
        vectors = sum(piece[128:144].astype(F32) for piece in attns[0:4])
        bias = attn_small[:, 0].astype(F32)
        g_b_up = up_small[:, 0, 0:128].astype(F32).reshape(1, WIDE)
        return (
            section_outputs,
            section_input_grads,
            g_query,
            bias[:, 0:HALF].reshape(1, 256),
            g_key,
            g_value,
            bias[:, HALF : 2 * HALF].reshape(1, 256),
            g_out,
            vectors[1:2],
            vectors[2:3],
            vectors[3:4],
            g_up,
            g_b_up,
            g_down,
            vectors[4:5],
            vectors[5:6],
            vectors[6:7],
        )

    vector = P("section", None)
    by_column = P("section", None, "mp")
    by_row = P("section", "mp", None)
    spread = P("section", "mp")
    tokens = P(None, ("dp", "mp"), None)
    layer_tokens = P("section", None, ("dp", "mp"), None)
    return jax.shard_map(
        per_device,
        mesh=mesh,
        in_specs=(
            tokens,
            tokens,
            P(None, "dp", None),
            by_column,
            spread,
            by_column,
            by_column,
            spread,
            by_row,
            vector,
            vector,
            vector,
            by_column,
            spread,
            by_row,
            vector,
            vector,
            vector,
        ),
        out_specs=(
            layer_tokens,
            layer_tokens,
            by_column,
            spread,
            by_column,
            by_column,
            spread,
            by_row,
            vector,
            vector,
            vector,
            by_column,
            spread,
            by_row,
            vector,
            vector,
            vector,
        ),
        check_vma=False,
    )
```

```python
from functools import partial

import jax
import jax.numpy as jnp
from jax import lax
from jax.experimental import pallas as pl
from jax.experimental.pallas import tpu as pltpu
from jax.sharding import PartitionSpec as P

HD = 64
SEQ = 512
SHARE = 128
WIDE = 1024
HEADS = 4
HALF = 32
ATTN = 144
FEED = 128
AXES = ("dp", "section", "mp")
EPSILON = 1e-05
NEGATIVE = -1e30
F32 = jnp.float32
BF16 = jnp.bfloat16
VMEM = pl.BlockSpec(memory_space=pltpu.VMEM)
ANY = pl.BlockSpec(memory_space=pl.ANY)
HBM = pl.BlockSpec(memory_space=pltpu.HBM)
SMEM = pl.BlockSpec(memory_space=pltpu.SMEM)


def dot_nt(left, right):
    return lax.dot_general(left, right, (((1,), (1,)), ((), ())), preferred_element_type=F32)


def dot_nn(left, right):
    return lax.dot_general(left, right, (((1,), (0,)), ((), ())), preferred_element_type=F32)


def dot_tn(left, right):
    return lax.dot_general(left, right, (((0,), (0,)), ((), ())), preferred_element_type=F32)


def shape(dims, dtype=BF16):
    return jax.ShapeDtypeStruct(dims, dtype)


DMA = pltpu.SemaphoreType.DMA


def scratch(dims, dtype=BF16):
    return pltpu.VMEM(dims, dtype)


def in_hbm(value):
    return pltpu.with_memory_space_constraint(value, pltpu.HBM)


class Arriving:
    def __init__(self, copies, target):
        self.copies, self.target = copies, target
        for copy in copies:
            copy.start()

    def get(self):
        for copy in self.copies:
            copy.wait()
        self.copies = []
        return self.target


class Leaving:
    def __init__(self, copies, buffer):
        self.copies, self.buffer, self.sent = copies, buffer, False

    def __setitem__(self, where, value):
        self.buffer[where] = value

    def __getitem__(self, where):
        return self.buffer[where]

    def send(self):
        for copy in self.copies:
            copy.start()
        self.sent = True


class Chunks:
    def __init__(self, rows):
        self.buffer = shape((4, rows, WIDE))
        cut = 80 if rows == ATTN else 64
        self.parts = [(z, start, end) for z in range(4) for start, end in ((0, cut), (cut, rows))]
        self.shapes = [shape((end - start, WIDE)) for _, start, end in self.parts]

    def views(self, buffer):
        return [buffer.at[z, start:end] for z, start, end in self.parts]


def call(kernel, name, ins, outs, scratches=(), limit=32):
    def arrays(item):
        return item.shapes if isinstance(item, Chunks) else [item]

    def buffer_of(item):
        held = item.buffer if isinstance(item, Chunks) else item
        return scratch(held.shape, held.dtype)

    loads = [i for i in ins if not isinstance(i, str)]
    stores = [o for where, o in outs if where == "h"]
    specs = {"v": VMEM, "s": SMEM, "r": HBM, "h": HBM, "a": ANY}
    in_specs, pinned = [], []
    for i in ins:
        count = 1 if isinstance(i, str) else len(arrays(i))
        in_specs += [specs[i] if isinstance(i, str) else HBM] * count
        pinned += [i == "r" or not isinstance(i, str)] * count
    out_specs, out_shapes = [], []
    for where, o in outs:
        for one in arrays(o):
            out_specs.append(specs[where])
            out_shapes.append(pltpu.HBM(one.shape, one.dtype) if where == "h" else one)
    n_loads = sum(len(arrays(i)) for i in loads)
    n_stores = sum(len(arrays(o)) for o in stores)

    def views(item, buffer):
        return item.views(buffer) if isinstance(item, Chunks) else [buffer]

    def body(after, *refs):
        refs = list(refs)
        in_refs = [refs.pop(0) for _ in in_specs]
        del refs[:after]
        out_refs = [refs.pop(0) for _ in out_specs]
        load_bufs = [refs.pop(0) for _ in loads]
        store_bufs = [refs.pop(0) for _ in stores]
        load_sems = refs.pop(0) if loads else None
        store_sems = refs.pop(0) if stores else None
        operands, results, n = [], [], 0
        for kind in ins:
            if isinstance(kind, str):
                operands.append(in_refs.pop(0))
                continue
            target, copies = load_bufs.pop(0), []
            for view in views(kind, target):
                copies.append(pltpu.make_async_copy(in_refs.pop(0), view, load_sems.at[n]))
                n += 1
            operands.append(Arriving(copies, target))
        n = 0
        for where, o in outs:
            if where == "v":
                results.append(out_refs.pop(0))
                continue
            buffer, copies = store_bufs.pop(0), []
            for view in views(o, buffer):
                copies.append(pltpu.make_async_copy(view, out_refs.pop(0), store_sems.at[n]))
                n += 1
            results.append(Leaving(copies, buffer))
        kernel(*operands, *results, *refs)
        for operand in operands:
            if isinstance(operand, Arriving):
                operand.get()
        leaving = [result for result in results if isinstance(result, Leaving)]
        for result in leaving:
            if not result.sent:
                result.send()
        for result in leaving:
            for copy in result.copies:
                copy.wait()

    def run(*operands):
        after = len(operands) - len(in_specs)
        operands = [
            in_hbm(operand) if pin else operand
            for pin, operand in zip(pinned + [True] * after, operands)
        ]
        return pl.pallas_call(
            partial(body, after),
            name=name,
            in_specs=in_specs + [ANY] * after,
            out_specs=tuple(out_specs),
            out_shape=tuple(out_shapes),
            scratch_shapes=[buffer_of(item) for item in loads + stores]
            + ([DMA((n_loads,))] if loads else [])
            + ([DMA((n_stores,))] if stores else [])
            + list(scratches),
            compiler_params=pltpu.CompilerParams(vmem_limit_bytes=limit << 20),
            cost_estimate=pl.CostEstimate(flops=0, bytes_accessed=0, transcendentals=0),
        )(*operands)

    return run


def hold(value, *after):
    return pl.pallas_call(
        lambda *refs: None,
        name="hold",
        in_specs=[HBM] + [ANY] * len(after),
        out_specs=HBM,
        out_shape=pltpu.HBM(value.shape, value.dtype),
        input_output_aliases={0: 0},
    )(in_hbm(value), *after)


def stamp(*values):
    def kernel(*refs):
        refs[-1][...] = jnp.zeros((8, 128), F32)

    return pl.pallas_call(
        kernel,
        name="stamp",
        in_specs=[ANY] * len(values),
        out_specs=VMEM,
        out_shape=shape((8, 128), F32),
        compiler_params=pltpu.CompilerParams(vmem_limit_bytes=16 << 20),
        cost_estimate=pl.CostEstimate(flops=0, bytes_accessed=0, transcendentals=0),
    )(*values)


def zero_after(after):
    def kernel(after, out):
        out[0] = 0

    return pl.pallas_call(
        kernel,
        name="zero",
        in_specs=[ANY],
        out_specs=SMEM,
        out_shape=shape((1,), jnp.int32),
    )(after)[0]


def at_rows(rows, values):
    place = lax.broadcasted_iota(jnp.int32, (rows, values[0].shape[1]), 0)
    block = jnp.zeros((rows, values[0].shape[1]), F32)
    for i, value in enumerate(values):
        block = jnp.where(place == i, value, block)
    return block


def columns(i, width=256):
    return pl.ds(pl.multiple_of(i * width, width), width)


def prep_attn_kernel(
    place, wq, wk, wv, wo, bq, bv, bu, v0, v1, v2, v3, v4, v5, own, peer, turned
):
    core, quarter = place[0], place[1]
    for a, w in enumerate((wq, wk, wv)):
        turned[a] = w.get()[0].T
    layer_rows = [v.get()[...].astype(F32) for v in (v0, v1, v2, v3, v4, v5)]
    wo, bq, bv, bu = wo.get(), bq.get(), bv.get(), bu.get()
    source = lax.broadcasted_iota(jnp.int32, (256, 128), 0)
    lane = lax.broadcasted_iota(jnp.int32, (256, 128), 1)
    for out, block in ((own, quarter), (peer, quarter ^ 1)):
        head = pl.multiple_of(block * HD + core * HALF, HALF)
        for a in range(3):
            out[HALF * a : HALF * a + HALF] = turned[a, pl.ds(head, HALF)]
        out[3 * HALF : 4 * HALF] = wo[0, pl.ds(head, HALF)]
        inner = lane & 63
        wanted = block * HD + (inner ^ (core * HALF))
        hit = source == wanted
        zero = jnp.zeros((256, 128), F32)
        one = jnp.ones((256, 128), F32)
        first = jnp.where(hit & (lane < 64), one, zero).astype(BF16)
        second = jnp.where(hit & (lane >= 64), one, zero).astype(BF16)
        bias = dot_nn(jnp.broadcast_to(bq[...], (16, 256)), first) + dot_nn(
            jnp.broadcast_to(bv[...], (16, 256)), second
        )
        rows = lax.broadcasted_iota(jnp.int32, (16, WIDE), 0)
        block_rows = jnp.zeros((16, WIDE), F32)
        for i, row in enumerate(layer_rows):
            block_rows = jnp.where(rows == i + 1, row, block_rows)
        out[128:144] = block_rows.astype(BF16)
        first_row = lax.broadcasted_iota(jnp.int32, (16, 128), 0) == 0
        out[128:144, 0:128] = jnp.where(first_row, bias, block_rows[:, 0:128]).astype(BF16)
        for h in range(2):
            unit = pl.multiple_of(block * 256 + (core ^ h) * 128, 128)
            lanes = slice(128 * (h + 1), 128 * (h + 2))
            piece = jnp.where(first_row, bu[:, pl.ds(unit, 128)].astype(F32), block_rows[:, lanes])
            out[128:144, lanes] = piece.astype(BF16)


def pick_kernel(place, own, got, out):
    own, got = own.get(), got.get()
    out[...] = jnp.where(jnp.full(own.shape, place[2]) == 0, own[...], got[...])


def prep_feed_kernel(place, up, down, own, peer, column, sems):
    core, quarter = place[0], place[1]
    copies = []
    outs = ((own, quarter), (peer, quarter ^ 1))
    for i, (out, block) in enumerate(outs):
        unit = pl.multiple_of(block * 256 + core * 128, 128)
        copies.append(
            pltpu.make_async_copy(up.at[0, :, pl.ds(unit, 128)], column.at[i], sems.at[2 * i])
        )
        copies.append(
            pltpu.make_async_copy(
                down.at[0, pl.ds(unit, 128)],
                out.buffer.at[FEED : 2 * FEED],
                sems.at[2 * i + 1],
            )
        )
    for copy in copies:
        copy.start()
    for i, (out, _) in enumerate(outs):
        copies[2 * i].wait()
        out[0:FEED] = column[i].T
        copies[2 * i + 1].wait()
        out.send()


def rows_of(ref, *which):
    block = ref[...].astype(F32)
    return [block[i : i + 1] for i in which]


def norm_forward(hidden, gain, offset):
    centre = jnp.mean(hidden, -1, keepdims=True)
    centred = hidden - centre
    variance = jnp.mean(centred * centred, -1, keepdims=True)
    inverse = lax.rsqrt(variance + EPSILON)
    normed = centred * inverse
    return (normed * gain + offset, normed, inverse)


def norm_backward(upstream, normed, inverse, gain):
    scaled = upstream * gain
    return inverse * (
        scaled
        - jnp.mean(scaled, -1, keepdims=True)
        - normed * jnp.mean(scaled * normed, -1, keepdims=True)
    )


def received(own, r1, r2, r3):
    return own[...] + r1[...].astype(F32) + r2[...].astype(F32) + r3[...].astype(F32)


def norm_kernel(first, own, r1, r2, r3, residual, vec, value, low, normed, inverse):
    bias, gain, offset = rows_of(vec, *((1, 2, 3) if first else (4, 5, 6)))
    hidden = residual[...].astype(F32) + received(own, r1, r2, r3) + bias
    result, flat, scale = norm_forward(hidden, gain, offset)
    low[...] = result.astype(BF16)
    value[...] = result
    normed[...] = flat.astype(BF16)
    inverse[...] = scale


def sums(*values):
    return at_rows(8, [jnp.sum(v, 0, keepdims=True) for v in values])


def norm_back(grad, gain, normed, inverse, total, low, vectors):
    flat = normed.get()[...].astype(F32)
    value = norm_backward(grad, flat, inverse.get()[...], gain)
    rounded = value.astype(BF16)
    low[...] = rounded
    total[...] = value
    total.send()
    vectors[...] = sums(rounded.astype(F32), grad * flat, grad)


def norm_two_back_kernel(upstream, vec, normed, inverse, total, low, vectors):
    (gain,) = rows_of(vec, 5)
    norm_back(upstream[...].astype(F32), gain, normed, inverse, total, low, vectors)


def norm_two_back_sum_kernel(
    own, r1, r2, r3, vec, before, normed, inverse, total, low, vectors, given
):
    (gain,) = rows_of(vec, 5)
    rounded = (before.get()[...] + received(own, r1, r2, r3)).astype(BF16)
    norm_back(rounded.astype(F32), gain, normed, inverse, total, low, vectors)
    given[...] = rounded


def norm_one_back_kernel(own, r1, r2, r3, vec, before, normed, inverse, total, low, vectors):
    (gain,) = rows_of(vec, 2)
    grad = before.get()[...] + received(own, r1, r2, r3)
    norm_back(grad, gain, normed, inverse, total, low, vectors)


def last_sum_kernel(own, r1, r2, r3, before, given):
    given[...] = (before.get()[...] + received(own, r1, r2, r3)).astype(BF16)


def load_attn(own, other, weight, sems):
    return [
        pltpu.make_async_copy(
            ref.at[:, HALF * a : HALF * a + HALF], weight.at[a, :, half], sems.at[4 * half + a]
        )
        for half, ref in enumerate((own, other))
        for a in range(4)
    ]


def join(target, pieces, sems):
    copies = [
        pltpu.make_async_copy(piece, target.at[SHARE * i : SHARE * i + SHARE], sems.at[i])
        for i, piece in enumerate(pieces)
    ]
    for copy in copies:
        copy.start()
    return copies


def arrive(copies):
    for copy in copies:
        copy.wait()


def spread_out(value, where, own, parts):
    own[:, where] = value[0:SHARE]
    for i, part in enumerate(parts):
        part[:, where] = value[SHARE * (i + 1) : SHARE * (i + 2)].astype(BF16)


def by_share(left, right, own, parts):
    for i in (3, 2, 1, 0):
        value = dot_nn(left[SHARE * i : SHARE * i + SHARE], right)
        if i:
            parts[i - 1][...] = value.astype(BF16)
        else:
            own[...] = value


def attn_kernel(
    x0, x1, x2, x3, id_row, a_own, a_other,
    own, p1, p2, p3, qkv, probs, mixed, x_out, weight_out,
    small, sems, x_sems,
):
    weight, x_all = weight_out.buffer, x_out.buffer
    copies = load_attn(a_own, a_other, weight, sems)
    copies.append(pltpu.make_async_copy(a_own.at[:, 128:144], small, sems.at[8]))
    for copy in copies:
        copy.start()
    arrive(join(x_all, (x0, x1, x2, x3), x_sems))
    x_out.send()
    arrive(copies)
    weight_out.send()
    ids = id_row[...]
    id_column = jnp.broadcast_to(ids, (128, SEQ)).T[:, 0:1]
    biases = [small[z].astype(F32)[0:1] for z in range(4)]
    bias_of = (
        jnp.concatenate([b[:, 0:64] for b in biases], 1),
        None,
        jnp.concatenate([b[:, 64:128] for b in biases], 1),
    )
    x = x_all[...]
    for a in range(3):
        rows = dot_nt(x, weight[a].reshape(256, WIDE))
        if bias_of[a] is not None:
            rows = rows + bias_of[a]
        qkv[:, 256 * a : 256 * a + 256] = rows.astype(BF16)
    qkv.send()
    for c in range(2):
        q_rows = slice(256 * c, 256 * c + 256)
        allowed = id_column[q_rows] == ids
        for h in range(HEADS):
            query = qkv[q_rows, HD * h : HD * h + HD]
            key = qkv[:, 256 + HD * h : 256 + HD * h + HD]
            value = qkv[:, 512 + HD * h : 512 + HD * h + HD]
            scores = jnp.where(allowed, dot_nt(query, key) * HD ** (-0.5), NEGATIVE)
            exponent = jnp.exp(scores - jnp.max(scores, -1, keepdims=True))
            low = (exponent / jnp.sum(exponent, -1, keepdims=True)).astype(BF16)
            probs[h, q_rows] = low
            mixed[q_rows, HD * h : HD * h + HD] = dot_nn(low, value).astype(BF16)
    probs.send()
    mixed.send()
    by_share(mixed, weight[3].reshape(256, WIDE), own, (p1, p2, p3))


def attn_back_kernel(
    g0, g1, g2, g3, weight, qkv, probs, own, p1, p2, p3, d_rows, g_out, x_sems
):
    g_all = g_out.buffer
    arrive(join(g_all, (g0, g1, g2, g3), x_sems))
    g_out.send()
    weight, qkv, probs = weight.get(), qkv.get(), probs.get()
    d_mixed = dot_nt(g_all[...], weight[3].reshape(256, WIDE)).astype(BF16)
    scale = HD ** (-0.5)
    for h in range(HEADS):
        query = qkv[:, HD * h : HD * h + HD]
        key = qkv[:, 256 + HD * h : 256 + HD * h + HD]
        value = qkv[:, 512 + HD * h : 512 + HD * h + HD]
        grad = d_mixed[:, HD * h : HD * h + HD]
        d_key = jnp.zeros((SEQ, HD), F32)
        d_value = jnp.zeros((SEQ, HD), F32)
        for c in range(2):
            q_rows = slice(256 * c, 256 * c + 256)
            low = probs[h, q_rows]
            p = low.astype(F32)
            d_probs = dot_nt(grad[q_rows], value)
            inner = jnp.sum(p * d_probs, -1, keepdims=True)
            d_scores = (p * (d_probs - inner)).astype(BF16)
            d_rows[q_rows, HD * h : HD * h + HD] = (dot_nn(d_scores, key) * scale).astype(BF16)
            d_key = d_key + dot_tn(d_scores, query[q_rows])
            d_value = d_value + dot_tn(low, grad[q_rows])
        d_rows[:, 256 + HD * h : 256 + HD * h + HD] = (d_key * scale).astype(BF16)
        d_rows[:, 512 + HD * h : 512 + HD * h + HD] = d_value.astype(BF16)
    d_rows.send()
    by_share(d_rows, weight[0:3].reshape(768, WIDE), own, (p1, p2, p3))


def attn_weights_kernel(
    d_rows, mixed, x_all, g_all, vec_one, vec_two, feed_bias, own, other
):
    operands = (d_rows, mixed, x_all, g_all, vec_one, vec_two, feed_bias)
    d_rows, mixed, x_all, g_all, vec_one, vec_two, feed_bias = (
        operand.get() for operand in operands
    )
    for a in range(4):
        if a < 3:
            value = dot_tn(d_rows[:, 256 * a : 256 * a + 256], x_all[...])
        else:
            value = dot_tn(mixed[...], g_all[...])
        value = value.astype(BF16).reshape(4, 2, HALF, WIDE)
        own[:, HALF * a : HALF * a + HALF] = value[:, 0]
        other[:, HALF * a : HALF * a + HALF] = value[:, 1]
    total = jnp.sum(d_rows[...].astype(F32), 0, keepdims=True)
    one, two = vec_one[...], vec_two[...]
    vectors = [one[i : i + 1] for i in range(3)] + [two[i : i + 1] for i in range(3)]
    block = at_rows(16, [jnp.zeros((1, WIDE), F32)] + vectors)
    first_row = lax.broadcasted_iota(jnp.int32, (16, 128), 0) == 0
    for half, out in ((1, other), (0, own)):
        for z in range(4):
            start = HD * z + HALF * half
            bias = jnp.concatenate(
                [
                    total[:, start : start + HALF],
                    total[:, 512 + start : 512 + start + HALF],
                    jnp.zeros((1, 64), F32),
                ],
                1,
            )
            out[z, 128:144] = block.astype(BF16)
            out[z, 128:144, 0:128] = jnp.where(first_row, bias, block[:, 0:128]).astype(BF16)
            unit = 512 * half + 128 * z
            piece = jnp.where(first_row, feed_bias[0:1, unit : unit + 128], block[:, 128:256])
            out[z, 128:144, 128:256] = piece.astype(BF16)
        out.send()


def load_feed(ups, downs, up, down, sems):
    copies = []
    for i, (refs, target) in enumerate(((ups, up), (downs, down))):
        for half in range(2):
            copies.append(
                pltpu.make_async_copy(
                    refs[half],
                    target.at[4 * half : 4 * half + 4],
                    sems.at[2 * i + half],
                )
            )
    return copies[:2], copies[2:]


def feed_kernel(
    x0, x1, x2, x3, a_own, up_own, up_other, down_own, down_other,
    own, p1, p2, p3, active, slope, x_out, up_out, down_out,
    small, bias, sems, x_sems,
):
    x_all, up, down = x_out.buffer, up_out.buffer, down_out.buffer
    ups, downs = load_feed((up_own, up_other), (down_own, down_other), up, down, sems)
    copies = [pltpu.make_async_copy(a_own.at[:, 128:144], small, sems.at[4])] + ups
    for copy in copies + downs:
        copy.start()
    arrive(join(x_all, (x0, x1, x2, x3), x_sems))
    x_out.send()
    arrive(copies)
    up_out.send()
    for half in range(2):
        for z in range(4):
            unit = 512 * half + 128 * z
            bias[0:8, unit : unit + 128] = jnp.broadcast_to(
                small[z, :, 128 * (half + 1) : 128 * (half + 2)].astype(F32)[0:1], (8, 128)
            )

    def units(i, carry):
        block = up[pl.ds(2 * i, 2)].reshape(256, WIDE)
        hidden = dot_nt(x_all[...], block) + bias[0:1, columns(i)]
        share = 0.5 * (1.0 + lax.erf(hidden * (0.5 ** 0.5)))
        density = jnp.exp(-0.5 * hidden * hidden) * 0.3989422804014327
        active[:, columns(i)] = (hidden * share).astype(BF16)
        slope[:, columns(i)] = (share + hidden * density).astype(BF16)
        return carry

    lax.fori_loop(0, 4, units, 0)
    active.send()
    slope.send()
    arrive(downs)
    down_out.send()

    def features(n, carry):
        block = down[:, :, columns(n)].reshape(WIDE, 256)
        spread_out(dot_nn(active[...], block), columns(n), own, (p1, p2, p3))
        return carry

    lax.fori_loop(0, 4, features, 0)


def feed_back_kernel(
    g0, g1, g2, g3, down, slope, up, own, p1, p2, p3, d_hidden, g_out, x_sems
):
    g_all = g_out.buffer
    arrive(join(g_all, (g0, g1, g2, g3), x_sems))
    g_out.send()
    down, slope = down.get(), slope.get()

    def units(i, carry):
        block = down[pl.ds(2 * i, 2)].reshape(256, WIDE)
        value = dot_nt(g_all[...], block) * slope[:, columns(i)].astype(F32)
        d_hidden[:, columns(i)] = value.astype(BF16)
        return carry

    lax.fori_loop(0, 4, units, 0)
    d_hidden.send()
    up = up.get()

    def features(n, carry):
        block = up[:, :, columns(n)].reshape(WIDE, 256)
        spread_out(dot_nn(d_hidden[...], block), columns(n), own, (p1, p2, p3))
        return carry

    lax.fori_loop(0, 4, features, 0)


def feed_weights_kernel(
    d_hidden, active, x_all, g_all, up_own, up_other, down_own, down_other, bias
):
    d_hidden, active, x_all, g_all = (v.get() for v in (d_hidden, active, x_all, g_all))
    for half, up, down in ((1, up_other, down_other), (0, up_own, down_own)):

        def pair(i, carry, half=half, up=up, down=down):
            where = columns(2 * half + i)
            value = dot_tn(d_hidden[:, where], x_all[...]).astype(BF16)
            up[pl.ds(2 * i, 2)] = value.reshape(2, 128, WIDE)
            value = dot_tn(active[:, where], g_all[...]).astype(BF16)
            down[pl.ds(2 * i, 2)] = value.reshape(2, 128, WIDE)
            return carry

        lax.fori_loop(0, 2, pair, 0)
        up.send()
        down.send()
    bias[...] = sums(d_hidden[...].astype(F32))


def assemble_kernel(place, x0, x1, x2, x3, out):
    for r, piece in enumerate((x0, x1, x2, x3)):
        out[place[3] ^ r] = piece[...]


def core_sum_feed_kernel(place, up, down, up_got, down_got, up_out, down_out):
    down_out[...] = (down.get()[...].astype(F32) + down_got[...].astype(F32)).astype(BF16)
    up_out[...] = (up.get()[...].astype(F32) + up_got[...].astype(F32)).astype(BF16)


def split_kernel(place, own, received, *outs):
    own = own.get()
    for r, out in enumerate(outs):
        z = place[3] ^ r
        out[...] = (own[z].astype(F32) + received[z].astype(F32)).astype(BF16)


def core_sum_kernel(*refs):
    count = len(refs) // 3
    for own, received, out in zip(refs[:count], refs[count : 2 * count], refs[2 * count :]):
        out[...] = (own.get()[...].astype(F32) + received[...].astype(F32)).astype(BF16)
        out.send()


def ordered(place):
    return [
        (4 * c + r, ((r ^ place[1]) * 2 + (c ^ place[0])).astype(jnp.int32))
        for c in range(2)
        for r in range(4)
    ]


def gathered(pieces, place, target, sems):
    copies = [
        pltpu.make_async_copy(pieces[i], target.at[to], sems.at[i]) for i, to in ordered(place)
    ]
    for copy in copies:
        copy.start()
    arrive(copies)


def finish_attn_kernel(place, *refs):
    pieces, refs = refs[:8], refs[8:]
    gq, gk, gv, go, bias_query, bias_value, bias_up, *vectors, block, sems = refs
    gathered(pieces, place, block, sems)
    for a, out in enumerate((gq, gk, gv)):
        rows = block[:, HALF * a : HALF * a + HALF].reshape(256, WIDE)
        out[0] = rows.astype(F32).T
        out.send()
    go[0] = block[:, 3 * HALF : 4 * HALF].reshape(256, WIDE).astype(F32)
    go.send()
    small = [block[i, 128:144].astype(F32) for i in range(8)]
    bias_query[...] = jnp.concatenate([v[0:1, 0:HALF] for v in small], 1)
    bias_value[...] = jnp.concatenate([v[0:1, HALF : 2 * HALF] for v in small], 1)
    for i in range(8):
        bias_up[:, 128 * i : 128 * i + 128] = small[i][0:1, 128:256]
    total = 0.5 * sum(small[1:], small[0])
    for i, out in enumerate(vectors):
        out[...] = total[i + 1 : i + 2]


def finish_up_kernel(place, *refs):
    pieces, refs = refs[:8], refs[8:]
    out, block, sems = refs
    gathered(pieces, place, block, sems)
    for i in range(8):
        out[0, :, 128 * i : 128 * i + 128] = block[i].astype(F32).T


def finish_down_kernel(place, *refs):
    pieces, refs = refs[:8], refs[8:]
    out, block, sems = refs
    gathered(pieces, place, block, sems)
    for i in range(8):
        out[0, 128 * i : 128 * i + 128] = block[i].astype(F32)


def finish_tokens_kernel(place, a, b, out):
    is_first = place[2] == 0

    @pl.when(is_first)
    def _():
        out[0, 0] = a[...].astype(out.buffer.dtype)
        out[0, 1] = b[...].astype(out.buffer.dtype)

    @pl.when(jnp.logical_not(is_first))
    def _():
        out[0, 0] = b[...].astype(out.buffer.dtype)
        out[0, 1] = a[...].astype(out.buffer.dtype)


RAW = ["a"] * 4
WHOLE = shape((SEQ, WIDE))
BLOCKS = shape((8, 128, WIDE))
HEAD_ROWS = shape((4, 4, 2, HALF, WIDE))
TOKEN = shape((SHARE, WIDE))
WIDE_TOKEN = shape((SHARE, WIDE), F32)
ONE = shape((SHARE, 1), F32)
PARTS = [("v", WIDE_TOKEN)] + [("v", TOKEN)] * 3
ROW = shape((1, WIDE))
FOUR = DMA((4,))
MASK = shape((1, SEQ), F32)
VECTORS = shape((8, WIDE), F32)

prep_attn = call(
    prep_attn_kernel,
    "pack_attention",
    ["s"]
    + [shape((1, WIDE, 256))] * 3
    + [shape((1, 256, WIDE))]
    + [shape((1, 256))] * 2
    + [ROW] * 7,
    [("h", shape((ATTN, WIDE)))] * 2,
    [scratch((3, 256, WIDE))],
)
pick = call(
    pick_kernel,
    "pick",
    ["s"] + [shape((ATTN, WIDE))] * 2,
    [("h", shape((ATTN, WIDE)))],
)
prep_feed = call(
    prep_feed_kernel,
    "pack_feed",
    ["s", "r", "r"],
    [("h", shape((2 * FEED, WIDE)))] * 2,
    [scratch((2, WIDE, 128)), DMA((4,))],
)
norm_one, norm_two = (
    call(
        partial(norm_kernel, first),
        name,
        ["v"] * 6,
        [("v", WIDE_TOKEN), ("v", TOKEN), ("h", TOKEN), ("h", ONE)],
        )
    for first, name in ((True, "norm_one"), (False, "norm_two"))
)
BACKS = [("h", WIDE_TOKEN), ("v", TOKEN), ("h", VECTORS)]
norm_two_back = call(
    norm_two_back_kernel, "norm_two_back", ["v", "v", TOKEN, ONE], BACKS
)
norm_two_back_sum = call(
    norm_two_back_sum_kernel,
    "norm_two_back_sum",
    ["v"] * 5 + [WIDE_TOKEN, TOKEN, ONE],
    BACKS + [("h", TOKEN)],
)
norm_one_back = call(
    norm_one_back_kernel,
    "norm_one_back",
    ["v"] * 5 + [WIDE_TOKEN, TOKEN, ONE],
    BACKS,
)
last_sum = call(
    last_sum_kernel, "last_sum", ["v"] * 4 + [WIDE_TOKEN], [("h", TOKEN)]
)
attn_forward = call(
    attn_kernel,
    "attention",
    RAW + ["v", "a", "a"],
    PARTS
    + [
        ("h", shape((SEQ, 768))),
        ("h", shape((HEADS, SEQ, SEQ))),
        ("h", shape((SEQ, 256))),
        ("h", WHOLE),
        ("h", HEAD_ROWS),
    ],
    [scratch((4, 16, WIDE)), DMA((9,)), FOUR],
)
attn_backward = call(
    attn_back_kernel,
    "attention_back",
    RAW + [HEAD_ROWS, shape((SEQ, 768)), shape((HEADS, SEQ, SEQ))],
    PARTS + [("h", shape((SEQ, 768))), ("h", WHOLE)],
    [FOUR],
)
attn_weights = call(
    attn_weights_kernel,
    "attention_weights",
    [shape((SEQ, 768)), shape((SEQ, 256)), WHOLE, WHOLE] + [VECTORS] * 3,
    [("h", shape((4, ATTN, WIDE)))] * 2,
)
feed_forward = call(
    feed_kernel,
    "feed",
    RAW + ["a"] * 5,
    PARTS + [("h", WHOLE)] * 3 + [("h", BLOCKS)] * 2,
    [scratch((4, 16, WIDE)), scratch((8, WIDE), F32), DMA((5,)), FOUR],
)
feed_backward = call(
    feed_back_kernel,
    "feed_back",
    RAW + [BLOCKS, WHOLE, BLOCKS],
    PARTS + [("h", WHOLE)] * 2,
    [FOUR],
)
feed_weights = call(
    feed_weights_kernel,
    "feed_weights",
    [WHOLE] * 4,
    [("h", shape((4, FEED, WIDE)))] * 4 + [("h", VECTORS)],
)
FEED_HALVES = ["s", shape((4, FEED, WIDE)), shape((4, FEED, WIDE)), "v", "v"]
core_sum_feed = call(
    core_sum_feed_kernel,
    "core_sum_feed",
    FEED_HALVES,
    [("h", shape((4, FEED, WIDE))), ("h", shape((4, FEED, WIDE)))],
)
split_attn, split_down = (
    call(
        split_kernel,
        "core_split",
        ["s", shape((4, rows, WIDE)), "v"],
        [("v", shape((rows, WIDE)))] * 4,
    )
    for rows in (ATTN, FEED)
)
core_sum_up = call(
    core_sum_kernel,
    "core_sum_up",
    [shape((4, FEED, WIDE)), "v"],
    [("h", shape((4, FEED, WIDE)))],
)
assemble = call(
    assemble_kernel,
    "assemble",
    ["s"] + ["v"] * 4,
    [("h", shape((4, FEED, WIDE)))],
)
core_sum_attn = call(
    core_sum_kernel,
    "core_sum_attention",
    [shape((4, ATTN, WIDE)), "v"],
    [("h", shape((4, ATTN, WIDE)))],
)
EIGHT = DMA((8,))
finish_attn = call(
    finish_attn_kernel,
    "finish_attention",
    ["s"] + ["a"] * 8,
    [("h", shape((1, WIDE, 256), F32))] * 3
    + [("h", shape((1, 256, WIDE), F32))]
    + [("h", shape((1, 256), F32))] * 2
    + [("h", shape((1, WIDE), F32))] * 7,
    [scratch((8, ATTN, WIDE)), EIGHT],
)
finish_up = call(
    finish_up_kernel,
    "finish_up",
    ["s"] + ["a"] * 8,
    [("h", shape((1, WIDE, WIDE), F32))],
    [scratch((8, FEED, WIDE)), EIGHT],
)
finish_down = call(
    finish_down_kernel,
    "finish_down",
    ["s"] + ["a"] * 8,
    [("h", shape((1, WIDE, WIDE), F32))],
    [scratch((8, FEED, WIDE)), EIGHT],
)
finish_tokens, finish_grads = (
    call(
        finish_tokens_kernel,
        name,
        ["s", "v", "v"],
        [("h", shape((1, 2, SHARE, WIDE), dtype))],
    )
    for name, dtype in (("finish_tokens", BF16), ("finish_grads", F32))
)


def mover(sizes, target, takes=None):
    replicas, sections, shards = sizes
    pairs = []
    for d in range(replicas):
        for s in range(sections):
            for z in range(shards):
                if takes is None or takes(d, s, z):
                    nd, ns, nz = target(d, s, z)
                    pairs.append(
                        ((d * sections + s) * shards + z, (nd * sections + ns) * shards + nz)
                    )

    def move(values):
        return lax.ppermute(values, AXES, pairs)

    return move


def solution(mesh):
    replicas, sections, shards = (mesh.shape[name] for name in AXES)
    sizes = (replicas, sections, shards)

    def block_of(d, s):
        return 2 * ((d >> 1) & 1) + s

    def quarter_of(d, s, z):
        return (block_of(d, s) + z) % 4

    swap_y = mover(sizes, lambda d, s, z: (d, s ^ 1, z))
    swap_x = mover(sizes, lambda d, s, z: (d ^ 2, s, z))
    swap_xy = mover(sizes, lambda d, s, z: (d ^ 2, s ^ 1, z))
    swap_core = mover(sizes, lambda d, s, z: (d ^ 1, s, z))
    swap_z = [mover(sizes, lambda d, s, z, r=r: (d, s, z ^ r)) for r in range(1, 4)]
    def into_place(d, s, z):
        x = (d >> 1) & 1
        micro = s ^ ((z - x) & 1)
        plane = 2 * micro + x
        block = (z - plane) % 4
        return (d & ~2) | ((block >> 1) << 1), block & 1, plane

    place_in = mover(sizes, into_place)
    place_out = [
        mover(
            sizes,
            lambda d, s, z, r=r: (
                (d & ~2) | ((z & 1) << 1),
                (z >> 1) ^ r,
                quarter_of(d, s, z),
            ),
        )
        for r in range(2)
    ]

    def gather(share):
        return (share, swap_y(share), swap_x(share), swap_xy(share))

    def scatter(parts):
        own, p1, p2, p3 = parts
        return (own, swap_y(p1), swap_x(p2), swap_xy(p3))

    def gather_direct(place, piece):
        return assemble(place, piece, *[move(piece) for move in swap_z])[0]

    def gather_mp(piece):
        return lax.all_gather(piece, "mp", axis=0)

    def scatter_mp(pieces):
        return lax.psum_scatter(pieces, "mp", scatter_dimension=0)

    def to_layers(first, second):
        is_first = (lax.axis_index("mp") >> 1) == 0
        return (
            place_out[0](jnp.where(is_first, first, second)),
            place_out[1](jnp.where(is_first, second, first)),
        )

    def per_device(
        inputs,
        cotangent,
        doc_ids,
        w_query,
        b_query,
        w_key,
        w_value,
        b_value,
        w_out,
        b_out,
        gain_one,
        shift_one,
        w_up,
        b_up,
        w_down,
        b_down,
        gain_two,
        shift_two,
    ):
        replica = lax.axis_index("dp")
        section = lax.axis_index("section")
        shard = lax.axis_index("mp")
        core = replica & 1
        block = block_of(replica, section)
        place = jnp.stack([core, block, section, shard]).astype(jnp.int32)

        attn_own, attn_peer = prep_attn(
            place,
            w_query,
            w_key,
            w_value,
            w_out,
            b_query,
            b_value,
            b_up,
            b_out,
            gain_one,
            shift_one,
            b_down,
            gain_two,
            shift_two,
        )
        attn_got = swap_y(attn_peer)
        which = section ^ ((shard - ((replica >> 1) & 1)) & 1)
        share_in = place_in(lax.dynamic_index_in_dim(inputs, which, 0, False))
        other_ids = swap_x(doc_ids)
        (attn_zero,) = pick(place, attn_own, attn_got, share_in, other_ids)
        whole_in = gather(share_in)
        feed_own, feed_peer = prep_feed(
            place, w_up, w_down, attn_zero, stamp(*whole_in[1:])
        )
        feed_got = swap_y(feed_peer)

        def of_layer(layer, own, got):
            return jnp.where(section == layer, own, got)

        attn_zero = gather_mp(attn_zero)
        attn_zero = (attn_zero, swap_core(attn_zero))
        feed_packs = [of_layer(layer, feed_own, feed_got) for layer in range(2)]
        up_zero = gather_mp(feed_packs[0][:FEED])
        down_zero = gather_direct(place, feed_packs[0][FEED:])
        attn_one = gather_mp(of_layer(1, attn_own, attn_got))
        up_one = gather_mp(feed_packs[1][:FEED])
        down_one = gather_mp(feed_packs[1][FEED:])

        mine = ((replica >> 1) & 1) == (shard & 1)
        ids = jnp.where(mine, doc_ids, other_ids)
        ids = lax.dynamic_index_in_dim(ids, shard >> 1, 0, False).reshape(4, SHARE)
        ids = jnp.concatenate(
            [
                lax.dynamic_index_in_dim(ids, ((block ^ r) + shard) % 4, 0, False)
                for r in range(4)
            ]
        )
        id_row = ids.astype(F32)[None, :]

        def attn_half(share, whole, weights, vec, *after):
            *parts, qkv, probs, mixed, whole, weights = attn_forward(*whole, id_row, *weights, *after)
            parts = scatter(parts)
            middle, low, normed, inverse = norm_one(*parts, share, vec)
            return middle, low, (whole, qkv, probs, mixed, normed, inverse, weights)

        def feed_half(middle, spread, weights, vec):
            *parts, active, slope, spread, up, down = feed_forward(*spread, *weights)
            parts = scatter(parts)
            _, result, normed, inverse = norm_two(*parts, middle, vec)
            return result, (spread, active, slope, normed, inverse, up, down)

        vec_zero = attn_zero[0][0, 128:144]
        middle, low, kept_attn_zero = attn_half(share_in, whole_in, attn_zero, vec_zero)
        spread = gather(low)
        up_zero = hold(up_zero, low)
        down_zero = hold(down_zero, stamp(*spread[1:]))
        feed_zero = (attn_zero[0], up_zero, swap_core(up_zero), down_zero, swap_core(down_zero))
        first, kept_feed_zero = feed_half(middle, spread, feed_zero, vec_zero)

        whole = gather(first)
        attn_one = hold(attn_one, first)
        vec_one = attn_one[0, 128:144]
        attn_one = (attn_one, swap_core(attn_one))
        middle, low, kept_attn_one = attn_half(first, whole, attn_one, vec_one)
        spread = gather(low)
        up_one = hold(up_one, low)
        down_one = hold(down_one, low)
        feed_one = (attn_one[0], up_one, swap_core(up_one), down_one, swap_core(down_one))
        grad_which = which ^ zero_after(kept_attn_zero[1])
        share_grad = place_in(lax.dynamic_index_in_dim(cotangent, grad_which, 0, False))
        second, kept_feed_one = feed_half(middle, spread, feed_one, vec_one)

        def feed_half_back(low, kept, *after):
            spread, active, slope, _, _, up, down = kept
            grads = gather(low)
            *parts, d_hidden, grads = feed_backward(*grads, down, slope, up, *after)
            parts = scatter(parts)
            return parts, feed_weights(d_hidden, active, spread, grads), d_hidden

        def attn_half_back(grads, kept, *after):
            _, qkv, probs, _, _, _, weights = kept
            *parts, d_rows, grads = attn_backward(*grads, weights, qkv, probs, *after)
            return parts, d_rows, grads

        def feed_sum(total, halves, start, *after):
            up, up_other, down, down_other, _ = halves
            received = [swap_core(hold(other, start)) for other in (up_other, down_other)]
            return total(place, up, down, *received, *after)

        total, low, vec_two = norm_two_back(
            share_grad, vec_one, kept_feed_one[3], kept_feed_one[4]
        )
        parts, halves, _ = feed_half_back(low, kept_feed_one)
        feed_bias = halves[4]
        outputs = to_layers(first, second)
        total, low, vec_first = norm_one_back(
            *parts, vec_one, total, kept_attn_one[4], kept_attn_one[5], halves[0], *outputs
        )
        (section_outputs,) = finish_tokens(place, *outputs)
        grads = gather(low)
        halves = feed_sum(core_sum_feed, halves, low)
        ready = stamp(*grads[1:], in_hbm(halves[0]))
        parts, d_rows, grads = attn_half_back(grads, kept_attn_one, ready)
        parts = scatter(parts)
        up_grad_one, down_grad_one = [scatter_mp(hold(part, ready)) for part in halves]
        own, other = attn_weights(
            d_rows, kept_attn_one[3], kept_attn_one[0], grads, vec_first, vec_two, feed_bias
        )
        total, low, vec_two, grad_one = norm_two_back_sum(
            *parts, vec_zero, total, kept_feed_zero[3], kept_feed_zero[4], own
        )
        (attn_grad_one,) = core_sum_attn(own, swap_core(hold(other, low)))
        parts, halves, d_hidden = feed_half_back(
            low, kept_feed_zero, attn_grad_one, up_grad_one
        )
        attn_grad_one = hold(attn_grad_one, d_hidden)
        total, low, vec_first = norm_one_back(
            *parts,
            vec_zero,
            total,
            kept_attn_zero[4],
            kept_attn_zero[5],
            halves[0],
            down_grad_one,
        )
        grads = gather(low)
        attn_grad_one = scatter_mp(attn_grad_one)
        up, up_other, down, down_other, feed_bias = halves
        (up,) = core_sum_up(up, swap_core(hold(up_other, low)))
        ready = stamp(*grads[1:], in_hbm(up))
        parts, d_rows, grads = attn_half_back(grads, kept_attn_zero, ready, attn_grad_one)
        up_grad_zero = scatter_mp(hold(up, ready))
        own, other = attn_weights(
            d_rows,
            kept_attn_zero[3],
            kept_attn_zero[0],
            grads,
            vec_first,
            vec_two,
            feed_bias,
        )
        attn_parts = split_attn(place, own, swap_core(other))
        down_parts = split_down(place, down, swap_core(hold(down_other, low)))
        parts = scatter(parts[:1] + [hold(part, attn_parts[1]) for part in parts[1:]])

        def scatter_direct(parts, *after):
            moved = [move(hold(part, *after)) for move, part in zip(swap_z, parts[1:])]
            total = sum((part.astype(F32) for part in moved), parts[0].astype(F32))
            return total.astype(BF16), stamp(*moved)

        down_grad_zero, down_there = scatter_direct(down_parts, up_grad_zero)
        attn_grad_zero, attn_there = scatter_direct(attn_parts, down_there)
        (grad_zero,) = last_sum(*parts, total)

        def exchange(zero, one, *after):
            if replicas > 4:
                groups = [[low + 4 * high for high in range(replicas // 4)] for low in range(4)]
                zero, one = lax.psum((zero, one), "dp", axis_index_groups=groups)
            mine = jnp.where(section == 0, zero, one)
            theirs = jnp.where(section == 0, one, zero)
            if after:
                mine, theirs = hold(mine, *after), hold(theirs, *after)
            pieces = [mine, swap_y(theirs), swap_x(mine), swap_xy(theirs)]
            return pieces + [swap_core(piece) for piece in pieces]

        moved = to_layers(hold(grad_zero, attn_there), grad_one)
        (section_input_grads,) = finish_grads(place, *moved)
        ups = exchange(up_grad_zero, up_grad_one, grad_zero)
        (g_up,) = finish_up(place, *ups)
        downs = exchange(down_grad_zero, down_grad_one)
        (g_down,) = finish_down(place, *downs)
        attns = exchange(attn_grad_zero, attn_grad_one)
        g_query, g_key, g_value, g_out, g_b_query, g_b_value, g_b_up, *vectors = finish_attn(place, *attns)
        return (
            section_outputs,
            section_input_grads,
            g_query,
            g_b_query,
            g_key,
            g_value,
            g_b_value,
            g_out,
            vectors[0],
            vectors[1],
            vectors[2],
            g_up,
            g_b_up,
            g_down,
            vectors[3],
            vectors[4],
            vectors[5],
        )

    vector = P("section", None)
    by_column = P("section", None, "mp")
    by_row = P("section", "mp", None)
    spread = P("section", "mp")
    tokens = P(None, ("dp", "mp"), None)
    layer_tokens = P("section", None, ("dp", "mp"), None)
    return jax.shard_map(
        per_device,
        mesh=mesh,
        in_specs=(
            tokens,
            tokens,
            P(None, "dp", None),
            by_column,
            spread,
            by_column,
            by_column,
            spread,
            by_row,
            vector,
            vector,
            vector,
            by_column,
            spread,
            by_row,
            vector,
            vector,
            vector,
        ),
        out_specs=(
            layer_tokens,
            layer_tokens,
            by_column,
            spread,
            by_column,
            by_column,
            spread,
            by_row,
            vector,
            vector,
            vector,
            by_column,
            spread,
            by_row,
            vector,
            vector,
            vector,
        ),
        check_vma=False,
    )
```

```python
from functools import partial

import jax
import jax.numpy as jnp
from jax import lax
from jax.experimental import pallas as pl
from jax.experimental.pallas import tpu as pltpu
from jax.sharding import PartitionSpec as P

HD = 64
SEQ = 512
SHARE = 128
WIDE = 1024
HEADS = 4
HALF = 32
ATTN = 144
FEED = 128
AXES = ("dp", "section", "mp")
EPSILON = 1e-05
NEGATIVE = -1e30
F32 = jnp.float32
BF16 = jnp.bfloat16
VMEM = pl.BlockSpec(memory_space=pltpu.VMEM)
ANY = pl.BlockSpec(memory_space=pl.ANY)
HBM = pl.BlockSpec(memory_space=pltpu.HBM)
SMEM = pl.BlockSpec(memory_space=pltpu.SMEM)


def dot_nt(left, right):
    return lax.dot_general(left, right, (((1,), (1,)), ((), ())), preferred_element_type=F32)


def dot_nn(left, right):
    return lax.dot_general(left, right, (((1,), (0,)), ((), ())), preferred_element_type=F32)


def dot_tn(left, right):
    return lax.dot_general(left, right, (((0,), (0,)), ((), ())), preferred_element_type=F32)


def shape(dims, dtype=BF16):
    return jax.ShapeDtypeStruct(dims, dtype)


DMA = pltpu.SemaphoreType.DMA


def scratch(dims, dtype=BF16):
    return pltpu.VMEM(dims, dtype)


def in_hbm(value):
    return pltpu.with_memory_space_constraint(value, pltpu.HBM)


class Arriving:
    def __init__(self, copies, target):
        self.copies, self.target = copies, target
        for copy in copies:
            copy.start()

    def get(self):
        for copy in self.copies:
            copy.wait()
        self.copies = []
        return self.target


class Leaving:
    def __init__(self, copies, buffer):
        self.copies, self.buffer, self.sent = copies, buffer, False

    def __setitem__(self, where, value):
        self.buffer[where] = value

    def __getitem__(self, where):
        return self.buffer[where]

    def send(self):
        for copy in self.copies:
            copy.start()
        self.sent = True


class Chunks:
    def __init__(self, rows):
        self.buffer = shape((4, rows, WIDE))
        cut = 80 if rows == ATTN else 64
        self.parts = [(z, start, end) for z in range(4) for start, end in ((0, cut), (cut, rows))]
        self.shapes = [shape((end - start, WIDE)) for _, start, end in self.parts]

    def views(self, buffer):
        return [buffer.at[z, start:end] for z, start, end in self.parts]


def call(kernel, name, ins, outs, scratches=(), limit=32):
    def arrays(item):
        return item.shapes if isinstance(item, Chunks) else [item]

    def buffer_of(item):
        held = item.buffer if isinstance(item, Chunks) else item
        return scratch(held.shape, held.dtype)

    loads = [i for i in ins if not isinstance(i, str)]
    stores = [o for where, o in outs if where == "h"]
    specs = {"v": VMEM, "s": SMEM, "r": HBM, "h": HBM, "a": ANY}
    in_specs, pinned = [], []
    for i in ins:
        count = 1 if isinstance(i, str) else len(arrays(i))
        in_specs += [specs[i] if isinstance(i, str) else HBM] * count
        pinned += [i == "r" or not isinstance(i, str)] * count
    out_specs, out_shapes = [], []
    for where, o in outs:
        for one in arrays(o):
            out_specs.append(specs[where])
            out_shapes.append(pltpu.HBM(one.shape, one.dtype) if where == "h" else one)
    n_loads = sum(len(arrays(i)) for i in loads)
    n_stores = sum(len(arrays(o)) for o in stores)

    def views(item, buffer):
        return item.views(buffer) if isinstance(item, Chunks) else [buffer]

    def body(after, *refs):
        refs = list(refs)
        in_refs = [refs.pop(0) for _ in in_specs]
        del refs[:after]
        out_refs = [refs.pop(0) for _ in out_specs]
        load_bufs = [refs.pop(0) for _ in loads]
        store_bufs = [refs.pop(0) for _ in stores]
        load_sems = refs.pop(0) if loads else None
        store_sems = refs.pop(0) if stores else None
        operands, results, n = [], [], 0
        for kind in ins:
            if isinstance(kind, str):
                operands.append(in_refs.pop(0))
                continue
            target, copies = load_bufs.pop(0), []
            for view in views(kind, target):
                copies.append(pltpu.make_async_copy(in_refs.pop(0), view, load_sems.at[n]))
                n += 1
            operands.append(Arriving(copies, target))
        n = 0
        for where, o in outs:
            if where == "v":
                results.append(out_refs.pop(0))
                continue
            buffer, copies = store_bufs.pop(0), []
            for view in views(o, buffer):
                copies.append(pltpu.make_async_copy(view, out_refs.pop(0), store_sems.at[n]))
                n += 1
            results.append(Leaving(copies, buffer))
        kernel(*operands, *results, *refs)
        for operand in operands:
            if isinstance(operand, Arriving):
                operand.get()
        leaving = [result for result in results if isinstance(result, Leaving)]
        for result in leaving:
            if not result.sent:
                result.send()
        for result in leaving:
            for copy in result.copies:
                copy.wait()

    def run(*operands):
        after = len(operands) - len(in_specs)
        operands = [
            in_hbm(operand) if pin else operand
            for pin, operand in zip(
                pinned + [o.size > 1 for o in operands[len(pinned) :]], operands
            )
        ]
        return pl.pallas_call(
            partial(body, after),
            name=name,
            in_specs=in_specs
            + [ANY if o.size > 1 else SMEM for o in operands[len(in_specs) :]],
            out_specs=tuple(out_specs),
            out_shape=tuple(out_shapes),
            scratch_shapes=[buffer_of(item) for item in loads + stores]
            + ([DMA((n_loads,))] if loads else [])
            + ([DMA((n_stores,))] if stores else [])
            + list(scratches),
            compiler_params=pltpu.CompilerParams(vmem_limit_bytes=limit << 20),
            cost_estimate=pl.CostEstimate(flops=0, bytes_accessed=0, transcendentals=0),
        )(*operands)

    return run


def hold(value, *after):
    return pl.pallas_call(
        lambda *refs: None,
        name="hold",
        in_specs=[HBM] + [ANY if o.size > 1 else SMEM for o in after],
        out_specs=HBM,
        out_shape=pltpu.HBM(value.shape, value.dtype),
        input_output_aliases={0: 0},
    )(in_hbm(value), *after)


def stamp(*values, kept=()):
    def kernel(*refs):
        refs[-1][0] = 0

    return pl.pallas_call(
        kernel,
        name="stamp",
        in_specs=[VMEM] * len(values) + [ANY] * len(kept),
        out_specs=SMEM,
        out_shape=shape((1,), jnp.int32),
        compiler_params=pltpu.CompilerParams(vmem_limit_bytes=16 << 20),
        cost_estimate=pl.CostEstimate(flops=0, bytes_accessed=0, transcendentals=0),
    )(*values, *[in_hbm(value) for value in kept])


def zero_after(after):
    def kernel(after, out):
        out[0] = 0

    return pl.pallas_call(
        kernel,
        name="zero",
        in_specs=[ANY],
        out_specs=SMEM,
        out_shape=shape((1,), jnp.int32),
    )(after)[0]


def at_rows(rows, values):
    place = lax.broadcasted_iota(jnp.int32, (rows, values[0].shape[1]), 0)
    block = jnp.zeros((rows, values[0].shape[1]), F32)
    for i, value in enumerate(values):
        block = jnp.where(place == i, value, block)
    return block


def columns(i, width=256):
    return pl.ds(pl.multiple_of(i * width, width), width)


def prep_attn_kernel(
    place, wq, wk, wv, wo, bq, bv, bu, v0, v1, v2, v3, v4, v5, own, peer, turned
):
    core, quarter = place[0], place[1]
    for a, w in enumerate((wq, wk, wv)):
        turned[a] = w.get()[0].T
    layer_rows = [v.get()[...].astype(F32) for v in (v0, v1, v2, v3, v4, v5)]
    wo, bq, bv, bu = wo.get(), bq.get(), bv.get(), bu.get()
    source = lax.broadcasted_iota(jnp.int32, (256, 128), 0)
    lane = lax.broadcasted_iota(jnp.int32, (256, 128), 1)
    for out, block in ((own, quarter), (peer, quarter ^ 1)):
        head = pl.multiple_of(block * HD + core * HALF, HALF)
        for a in range(3):
            out[HALF * a : HALF * a + HALF] = turned[a, pl.ds(head, HALF)]
        out[3 * HALF : 4 * HALF] = wo[0, pl.ds(head, HALF)]
        inner = lane & 63
        wanted = block * HD + (inner ^ (core * HALF))
        hit = source == wanted
        zero = jnp.zeros((256, 128), F32)
        one = jnp.ones((256, 128), F32)
        first = jnp.where(hit & (lane < 64), one, zero).astype(BF16)
        second = jnp.where(hit & (lane >= 64), one, zero).astype(BF16)
        bias = dot_nn(jnp.broadcast_to(bq[...], (16, 256)), first) + dot_nn(
            jnp.broadcast_to(bv[...], (16, 256)), second
        )
        rows = lax.broadcasted_iota(jnp.int32, (16, WIDE), 0)
        block_rows = jnp.zeros((16, WIDE), F32)
        for i, row in enumerate(layer_rows):
            block_rows = jnp.where(rows == i + 1, row, block_rows)
        out[128:144] = block_rows.astype(BF16)
        first_row = lax.broadcasted_iota(jnp.int32, (16, 128), 0) == 0
        out[128:144, 0:128] = jnp.where(first_row, bias, block_rows[:, 0:128]).astype(BF16)
        for h in range(2):
            unit = pl.multiple_of(block * 256 + (core ^ h) * 128, 128)
            lanes = slice(128 * (h + 1), 128 * (h + 2))
            piece = jnp.where(first_row, bu[:, pl.ds(unit, 128)].astype(F32), block_rows[:, lanes])
            out[128:144, lanes] = piece.astype(BF16)


def pick_kernel(place, own, got, out):
    own, got = own.get(), got.get()
    out[...] = jnp.where(jnp.full(own.shape, place[2]) == 0, own[...], got[...])


def prep_feed_kernel(place, up, down, own, peer, column, sems):
    core, quarter = place[0], place[1]
    copies = []
    outs = ((own, quarter), (peer, quarter ^ 1))
    for i, (out, block) in enumerate(outs):
        unit = pl.multiple_of(block * 256 + core * 128, 128)
        copies.append(
            pltpu.make_async_copy(up.at[0, :, pl.ds(unit, 128)], column.at[i], sems.at[2 * i])
        )
        copies.append(
            pltpu.make_async_copy(
                down.at[0, pl.ds(unit, 128)],
                out.buffer.at[FEED : 2 * FEED],
                sems.at[2 * i + 1],
            )
        )
    for copy in copies:
        copy.start()
    for i, (out, _) in enumerate(outs):
        copies[2 * i].wait()
        out[0:FEED] = column[i].T
        copies[2 * i + 1].wait()
        out.send()


def rows_of(ref, *which):
    block = ref[...].astype(F32)
    return [block[i : i + 1] for i in which]


def norm_forward(hidden, gain, offset):
    centre = jnp.mean(hidden, -1, keepdims=True)
    centred = hidden - centre
    variance = jnp.mean(centred * centred, -1, keepdims=True)
    inverse = lax.rsqrt(variance + EPSILON)
    normed = centred * inverse
    return (normed * gain + offset, normed, inverse)


def norm_backward(upstream, normed, inverse, gain):
    scaled = upstream * gain
    return inverse * (
        scaled
        - jnp.mean(scaled, -1, keepdims=True)
        - normed * jnp.mean(scaled * normed, -1, keepdims=True)
    )


def received(own, r1, r2, r3):
    return own[...] + r1[...].astype(F32) + r2[...].astype(F32) + r3[...].astype(F32)


def norm_kernel(first, own, r1, r2, r3, residual, vec, value, low, normed, inverse):
    bias, gain, offset = rows_of(vec, *((1, 2, 3) if first else (4, 5, 6)))
    hidden = residual[...].astype(F32) + received(own, r1, r2, r3) + bias
    result, flat, scale = norm_forward(hidden, gain, offset)
    low[...] = result.astype(BF16)
    value[...] = result
    normed[...] = flat.astype(BF16)
    inverse[...] = scale


def sums(*values):
    return at_rows(8, [jnp.sum(v, 0, keepdims=True) for v in values])


def norm_back(grad, gain, normed, inverse, total, low, vectors):
    flat = normed.get()[...].astype(F32)
    value = norm_backward(grad, flat, inverse.get()[...], gain)
    rounded = value.astype(BF16)
    low[...] = rounded
    total[...] = value
    total.send()
    vectors[...] = sums(rounded.astype(F32), grad * flat, grad)


def norm_two_back_kernel(upstream, vec, normed, inverse, total, low, vectors):
    (gain,) = rows_of(vec, 5)
    norm_back(upstream[...].astype(F32), gain, normed, inverse, total, low, vectors)


def norm_two_back_sum_kernel(
    own, r1, r2, r3, vec, before, normed, inverse, total, low, vectors, given
):
    (gain,) = rows_of(vec, 5)
    rounded = (before.get()[...] + received(own, r1, r2, r3)).astype(BF16)
    norm_back(rounded.astype(F32), gain, normed, inverse, total, low, vectors)
    given[...] = rounded


def norm_one_back_kernel(own, r1, r2, r3, vec, before, normed, inverse, total, low, vectors):
    (gain,) = rows_of(vec, 2)
    grad = before.get()[...] + received(own, r1, r2, r3)
    norm_back(grad, gain, normed, inverse, total, low, vectors)


def last_sum_kernel(own, r1, r2, r3, before, given):
    given[...] = (before.get()[...] + received(own, r1, r2, r3)).astype(BF16)


def load_attn(own, other, weight, sems):
    return [
        pltpu.make_async_copy(
            ref.at[:, HALF * a : HALF * a + HALF], weight.at[a, :, half], sems.at[4 * half + a]
        )
        for half, ref in enumerate((own, other))
        for a in range(4)
    ]


def join(target, pieces, sems):
    copies = [
        pltpu.make_async_copy(piece, target.at[SHARE * i : SHARE * i + SHARE], sems.at[i])
        for i, piece in enumerate(pieces)
    ]
    for copy in copies:
        copy.start()
    return copies


def arrive(copies):
    for copy in copies:
        copy.wait()


def spread_out(value, where, own, parts):
    own[:, where] = value[0:SHARE]
    for i, part in enumerate(parts):
        part[:, where] = value[SHARE * (i + 1) : SHARE * (i + 2)].astype(BF16)


def by_share(left, right, own, parts):
    for i in (3, 2, 1, 0):
        value = dot_nn(left[SHARE * i : SHARE * i + SHARE], right)
        if i:
            parts[i - 1][...] = value.astype(BF16)
        else:
            own[...] = value


def attn_kernel(
    x0, x1, x2, x3, id_row, a_own, a_other,
    own, p1, p2, p3, qkv, probs, mixed, x_out, weight_out,
    small, sems, x_sems,
):
    weight, x_all = weight_out.buffer, x_out.buffer
    copies = load_attn(a_own, a_other, weight, sems)
    copies.append(pltpu.make_async_copy(a_own.at[:, 128:144], small, sems.at[8]))
    for copy in copies:
        copy.start()
    arrive(join(x_all, (x0, x1, x2, x3), x_sems))
    x_out.send()
    arrive(copies)
    weight_out.send()
    ids = id_row[...]
    id_column = jnp.broadcast_to(ids, (128, SEQ)).T[:, 0:1]
    biases = [small[z].astype(F32)[0:1] for z in range(4)]
    bias_of = (
        jnp.concatenate([b[:, 0:64] for b in biases], 1),
        None,
        jnp.concatenate([b[:, 64:128] for b in biases], 1),
    )
    x = x_all[...]
    for a in range(3):
        rows = dot_nt(x, weight[a].reshape(256, WIDE))
        if bias_of[a] is not None:
            rows = rows + bias_of[a]
        qkv[:, 256 * a : 256 * a + 256] = rows.astype(BF16)
    qkv.send()
    for c in range(2):
        q_rows = slice(256 * c, 256 * c + 256)
        allowed = id_column[q_rows] == ids
        for h in range(HEADS):
            query = qkv[q_rows, HD * h : HD * h + HD]
            key = qkv[:, 256 + HD * h : 256 + HD * h + HD]
            value = qkv[:, 512 + HD * h : 512 + HD * h + HD]
            scores = jnp.where(allowed, dot_nt(query, key) * HD ** (-0.5), NEGATIVE)
            exponent = jnp.exp(scores - jnp.max(scores, -1, keepdims=True))
            low = (exponent / jnp.sum(exponent, -1, keepdims=True)).astype(BF16)
            probs[h, q_rows] = low
            mixed[q_rows, HD * h : HD * h + HD] = dot_nn(low, value).astype(BF16)
    probs.send()
    mixed.send()
    by_share(mixed, weight[3].reshape(256, WIDE), own, (p1, p2, p3))


def attn_back_kernel(
    g0, g1, g2, g3, weight, qkv, probs, own, p1, p2, p3, d_rows, g_out, x_sems
):
    g_all = g_out.buffer
    arrive(join(g_all, (g0, g1, g2, g3), x_sems))
    g_out.send()
    weight, qkv, probs = weight.get(), qkv.get(), probs.get()
    d_mixed = dot_nt(g_all[...], weight[3].reshape(256, WIDE)).astype(BF16)
    scale = HD ** (-0.5)
    for h in range(HEADS):
        query = qkv[:, HD * h : HD * h + HD]
        key = qkv[:, 256 + HD * h : 256 + HD * h + HD]
        value = qkv[:, 512 + HD * h : 512 + HD * h + HD]
        grad = d_mixed[:, HD * h : HD * h + HD]
        d_key = jnp.zeros((SEQ, HD), F32)
        d_value = jnp.zeros((SEQ, HD), F32)
        for c in range(2):
            q_rows = slice(256 * c, 256 * c + 256)
            low = probs[h, q_rows]
            p = low.astype(F32)
            d_probs = dot_nt(grad[q_rows], value)
            inner = jnp.sum(p * d_probs, -1, keepdims=True)
            d_scores = (p * (d_probs - inner)).astype(BF16)
            d_rows[q_rows, HD * h : HD * h + HD] = (dot_nn(d_scores, key) * scale).astype(BF16)
            d_key = d_key + dot_tn(d_scores, query[q_rows])
            d_value = d_value + dot_tn(low, grad[q_rows])
        d_rows[:, 256 + HD * h : 256 + HD * h + HD] = (d_key * scale).astype(BF16)
        d_rows[:, 512 + HD * h : 512 + HD * h + HD] = d_value.astype(BF16)
    d_rows.send()
    by_share(d_rows, weight[0:3].reshape(768, WIDE), own, (p1, p2, p3))


def attn_weights_kernel(
    d_rows, mixed, x_all, g_all, vec_one, vec_two, feed_bias, own, other
):
    operands = (d_rows, mixed, x_all, g_all, vec_one, vec_two, feed_bias)
    d_rows, mixed, x_all, g_all, vec_one, vec_two, feed_bias = (
        operand.get() for operand in operands
    )
    for a in range(4):
        if a < 3:
            value = dot_tn(d_rows[:, 256 * a : 256 * a + 256], x_all[...])
        else:
            value = dot_tn(mixed[...], g_all[...])
        value = value.astype(BF16).reshape(4, 2, HALF, WIDE)
        own[:, HALF * a : HALF * a + HALF] = value[:, 0]
        other[:, HALF * a : HALF * a + HALF] = value[:, 1]
    total = jnp.sum(d_rows[...].astype(F32), 0, keepdims=True)
    one, two = vec_one[...], vec_two[...]
    vectors = [one[i : i + 1] for i in range(3)] + [two[i : i + 1] for i in range(3)]
    block = at_rows(16, [jnp.zeros((1, WIDE), F32)] + vectors)
    first_row = lax.broadcasted_iota(jnp.int32, (16, 128), 0) == 0
    for half, out in ((1, other), (0, own)):
        for z in range(4):
            start = HD * z + HALF * half
            bias = jnp.concatenate(
                [
                    total[:, start : start + HALF],
                    total[:, 512 + start : 512 + start + HALF],
                    jnp.zeros((1, 64), F32),
                ],
                1,
            )
            out[z, 128:144] = block.astype(BF16)
            out[z, 128:144, 0:128] = jnp.where(first_row, bias, block[:, 0:128]).astype(BF16)
            unit = 512 * half + 128 * z
            piece = jnp.where(first_row, feed_bias[0:1, unit : unit + 128], block[:, 128:256])
            out[z, 128:144, 128:256] = piece.astype(BF16)
        out.send()


def load_feed(ups, downs, up, down, sems):
    copies = []
    for i, (refs, target) in enumerate(((ups, up), (downs, down))):
        for half in range(2):
            copies.append(
                pltpu.make_async_copy(
                    refs[half],
                    target.at[4 * half : 4 * half + 4],
                    sems.at[2 * i + half],
                )
            )
    return copies[:2], copies[2:]


def feed_kernel(
    x0, x1, x2, x3, a_own, up_own, up_other, down_own, down_other,
    own, p1, p2, p3, active, slope, x_out, up_out, down_out,
    small, bias, sems, x_sems,
):
    x_all, up, down = x_out.buffer, up_out.buffer, down_out.buffer
    ups, downs = load_feed((up_own, up_other), (down_own, down_other), up, down, sems)
    copies = [pltpu.make_async_copy(a_own.at[:, 128:144], small, sems.at[4])] + ups
    for copy in copies + downs:
        copy.start()
    arrive(join(x_all, (x0, x1, x2, x3), x_sems))
    x_out.send()
    arrive(copies)
    up_out.send()
    for half in range(2):
        for z in range(4):
            unit = 512 * half + 128 * z
            bias[0:8, unit : unit + 128] = jnp.broadcast_to(
                small[z, :, 128 * (half + 1) : 128 * (half + 2)].astype(F32)[0:1], (8, 128)
            )

    def units(i, carry):
        block = up[pl.ds(2 * i, 2)].reshape(256, WIDE)
        hidden = dot_nt(x_all[...], block) + bias[0:1, columns(i)]
        share = 0.5 * (1.0 + lax.erf(hidden * (0.5 ** 0.5)))
        density = jnp.exp(-0.5 * hidden * hidden) * 0.3989422804014327
        active[:, columns(i)] = (hidden * share).astype(BF16)
        slope[:, columns(i)] = (share + hidden * density).astype(BF16)
        return carry

    lax.fori_loop(0, 4, units, 0)
    active.send()
    slope.send()
    arrive(downs)
    down_out.send()

    def features(n, carry):
        block = down[:, :, columns(n)].reshape(WIDE, 256)
        spread_out(dot_nn(active[...], block), columns(n), own, (p1, p2, p3))
        return carry

    lax.fori_loop(0, 4, features, 0)


def feed_back_kernel(
    g0, g1, g2, g3, down, slope, up, own, p1, p2, p3, d_hidden, g_out, x_sems
):
    g_all = g_out.buffer
    arrive(join(g_all, (g0, g1, g2, g3), x_sems))
    g_out.send()
    down, slope = down.get(), slope.get()

    def units(i, carry):
        block = down[pl.ds(2 * i, 2)].reshape(256, WIDE)
        value = dot_nt(g_all[...], block) * slope[:, columns(i)].astype(F32)
        d_hidden[:, columns(i)] = value.astype(BF16)
        return carry

    lax.fori_loop(0, 4, units, 0)
    d_hidden.send()
    up = up.get()

    def features(n, carry):
        block = up[:, :, columns(n)].reshape(WIDE, 256)
        spread_out(dot_nn(d_hidden[...], block), columns(n), own, (p1, p2, p3))
        return carry

    lax.fori_loop(0, 4, features, 0)


def feed_weights_kernel(
    d_hidden, active, x_all, g_all, up_own, up_other, down_own, down_other, bias
):
    d_hidden, active, x_all, g_all = (v.get() for v in (d_hidden, active, x_all, g_all))
    for half, up, down in ((1, up_other, down_other), (0, up_own, down_own)):

        def pair(i, carry, half=half, up=up, down=down):
            where = columns(2 * half + i)
            value = dot_tn(d_hidden[:, where], x_all[...]).astype(BF16)
            up[pl.ds(2 * i, 2)] = value.reshape(2, 128, WIDE)
            value = dot_tn(active[:, where], g_all[...]).astype(BF16)
            down[pl.ds(2 * i, 2)] = value.reshape(2, 128, WIDE)
            return carry

        lax.fori_loop(0, 2, pair, 0)
        up.send()
        down.send()
    bias[...] = sums(d_hidden[...].astype(F32))


def assemble_kernel(place, x0, x1, x2, x3, out):
    for r, piece in enumerate((x0, x1, x2, x3)):
        out[place[3] ^ r] = piece[...]


def core_sum_feed_kernel(place, up, down, up_got, down_got, up_out, down_out):
    down_out[...] = (down.get()[...].astype(F32) + down_got[...].astype(F32)).astype(BF16)
    up_out[...] = (up.get()[...].astype(F32) + up_got[...].astype(F32)).astype(BF16)


def split_kernel(place, own, received, *outs):
    own = own.get()
    for r, out in enumerate(outs):
        z = place[3] ^ r
        out[...] = (own[z].astype(F32) + received[z].astype(F32)).astype(BF16)


def core_sum_kernel(*refs):
    count = len(refs) // 3
    for own, received, out in zip(refs[:count], refs[count : 2 * count], refs[2 * count :]):
        out[...] = (own.get()[...].astype(F32) + received[...].astype(F32)).astype(BF16)
        out.send()


def ordered(place):
    return [
        (4 * c + r, ((r ^ place[1]) * 2 + (c ^ place[0])).astype(jnp.int32))
        for c in range(2)
        for r in range(4)
    ]


def gathered(pieces, place, target, sems):
    copies = [
        pltpu.make_async_copy(pieces[i], target.at[to], sems.at[i]) for i, to in ordered(place)
    ]
    for copy in copies:
        copy.start()
    arrive(copies)


def finish_attn_kernel(place, *refs):
    pieces, refs = refs[:8], refs[8:]
    gq, gk, gv, go, bias_query, bias_value, bias_up, *vectors, block, sems = refs
    gathered(pieces, place, block, sems)
    for a, out in enumerate((gq, gk, gv)):
        rows = block[:, HALF * a : HALF * a + HALF].reshape(256, WIDE)
        out[0] = rows.astype(F32).T
        out.send()
    go[0] = block[:, 3 * HALF : 4 * HALF].reshape(256, WIDE).astype(F32)
    go.send()
    small = [block[i, 128:144].astype(F32) for i in range(8)]
    bias_query[...] = jnp.concatenate([v[0:1, 0:HALF] for v in small], 1)
    bias_value[...] = jnp.concatenate([v[0:1, HALF : 2 * HALF] for v in small], 1)
    for i in range(8):
        bias_up[:, 128 * i : 128 * i + 128] = small[i][0:1, 128:256]
    total = 0.5 * sum(small[1:], small[0])
    for i, out in enumerate(vectors):
        out[...] = total[i + 1 : i + 2]


def finish_up_kernel(place, *refs):
    pieces, refs = refs[:8], refs[8:]
    out, block, sems = refs
    gathered(pieces, place, block, sems)
    for i in range(8):
        out[0, :, 128 * i : 128 * i + 128] = block[i].astype(F32).T


def finish_down_kernel(place, *refs):
    pieces, refs = refs[:8], refs[8:]
    out, block, sems = refs
    gathered(pieces, place, block, sems)
    for i in range(8):
        out[0, 128 * i : 128 * i + 128] = block[i].astype(F32)


def finish_tokens_kernel(place, a, b, out):
    is_first = place[2] == 0

    @pl.when(is_first)
    def _():
        out[0, 0] = a[...].astype(out.buffer.dtype)
        out[0, 1] = b[...].astype(out.buffer.dtype)

    @pl.when(jnp.logical_not(is_first))
    def _():
        out[0, 0] = b[...].astype(out.buffer.dtype)
        out[0, 1] = a[...].astype(out.buffer.dtype)


RAW = ["a"] * 4
WHOLE = shape((SEQ, WIDE))
BLOCKS = shape((8, 128, WIDE))
HEAD_ROWS = shape((4, 4, 2, HALF, WIDE))
TOKEN = shape((SHARE, WIDE))
WIDE_TOKEN = shape((SHARE, WIDE), F32)
ONE = shape((SHARE, 1), F32)
PARTS = [("v", WIDE_TOKEN)] + [("v", TOKEN)] * 3
ROW = shape((1, WIDE))
FOUR = DMA((4,))
MASK = shape((1, SEQ), F32)
VECTORS = shape((8, WIDE), F32)

prep_attn = call(
    prep_attn_kernel,
    "pack_attention",
    ["s"]
    + [shape((1, WIDE, 256))] * 3
    + [shape((1, 256, WIDE))]
    + [shape((1, 256))] * 2
    + [ROW] * 7,
    [("h", shape((ATTN, WIDE)))] * 2,
    [scratch((3, 256, WIDE))],
)
pick = call(
    pick_kernel,
    "pick",
    ["s"] + [shape((ATTN, WIDE))] * 2,
    [("h", shape((ATTN, WIDE)))],
)
prep_feed = call(
    prep_feed_kernel,
    "pack_feed",
    ["s", "r", "r"],
    [("h", shape((2 * FEED, WIDE)))] * 2,
    [scratch((2, WIDE, 128)), DMA((4,))],
)
norm_one, norm_two = (
    call(
        partial(norm_kernel, first),
        name,
        ["v"] * 6,
        [("v", WIDE_TOKEN), ("v", TOKEN), ("h", TOKEN), ("h", ONE)],
        )
    for first, name in ((True, "norm_one"), (False, "norm_two"))
)
BACKS = [("h", WIDE_TOKEN), ("v", TOKEN), ("h", VECTORS)]
norm_two_back = call(
    norm_two_back_kernel, "norm_two_back", ["v", "v", TOKEN, ONE], BACKS
)
norm_two_back_sum = call(
    norm_two_back_sum_kernel,
    "norm_two_back_sum",
    ["v"] * 5 + [WIDE_TOKEN, TOKEN, ONE],
    BACKS + [("h", TOKEN)],
)
norm_one_back = call(
    norm_one_back_kernel,
    "norm_one_back",
    ["v"] * 5 + [WIDE_TOKEN, TOKEN, ONE],
    BACKS,
)
last_sum = call(
    last_sum_kernel, "last_sum", ["v"] * 4 + [WIDE_TOKEN], [("h", TOKEN)]
)
attn_forward = call(
    attn_kernel,
    "attention",
    RAW + ["v", "r", "a"],
    PARTS
    + [
        ("h", shape((SEQ, 768))),
        ("h", shape((HEADS, SEQ, SEQ))),
        ("h", shape((SEQ, 256))),
        ("h", WHOLE),
        ("h", HEAD_ROWS),
    ],
    [scratch((4, 16, WIDE)), DMA((9,)), FOUR],
)
attn_backward = call(
    attn_back_kernel,
    "attention_back",
    RAW + [HEAD_ROWS, shape((SEQ, 768)), shape((HEADS, SEQ, SEQ))],
    PARTS + [("h", shape((SEQ, 768))), ("h", WHOLE)],
    [FOUR],
)
attn_weights = call(
    attn_weights_kernel,
    "attention_weights",
    [shape((SEQ, 768)), shape((SEQ, 256)), WHOLE, WHOLE] + [VECTORS] * 3,
    [("h", shape((4, ATTN, WIDE)))] * 2,
)
feed_forward = call(
    feed_kernel,
    "feed",
    RAW + ["r", "r", "a", "r", "a"],
    PARTS + [("h", WHOLE)] * 3 + [("h", BLOCKS)] * 2,
    [scratch((4, 16, WIDE)), scratch((8, WIDE), F32), DMA((5,)), FOUR],
)
feed_backward = call(
    feed_back_kernel,
    "feed_back",
    RAW + [BLOCKS, WHOLE, BLOCKS],
    PARTS + [("h", WHOLE)] * 2,
    [FOUR],
)
feed_weights = call(
    feed_weights_kernel,
    "feed_weights",
    [WHOLE] * 4,
    [("h", shape((4, FEED, WIDE)))] * 4 + [("h", VECTORS)],
)
FEED_HALVES = ["s", shape((4, FEED, WIDE)), shape((4, FEED, WIDE)), "v", "v"]
core_sum_feed = call(
    core_sum_feed_kernel,
    "core_sum_feed",
    FEED_HALVES,
    [("h", shape((4, FEED, WIDE))), ("h", shape((4, FEED, WIDE)))],
)
split_attn, split_down = (
    call(
        split_kernel,
        "core_split",
        ["s", shape((4, rows, WIDE)), "v"],
        [("v", shape((rows, WIDE)))] * 4,
    )
    for rows in (ATTN, FEED)
)
core_sum_up = call(
    core_sum_kernel,
    "core_sum_up",
    [shape((4, FEED, WIDE)), "v"],
    [("h", shape((4, FEED, WIDE)))],
)
assemble = call(
    assemble_kernel,
    "assemble",
    ["s"] + ["v"] * 4,
    [("h", shape((4, FEED, WIDE)))],
)
core_sum_attn = call(
    core_sum_kernel,
    "core_sum_attention",
    [shape((4, ATTN, WIDE)), "v"],
    [("h", shape((4, ATTN, WIDE)))],
)
EIGHT = DMA((8,))
finish_attn = call(
    finish_attn_kernel,
    "finish_attention",
    ["s"] + ["a"] * 8,
    [("h", shape((1, WIDE, 256), F32))] * 3
    + [("h", shape((1, 256, WIDE), F32))]
    + [("h", shape((1, 256), F32))] * 2
    + [("h", shape((1, WIDE), F32))] * 7,
    [scratch((8, ATTN, WIDE)), EIGHT],
)
finish_up = call(
    finish_up_kernel,
    "finish_up",
    ["s"] + ["a"] * 8,
    [("h", shape((1, WIDE, WIDE), F32))],
    [scratch((8, FEED, WIDE)), EIGHT],
)
finish_down = call(
    finish_down_kernel,
    "finish_down",
    ["s"] + ["a"] * 8,
    [("h", shape((1, WIDE, WIDE), F32))],
    [scratch((8, FEED, WIDE)), EIGHT],
)
finish_tokens, finish_grads = (
    call(
        finish_tokens_kernel,
        name,
        ["s", "v", "v"],
        [("h", shape((1, 2, SHARE, WIDE), dtype))],
    )
    for name, dtype in (("finish_tokens", BF16), ("finish_grads", F32))
)


def mover(sizes, target, takes=None):
    replicas, sections, shards = sizes
    pairs = []
    for d in range(replicas):
        for s in range(sections):
            for z in range(shards):
                if takes is None or takes(d, s, z):
                    nd, ns, nz = target(d, s, z)
                    pairs.append(
                        ((d * sections + s) * shards + z, (nd * sections + ns) * shards + nz)
                    )

    def move(values):
        return lax.ppermute(values, AXES, pairs)

    return move


def solution(mesh):
    replicas, sections, shards = (mesh.shape[name] for name in AXES)
    sizes = (replicas, sections, shards)

    def block_of(d, s):
        return 2 * ((d >> 1) & 1) + s

    def quarter_of(d, s, z):
        return (block_of(d, s) + z) % 4

    swap_y = mover(sizes, lambda d, s, z: (d, s ^ 1, z))
    swap_x = mover(sizes, lambda d, s, z: (d ^ 2, s, z))
    swap_xy = mover(sizes, lambda d, s, z: (d ^ 2, s ^ 1, z))
    swap_core = mover(sizes, lambda d, s, z: (d ^ 1, s, z))
    swap_z = [mover(sizes, lambda d, s, z, r=r: (d, s, z ^ r)) for r in range(1, 4)]
    def into_place(d, s, z):
        x = (d >> 1) & 1
        micro = s ^ ((z - x) & 1)
        plane = 2 * micro + x
        block = (z - plane) % 4
        return (d & ~2) | ((block >> 1) << 1), block & 1, plane

    place_in = mover(sizes, into_place)
    place_out = [
        mover(
            sizes,
            lambda d, s, z, r=r: (
                (d & ~2) | ((z & 1) << 1),
                (z >> 1) ^ r,
                quarter_of(d, s, z),
            ),
        )
        for r in range(2)
    ]

    def gather(share):
        return (share, swap_y(share), swap_x(share), swap_xy(share))

    def scatter(parts):
        own, p1, p2, p3 = parts
        return (own, swap_y(p1), swap_x(p2), swap_xy(p3))

    def gather_direct(place, piece):
        return assemble(place, piece, *[move(piece) for move in swap_z])[0]

    def gather_mp(piece):
        return lax.all_gather(piece, "mp", axis=0)

    def scatter_mp(pieces):
        return lax.psum_scatter(pieces, "mp", scatter_dimension=0)

    def to_layers(first, second):
        is_first = (lax.axis_index("mp") >> 1) == 0
        return (
            place_out[0](jnp.where(is_first, first, second)),
            place_out[1](jnp.where(is_first, second, first)),
        )

    def per_device(
        inputs,
        cotangent,
        doc_ids,
        w_query,
        b_query,
        w_key,
        w_value,
        b_value,
        w_out,
        b_out,
        gain_one,
        shift_one,
        w_up,
        b_up,
        w_down,
        b_down,
        gain_two,
        shift_two,
    ):
        replica = lax.axis_index("dp")
        section = lax.axis_index("section")
        shard = lax.axis_index("mp")
        core = replica & 1
        block = block_of(replica, section)
        place = jnp.stack([core, block, section, shard]).astype(jnp.int32)

        attn_own, attn_peer = prep_attn(
            place,
            w_query,
            w_key,
            w_value,
            w_out,
            b_query,
            b_value,
            b_up,
            b_out,
            gain_one,
            shift_one,
            b_down,
            gain_two,
            shift_two,
        )
        attn_got = swap_y(attn_peer)
        which = section ^ ((shard - ((replica >> 1) & 1)) & 1)
        share_in = place_in(lax.dynamic_index_in_dim(inputs, which, 0, False))
        other_ids = swap_x(doc_ids)
        (attn_zero,) = pick(place, attn_own, attn_got, share_in, other_ids)
        whole_in = gather(share_in)
        feed_own, feed_peer = prep_feed(
            place, w_up, w_down, attn_zero, stamp(*whole_in[1:])
        )
        feed_got = swap_y(feed_peer)

        def of_layer(layer, own, got):
            return jnp.where(section == layer, own, got)

        attn_zero = gather_mp(attn_zero)
        attn_zero = (attn_zero, swap_core(attn_zero))
        feed_packs = [of_layer(layer, feed_own, feed_got) for layer in range(2)]
        up_zero = gather_mp(feed_packs[0][:FEED])
        down_zero = gather_direct(place, feed_packs[0][FEED:])
        attn_one = gather_mp(of_layer(1, attn_own, attn_got))
        up_one = gather_mp(feed_packs[1][:FEED])
        down_one = gather_mp(feed_packs[1][FEED:])

        mine = ((replica >> 1) & 1) == (shard & 1)
        ids = jnp.where(mine, doc_ids, other_ids)
        ids = lax.dynamic_index_in_dim(ids, shard >> 1, 0, False).reshape(4, SHARE)
        ids = jnp.concatenate(
            [
                lax.dynamic_index_in_dim(ids, ((block ^ r) + shard) % 4, 0, False)
                for r in range(4)
            ]
        )
        id_row = ids.astype(F32)[None, :]

        def attn_half(share, whole, weights, vec, *after):
            *parts, qkv, probs, mixed, whole, weights = attn_forward(*whole, id_row, *weights, *after)
            parts = scatter(parts)
            middle, low, normed, inverse = norm_one(*parts, share, vec)
            return middle, low, (whole, qkv, probs, mixed, normed, inverse, weights)

        def feed_half(middle, spread, weights, vec):
            *parts, active, slope, spread, up, down = feed_forward(*spread, *weights)
            parts = scatter(parts)
            _, result, normed, inverse = norm_two(*parts, middle, vec)
            return result, (spread, active, slope, normed, inverse, up, down)

        vec_zero = attn_zero[0][0, 128:144]
        middle, low, kept_attn_zero = attn_half(share_in, whole_in, attn_zero, vec_zero)
        spread = gather(low)
        up_zero = hold(up_zero, kept_attn_zero[4])
        down_zero = hold(down_zero, stamp(*spread[1:]))
        feed_zero = (attn_zero[0], up_zero, swap_core(up_zero), down_zero, swap_core(down_zero))
        first, kept_feed_zero = feed_half(middle, spread, feed_zero, vec_zero)

        whole = gather(first)
        attn_one = hold(attn_one, kept_feed_zero[3])
        vec_one = attn_one[0, 128:144]
        attn_one = (attn_one, swap_core(attn_one))
        middle, low, kept_attn_one = attn_half(first, whole, attn_one, vec_one)
        spread = gather(low)
        up_one = hold(up_one, kept_attn_one[4])
        down_one = hold(down_one, stamp(*spread[1:]))
        feed_one = (attn_one[0], up_one, swap_core(up_one), down_one, swap_core(down_one))
        grad_which = which ^ zero_after(kept_attn_zero[1])
        share_grad = place_in(lax.dynamic_index_in_dim(cotangent, grad_which, 0, False))
        second, kept_feed_one = feed_half(middle, spread, feed_one, vec_one)

        def feed_half_back(low, kept, *after):
            spread, active, slope, _, _, up, down = kept
            grads = gather(low)
            *parts, d_hidden, grads = feed_backward(*grads, down, slope, up, *after)
            parts = scatter(parts)
            return parts, feed_weights(d_hidden, active, spread, grads), d_hidden

        def attn_half_back(grads, kept, *after):
            _, qkv, probs, _, _, _, weights = kept
            *parts, d_rows, grads = attn_backward(*grads, weights, qkv, probs, *after)
            return parts, d_rows, grads

        def feed_sum(total, halves, start, *after):
            up, up_other, down, down_other, _ = halves
            received = [swap_core(hold(other, start)) for other in (up_other, down_other)]
            return total(place, up, down, *received, *after)

        total, low, vec_two = norm_two_back(
            share_grad, vec_one, kept_feed_one[3], kept_feed_one[4]
        )
        parts, halves, _ = feed_half_back(low, kept_feed_one)
        feed_bias = halves[4]
        outputs = to_layers(first, second)
        total, low, vec_first = norm_one_back(
            *parts, vec_one, total, kept_attn_one[4], kept_attn_one[5], halves[0], *outputs
        )
        (section_outputs,) = finish_tokens(place, *outputs)
        grads = gather(low)
        halves = feed_sum(core_sum_feed, halves, total)
        ready = stamp(*grads[1:], kept=[halves[0]])
        parts, d_rows, grads = attn_half_back(grads, kept_attn_one, ready)
        parts = scatter(parts)
        up_grad_one, down_grad_one = [scatter_mp(hold(part, ready)) for part in halves]
        own, other = attn_weights(
            d_rows, kept_attn_one[3], kept_attn_one[0], grads, vec_first, vec_two, feed_bias
        )
        total, low, vec_two, grad_one = norm_two_back_sum(
            *parts, vec_zero, total, kept_feed_zero[3], kept_feed_zero[4], own, section_outputs
        )
        (attn_grad_one,) = core_sum_attn(own, swap_core(hold(other, total)))
        parts, halves, d_hidden = feed_half_back(
            low, kept_feed_zero, attn_grad_one, up_grad_one
        )
        attn_grad_one = hold(attn_grad_one, d_hidden)
        total, low, vec_first = norm_one_back(
            *parts,
            vec_zero,
            total,
            kept_attn_zero[4],
            kept_attn_zero[5],
            halves[0],
            down_grad_one,
        )
        grads = gather(low)
        attn_grad_one = scatter_mp(attn_grad_one)
        up, up_other, down, down_other, feed_bias = halves
        (up,) = core_sum_up(up, swap_core(hold(up_other, total)))
        ready = stamp(*grads[1:], kept=[up])
        parts, d_rows, grads = attn_half_back(grads, kept_attn_zero, ready, attn_grad_one)
        up_grad_zero = scatter_mp(hold(up, ready))
        own, other = attn_weights(
            d_rows,
            kept_attn_zero[3],
            kept_attn_zero[0],
            grads,
            vec_first,
            vec_two,
            feed_bias,
        )
        attn_parts = split_attn(place, own, swap_core(other))
        down_parts = split_down(place, down, swap_core(hold(down_other, total)))
        parts = scatter(parts[:1] + [hold(part, own) for part in parts[1:]])

        def scatter_direct(parts, *after):
            moved = [move(hold(part, *after)) for move, part in zip(swap_z, parts[1:])]
            total = sum((part.astype(F32) for part in moved), parts[0].astype(F32))
            return total.astype(BF16), stamp(*moved)

        (grad_zero,) = last_sum(*parts, total)
        down_grad_zero, _ = scatter_direct(down_parts, up_grad_zero)
        attn_grad_zero, attn_there = scatter_direct(attn_parts, up_grad_zero)
        def exchange(zero, one, *after, last=False):
            if replicas > 4:
                groups = [[low + 4 * high for high in range(replicas // 4)] for low in range(4)]
                zero, one = lax.psum((zero, one), "dp", axis_index_groups=groups)
            mine = jnp.where(section == 0, zero, one)
            theirs = jnp.where(section == 0, one, zero)
            if after:
                mine, theirs = hold(mine, *after), hold(theirs, *after)
            pieces = [mine, swap_y(theirs), swap_x(mine), swap_xy(theirs)]
            own = hold(mine, stamp(pieces[1])) if last else mine
            return pieces + [swap_core(piece) for piece in [own] + pieces[1:]]

        ups = exchange(up_grad_zero, up_grad_one, grad_zero)
        (g_up,) = finish_up(place, *ups)
        downs = exchange(down_grad_zero, down_grad_one)
        (g_down,) = finish_down(place, *downs)
        attns = exchange(attn_grad_zero, attn_grad_one, last=True)
        g_query, g_key, g_value, g_out, g_b_query, g_b_value, g_b_up, *vectors = finish_attn(place, *attns)
        moved = to_layers(hold(grad_zero, attn_there), grad_one)
        (section_input_grads,) = finish_grads(place, *moved, g_query)
        return (
            section_outputs,
            section_input_grads,
            g_query,
            g_b_query,
            g_key,
            g_value,
            g_b_value,
            g_out,
            vectors[0],
            vectors[1],
            vectors[2],
            g_up,
            g_b_up,
            g_down,
            vectors[3],
            vectors[4],
            vectors[5],
        )

    vector = P("section", None)
    by_column = P("section", None, "mp")
    by_row = P("section", "mp", None)
    spread = P("section", "mp")
    tokens = P(None, ("dp", "mp"), None)
    layer_tokens = P("section", None, ("dp", "mp"), None)
    return jax.shard_map(
        per_device,
        mesh=mesh,
        in_specs=(
            tokens,
            tokens,
            P(None, "dp", None),
            by_column,
            spread,
            by_column,
            by_column,
            spread,
            by_row,
            vector,
            vector,
            vector,
            by_column,
            spread,
            by_row,
            vector,
            vector,
            vector,
        ),
        out_specs=(
            layer_tokens,
            layer_tokens,
            by_column,
            spread,
            by_column,
            by_column,
            spread,
            by_row,
            vector,
            vector,
            vector,
            by_column,
            spread,
            by_row,
            vector,
            vector,
            vector,
        ),
        check_vma=False,
    )
```

```python
from functools import partial

import jax
import jax.numpy as jnp
from jax import lax
from jax.experimental import pallas as pl
from jax.experimental.pallas import tpu as pltpu
from jax.sharding import PartitionSpec as P

HD = 64
SEQ = 512
SHARE = 128
WIDE = 1024
HEADS = 4
HALF = 32
ATTN = 144
FEED = 128
AXES = ("dp", "section", "mp")
EPSILON = 1e-05
NEGATIVE = -1e30
F32 = jnp.float32
BF16 = jnp.bfloat16
VMEM = pl.BlockSpec(memory_space=pltpu.VMEM)
ANY = pl.BlockSpec(memory_space=pl.ANY)
HBM = pl.BlockSpec(memory_space=pltpu.HBM)
SMEM = pl.BlockSpec(memory_space=pltpu.SMEM)


def dot_nt(left, right):
    return lax.dot_general(left, right, (((1,), (1,)), ((), ())), preferred_element_type=F32)


def dot_nn(left, right):
    return lax.dot_general(left, right, (((1,), (0,)), ((), ())), preferred_element_type=F32)


def dot_tn(left, right):
    return lax.dot_general(left, right, (((0,), (0,)), ((), ())), preferred_element_type=F32)


def shape(dims, dtype=BF16):
    return jax.ShapeDtypeStruct(dims, dtype)


DMA = pltpu.SemaphoreType.DMA


def scratch(dims, dtype=BF16):
    return pltpu.VMEM(dims, dtype)


def in_hbm(value):
    return pltpu.with_memory_space_constraint(value, pltpu.HBM)


class Arriving:
    def __init__(self, copies, target):
        self.copies, self.target = copies, target
        for copy in copies:
            copy.start()

    def get(self):
        for copy in self.copies:
            copy.wait()
        self.copies = []
        return self.target


class Leaving:
    def __init__(self, copies, buffer):
        self.copies, self.buffer, self.sent = copies, buffer, False

    def __setitem__(self, where, value):
        self.buffer[where] = value

    def __getitem__(self, where):
        return self.buffer[where]

    def send(self):
        for copy in self.copies:
            copy.start()
        self.sent = True


class Chunks:
    def __init__(self, rows):
        self.buffer = shape((4, rows, WIDE))
        cut = 80 if rows == ATTN else 64
        self.parts = [(z, start, end) for z in range(4) for start, end in ((0, cut), (cut, rows))]
        self.shapes = [shape((end - start, WIDE)) for _, start, end in self.parts]

    def views(self, buffer):
        return [buffer.at[z, start:end] for z, start, end in self.parts]


def call(kernel, name, ins, outs, scratches=(), limit=32):
    def arrays(item):
        return item.shapes if isinstance(item, Chunks) else [item]

    def buffer_of(item):
        held = item.buffer if isinstance(item, Chunks) else item
        return scratch(held.shape, held.dtype)

    loads = [i for i in ins if not isinstance(i, str)]
    stores = [o for where, o in outs if where == "h"]
    specs = {"v": VMEM, "s": SMEM, "r": HBM, "h": HBM, "a": ANY}
    in_specs, pinned = [], []
    for i in ins:
        count = 1 if isinstance(i, str) else len(arrays(i))
        in_specs += [specs[i] if isinstance(i, str) else HBM] * count
        pinned += [i == "r" or not isinstance(i, str)] * count
    out_specs, out_shapes = [], []
    for where, o in outs:
        for one in arrays(o):
            out_specs.append(specs[where])
            out_shapes.append(pltpu.HBM(one.shape, one.dtype) if where == "h" else one)
    n_loads = sum(len(arrays(i)) for i in loads)
    n_stores = sum(len(arrays(o)) for o in stores)

    def views(item, buffer):
        return item.views(buffer) if isinstance(item, Chunks) else [buffer]

    def body(after, *refs):
        refs = list(refs)
        in_refs = [refs.pop(0) for _ in in_specs]
        del refs[:after]
        out_refs = [refs.pop(0) for _ in out_specs]
        load_bufs = [refs.pop(0) for _ in loads]
        store_bufs = [refs.pop(0) for _ in stores]
        load_sems = refs.pop(0) if loads else None
        store_sems = refs.pop(0) if stores else None
        operands, results, n = [], [], 0
        for kind in ins:
            if isinstance(kind, str):
                operands.append(in_refs.pop(0))
                continue
            target, copies = load_bufs.pop(0), []
            for view in views(kind, target):
                copies.append(pltpu.make_async_copy(in_refs.pop(0), view, load_sems.at[n]))
                n += 1
            operands.append(Arriving(copies, target))
        n = 0
        for where, o in outs:
            if where == "v":
                results.append(out_refs.pop(0))
                continue
            buffer, copies = store_bufs.pop(0), []
            for view in views(o, buffer):
                copies.append(pltpu.make_async_copy(view, out_refs.pop(0), store_sems.at[n]))
                n += 1
            results.append(Leaving(copies, buffer))
        kernel(*operands, *results, *refs)
        for operand in operands:
            if isinstance(operand, Arriving):
                operand.get()
        leaving = [result for result in results if isinstance(result, Leaving)]
        for result in leaving:
            if not result.sent:
                result.send()
        for result in leaving:
            for copy in result.copies:
                copy.wait()

    def run(*operands):
        after = len(operands) - len(in_specs)
        operands = [
            in_hbm(operand) if pin else operand
            for pin, operand in zip(
                pinned + [o.size > 1 for o in operands[len(pinned) :]], operands
            )
        ]
        return pl.pallas_call(
            partial(body, after),
            name=name,
            in_specs=in_specs
            + [ANY if o.size > 1 else SMEM for o in operands[len(in_specs) :]],
            out_specs=tuple(out_specs),
            out_shape=tuple(out_shapes),
            scratch_shapes=[buffer_of(item) for item in loads + stores]
            + ([DMA((n_loads,))] if loads else [])
            + ([DMA((n_stores,))] if stores else [])
            + list(scratches),
            compiler_params=pltpu.CompilerParams(vmem_limit_bytes=limit << 20),
            cost_estimate=pl.CostEstimate(flops=0, bytes_accessed=0, transcendentals=0),
        )(*operands)

    return run


def hold(value, *after):
    return pl.pallas_call(
        lambda *refs: None,
        name="hold",
        in_specs=[HBM] + [ANY if o.size > 1 else SMEM for o in after],
        out_specs=HBM,
        out_shape=pltpu.HBM(value.shape, value.dtype),
        input_output_aliases={0: 0},
    )(in_hbm(value), *after)


def stamp(*values, kept=()):
    def kernel(*refs):
        refs[-1][0] = 0

    return pl.pallas_call(
        kernel,
        name="stamp",
        in_specs=[VMEM] * len(values) + [ANY] * len(kept),
        out_specs=SMEM,
        out_shape=shape((1,), jnp.int32),
        compiler_params=pltpu.CompilerParams(vmem_limit_bytes=16 << 20),
        cost_estimate=pl.CostEstimate(flops=0, bytes_accessed=0, transcendentals=0),
    )(*values, *[in_hbm(value) for value in kept])


def zero_after(after):
    def kernel(after, out):
        out[0] = 0

    return pl.pallas_call(
        kernel,
        name="zero",
        in_specs=[ANY],
        out_specs=SMEM,
        out_shape=shape((1,), jnp.int32),
    )(after)[0]


def at_rows(rows, values):
    place = lax.broadcasted_iota(jnp.int32, (rows, values[0].shape[1]), 0)
    block = jnp.zeros((rows, values[0].shape[1]), F32)
    for i, value in enumerate(values):
        block = jnp.where(place == i, value, block)
    return block


def columns(i, width=256):
    return pl.ds(pl.multiple_of(i * width, width), width)


def prep_attn_kernel(
    place, wq, wk, wv, wo, bq, bv, bu, v0, v1, v2, v3, v4, v5, own, peer, turned
):
    core, quarter = place[0], place[1]
    for a, w in enumerate((wq, wk, wv)):
        turned[a] = w.get()[0].T
    layer_rows = [v.get()[...].astype(F32) for v in (v0, v1, v2, v3, v4, v5)]
    wo, bq, bv, bu = wo.get(), bq.get(), bv.get(), bu.get()
    source = lax.broadcasted_iota(jnp.int32, (256, 128), 0)
    lane = lax.broadcasted_iota(jnp.int32, (256, 128), 1)
    for out, block in ((own, quarter), (peer, quarter ^ 1)):
        head = pl.multiple_of(block * HD + core * HALF, HALF)
        for a in range(3):
            out[HALF * a : HALF * a + HALF] = turned[a, pl.ds(head, HALF)]
        out[3 * HALF : 4 * HALF] = wo[0, pl.ds(head, HALF)]
        inner = lane & 63
        wanted = block * HD + (inner ^ (core * HALF))
        hit = source == wanted
        zero = jnp.zeros((256, 128), F32)
        one = jnp.ones((256, 128), F32)
        first = jnp.where(hit & (lane < 64), one, zero).astype(BF16)
        second = jnp.where(hit & (lane >= 64), one, zero).astype(BF16)
        bias = dot_nn(jnp.broadcast_to(bq[...], (16, 256)), first) + dot_nn(
            jnp.broadcast_to(bv[...], (16, 256)), second
        )
        rows = lax.broadcasted_iota(jnp.int32, (16, WIDE), 0)
        block_rows = jnp.zeros((16, WIDE), F32)
        for i, row in enumerate(layer_rows):
            block_rows = jnp.where(rows == i + 1, row, block_rows)
        out[128:144] = block_rows.astype(BF16)
        first_row = lax.broadcasted_iota(jnp.int32, (16, 128), 0) == 0
        out[128:144, 0:128] = jnp.where(first_row, bias, block_rows[:, 0:128]).astype(BF16)
        for h in range(2):
            unit = pl.multiple_of(block * 256 + (core ^ h) * 128, 128)
            lanes = slice(128 * (h + 1), 128 * (h + 2))
            piece = jnp.where(first_row, bu[:, pl.ds(unit, 128)].astype(F32), block_rows[:, lanes])
            out[128:144, lanes] = piece.astype(BF16)


def pick_kernel(place, own, got, out):
    own, got = own.get(), got.get()
    out[...] = jnp.where(jnp.full(own.shape, place[2]) == 0, own[...], got[...])


def prep_feed_kernel(place, up, down, own, peer, column, sems):
    core, quarter = place[0], place[1]
    copies = []
    outs = ((own, quarter), (peer, quarter ^ 1))
    for i, (out, block) in enumerate(outs):
        unit = pl.multiple_of(block * 256 + core * 128, 128)
        copies.append(
            pltpu.make_async_copy(up.at[0, :, pl.ds(unit, 128)], column.at[i], sems.at[2 * i])
        )
        copies.append(
            pltpu.make_async_copy(
                down.at[0, pl.ds(unit, 128)],
                out.buffer.at[FEED : 2 * FEED],
                sems.at[2 * i + 1],
            )
        )
    for copy in copies:
        copy.start()
    for i, (out, _) in enumerate(outs):
        copies[2 * i].wait()
        out[0:FEED] = column[i].T
        copies[2 * i + 1].wait()
        out.send()


def rows_of(ref, *which):
    block = ref[...].astype(F32)
    return [block[i : i + 1] for i in which]


def norm_forward(hidden, gain, offset):
    centre = jnp.mean(hidden, -1, keepdims=True)
    centred = hidden - centre
    variance = jnp.mean(centred * centred, -1, keepdims=True)
    inverse = lax.rsqrt(variance + EPSILON)
    normed = centred * inverse
    return (normed * gain + offset, normed, inverse)


def norm_backward(upstream, normed, inverse, gain):
    scaled = upstream * gain
    return inverse * (
        scaled
        - jnp.mean(scaled, -1, keepdims=True)
        - normed * jnp.mean(scaled * normed, -1, keepdims=True)
    )


def received(own, r1, r2, r3):
    return own[...] + r1[...].astype(F32) + r2[...].astype(F32) + r3[...].astype(F32)


def norm_kernel(first, own, r1, r2, r3, residual, vec, value, low, normed, inverse):
    bias, gain, offset = rows_of(vec, *((1, 2, 3) if first else (4, 5, 6)))
    hidden = residual[...].astype(F32) + received(own, r1, r2, r3) + bias
    result, flat, scale = norm_forward(hidden, gain, offset)
    low[...] = result.astype(BF16)
    value[...] = result
    normed[...] = flat.astype(BF16)
    inverse[...] = scale


def sums(*values):
    return at_rows(8, [jnp.sum(v, 0, keepdims=True) for v in values])


def norm_back(grad, gain, normed, inverse, total, low, vectors):
    flat = normed.get()[...].astype(F32)
    value = norm_backward(grad, flat, inverse.get()[...], gain)
    rounded = value.astype(BF16)
    low[...] = rounded
    total[...] = value
    total.send()
    vectors[...] = sums(rounded.astype(F32), grad * flat, grad)


def norm_two_both_kernel(own, r1, r2, r3, residual, upstream, vec, low, total, low_grad, vectors):
    bias, gain, offset = rows_of(vec, 4, 5, 6)
    hidden = residual[...].astype(F32) + received(own, r1, r2, r3) + bias
    result, flat, scale = norm_forward(hidden, gain, offset)
    low[...] = result.astype(BF16)
    grad = upstream[...].astype(F32)
    value = norm_backward(grad, flat, scale, gain)
    rounded = value.astype(BF16)
    low_grad[...] = rounded
    total[...] = value
    total.send()
    vectors[...] = sums(rounded.astype(F32), grad * flat, grad)


def norm_two_back_sum_kernel(
    own, r1, r2, r3, vec, before, normed, inverse, total, low, vectors, given
):
    (gain,) = rows_of(vec, 5)
    rounded = (before.get()[...] + received(own, r1, r2, r3)).astype(BF16)
    norm_back(rounded.astype(F32), gain, normed, inverse, total, low, vectors)
    given[...] = rounded


def norm_one_back_kernel(own, r1, r2, r3, vec, before, normed, inverse, total, low, vectors):
    (gain,) = rows_of(vec, 2)
    grad = before.get()[...] + received(own, r1, r2, r3)
    norm_back(grad, gain, normed, inverse, total, low, vectors)


def last_sum_kernel(own, r1, r2, r3, before, given):
    given[...] = (before.get()[...] + received(own, r1, r2, r3)).astype(BF16)


def load_attn(own, other, weight, sems):
    return [
        pltpu.make_async_copy(
            ref.at[:, HALF * a : HALF * a + HALF], weight.at[a, :, half], sems.at[4 * half + a]
        )
        for half, ref in enumerate((own, other))
        for a in range(4)
    ]


def join(target, pieces, sems):
    copies = [
        pltpu.make_async_copy(piece, target.at[SHARE * i : SHARE * i + SHARE], sems.at[i])
        for i, piece in enumerate(pieces)
    ]
    for copy in copies:
        copy.start()
    return copies


def arrive(copies):
    for copy in copies:
        copy.wait()


def spread_out(value, where, own, parts):
    own[:, where] = value[0:SHARE]
    for i, part in enumerate(parts):
        part[:, where] = value[SHARE * (i + 1) : SHARE * (i + 2)].astype(BF16)


def by_share(left, right, own, parts):
    for i in (3, 2, 1, 0):
        value = dot_nn(left[SHARE * i : SHARE * i + SHARE], right)
        if i:
            parts[i - 1][...] = value.astype(BF16)
        else:
            own[...] = value


def attn_kernel(
    x0, x1, x2, x3, id_row, a_own, a_other,
    own, p1, p2, p3, qkv, probs, mixed, x_out, weight_out,
    small, sems, x_sems,
):
    weight, x_all = weight_out.buffer, x_out.buffer
    copies = load_attn(a_own, a_other, weight, sems)
    copies.append(pltpu.make_async_copy(a_own.at[:, 128:144], small, sems.at[8]))
    for copy in copies:
        copy.start()
    arrive(join(x_all, (x0, x1, x2, x3), x_sems))
    x_out.send()
    arrive(copies)
    weight_out.send()
    ids = id_row[...]
    id_column = jnp.broadcast_to(ids, (128, SEQ)).T[:, 0:1]
    biases = [small[z].astype(F32)[0:1] for z in range(4)]
    bias_of = (
        jnp.concatenate([b[:, 0:64] for b in biases], 1),
        None,
        jnp.concatenate([b[:, 64:128] for b in biases], 1),
    )
    x = x_all[...]
    for a in range(3):
        rows = dot_nt(x, weight[a].reshape(256, WIDE))
        if bias_of[a] is not None:
            rows = rows + bias_of[a]
        qkv[:, 256 * a : 256 * a + 256] = rows.astype(BF16)
    qkv.send()
    for c in range(2):
        q_rows = slice(256 * c, 256 * c + 256)
        allowed = id_column[q_rows] == ids
        for h in range(HEADS):
            query = qkv[q_rows, HD * h : HD * h + HD]
            key = qkv[:, 256 + HD * h : 256 + HD * h + HD]
            value = qkv[:, 512 + HD * h : 512 + HD * h + HD]
            scores = jnp.where(allowed, dot_nt(query, key) * HD ** (-0.5), NEGATIVE)
            exponent = jnp.exp(scores - jnp.max(scores, -1, keepdims=True))
            low = (exponent / jnp.sum(exponent, -1, keepdims=True)).astype(BF16)
            probs[h, q_rows] = low
            mixed[q_rows, HD * h : HD * h + HD] = dot_nn(low, value).astype(BF16)
    probs.send()
    mixed.send()
    by_share(mixed, weight[3].reshape(256, WIDE), own, (p1, p2, p3))


def attn_back_kernel(
    g0, g1, g2, g3, weight, qkv, probs, own, p1, p2, p3, d_rows, g_out, x_sems
):
    g_all = g_out.buffer
    arrive(join(g_all, (g0, g1, g2, g3), x_sems))
    g_out.send()
    weight, qkv, probs = weight.get(), qkv.get(), probs.get()
    d_mixed = dot_nt(g_all[...], weight[3].reshape(256, WIDE)).astype(BF16)
    scale = HD ** (-0.5)
    for h in range(HEADS):
        query = qkv[:, HD * h : HD * h + HD]
        key = qkv[:, 256 + HD * h : 256 + HD * h + HD]
        value = qkv[:, 512 + HD * h : 512 + HD * h + HD]
        grad = d_mixed[:, HD * h : HD * h + HD]
        d_key = jnp.zeros((SEQ, HD), F32)
        d_value = jnp.zeros((SEQ, HD), F32)
        for c in range(2):
            q_rows = slice(256 * c, 256 * c + 256)
            low = probs[h, q_rows]
            p = low.astype(F32)
            d_probs = dot_nt(grad[q_rows], value)
            inner = jnp.sum(p * d_probs, -1, keepdims=True)
            d_scores = (p * (d_probs - inner)).astype(BF16)
            d_rows[q_rows, HD * h : HD * h + HD] = (dot_nn(d_scores, key) * scale).astype(BF16)
            d_key = d_key + dot_tn(d_scores, query[q_rows])
            d_value = d_value + dot_tn(low, grad[q_rows])
        d_rows[:, 256 + HD * h : 256 + HD * h + HD] = (d_key * scale).astype(BF16)
        d_rows[:, 512 + HD * h : 512 + HD * h + HD] = d_value.astype(BF16)
    d_rows.send()
    by_share(d_rows, weight[0:3].reshape(768, WIDE), own, (p1, p2, p3))


def attn_weights_kernel(
    d_rows, mixed, x_all, g_all, vec_one, vec_two, feed_bias, own, other
):
    operands = (d_rows, mixed, x_all, g_all, vec_one, vec_two, feed_bias)
    d_rows, mixed, x_all, g_all, vec_one, vec_two, feed_bias = (
        operand.get() for operand in operands
    )
    for a in range(4):
        if a < 3:
            value = dot_tn(d_rows[:, 256 * a : 256 * a + 256], x_all[...])
        else:
            value = dot_tn(mixed[...], g_all[...])
        value = value.astype(BF16).reshape(4, 2, HALF, WIDE)
        own[:, HALF * a : HALF * a + HALF] = value[:, 0]
        other[:, HALF * a : HALF * a + HALF] = value[:, 1]
    total = jnp.sum(d_rows[...].astype(F32), 0, keepdims=True)
    one, two = vec_one[...], vec_two[...]
    vectors = [one[i : i + 1] for i in range(3)] + [two[i : i + 1] for i in range(3)]
    block = at_rows(16, [jnp.zeros((1, WIDE), F32)] + vectors)
    first_row = lax.broadcasted_iota(jnp.int32, (16, 128), 0) == 0
    for half, out in ((1, other), (0, own)):
        for z in range(4):
            start = HD * z + HALF * half
            bias = jnp.concatenate(
                [
                    total[:, start : start + HALF],
                    total[:, 512 + start : 512 + start + HALF],
                    jnp.zeros((1, 64), F32),
                ],
                1,
            )
            out[z, 128:144] = block.astype(BF16)
            out[z, 128:144, 0:128] = jnp.where(first_row, bias, block[:, 0:128]).astype(BF16)
            unit = 512 * half + 128 * z
            piece = jnp.where(first_row, feed_bias[0:1, unit : unit + 128], block[:, 128:256])
            out[z, 128:144, 128:256] = piece.astype(BF16)
        out.send()


def load_feed(ups, downs, up, down, sems):
    copies = []
    for i, (refs, target) in enumerate(((ups, up), (downs, down))):
        for half in range(2):
            copies.append(
                pltpu.make_async_copy(
                    refs[half],
                    target.at[4 * half : 4 * half + 4],
                    sems.at[2 * i + half],
                )
            )
    return copies[:2], copies[2:]


def feed_kernel(
    x0, x1, x2, x3, a_own, up_own, up_other, down_own, down_other,
    own, p1, p2, p3, active, slope, x_out, up_out, down_out,
    small, bias, sems, x_sems,
):
    x_all, up, down = x_out.buffer, up_out.buffer, down_out.buffer
    ups, downs = load_feed((up_own, up_other), (down_own, down_other), up, down, sems)
    copies = [pltpu.make_async_copy(a_own.at[:, 128:144], small, sems.at[4])] + ups
    for copy in copies + downs:
        copy.start()
    arrive(join(x_all, (x0, x1, x2, x3), x_sems))
    x_out.send()
    arrive(copies)
    up_out.send()
    for half in range(2):
        for z in range(4):
            unit = 512 * half + 128 * z
            bias[0:8, unit : unit + 128] = jnp.broadcast_to(
                small[z, :, 128 * (half + 1) : 128 * (half + 2)].astype(F32)[0:1], (8, 128)
            )

    def units(i, carry):
        block = up[pl.ds(2 * i, 2)].reshape(256, WIDE)
        hidden = dot_nt(x_all[...], block) + bias[0:1, columns(i)]
        share = 0.5 * (1.0 + lax.erf(hidden * (0.5 ** 0.5)))
        density = jnp.exp(-0.5 * hidden * hidden) * 0.3989422804014327
        active[:, columns(i)] = (hidden * share).astype(BF16)
        slope[:, columns(i)] = (share + hidden * density).astype(BF16)
        return carry

    lax.fori_loop(0, 4, units, 0)
    active.send()
    slope.send()
    arrive(downs)
    down_out.send()

    def features(n, carry):
        block = down[:, :, columns(n)].reshape(WIDE, 256)
        spread_out(dot_nn(active[...], block), columns(n), own, (p1, p2, p3))
        return carry

    lax.fori_loop(0, 4, features, 0)


def feed_back_kernel(
    g0, g1, g2, g3, down, slope, up, own, p1, p2, p3, d_hidden, g_out, x_sems
):
    g_all = g_out.buffer
    arrive(join(g_all, (g0, g1, g2, g3), x_sems))
    g_out.send()
    down, slope = down.get(), slope.get()

    def units(i, carry):
        block = down[pl.ds(2 * i, 2)].reshape(256, WIDE)
        value = dot_nt(g_all[...], block) * slope[:, columns(i)].astype(F32)
        d_hidden[:, columns(i)] = value.astype(BF16)
        return carry

    lax.fori_loop(0, 4, units, 0)
    d_hidden.send()
    up = up.get()

    def features(n, carry):
        block = up[:, :, columns(n)].reshape(WIDE, 256)
        spread_out(dot_nn(d_hidden[...], block), columns(n), own, (p1, p2, p3))
        return carry

    lax.fori_loop(0, 4, features, 0)


def feed_weights_kernel(
    d_hidden, active, x_all, g_all, up_own, up_other, down_own, down_other, bias
):
    d_hidden, active, x_all, g_all = (v.get() for v in (d_hidden, active, x_all, g_all))
    for half, up, down in ((1, up_other, down_other), (0, up_own, down_own)):

        def pair(i, carry, half=half, up=up, down=down):
            where = columns(2 * half + i)
            value = dot_tn(d_hidden[:, where], x_all[...]).astype(BF16)
            up[pl.ds(2 * i, 2)] = value.reshape(2, 128, WIDE)
            value = dot_tn(active[:, where], g_all[...]).astype(BF16)
            down[pl.ds(2 * i, 2)] = value.reshape(2, 128, WIDE)
            return carry

        lax.fori_loop(0, 2, pair, 0)
        up.send()
        down.send()
    bias[...] = sums(d_hidden[...].astype(F32))


def assemble_kernel(place, x0, x1, x2, x3, out):
    for r, piece in enumerate((x0, x1, x2, x3)):
        out[place[3] ^ r] = piece[...]


def core_sum_feed_kernel(place, up, down, up_got, down_got, up_out, down_out):
    down_out[...] = (down.get()[...].astype(F32) + down_got[...].astype(F32)).astype(BF16)
    up_out[...] = (up.get()[...].astype(F32) + up_got[...].astype(F32)).astype(BF16)


def split_kernel(place, own, received, *outs):
    own = own.get()
    for r, out in enumerate(outs):
        z = place[3] ^ r
        out[...] = (own[z].astype(F32) + received[z].astype(F32)).astype(BF16)


def core_sum_kernel(*refs):
    count = len(refs) // 3
    for own, received, out in zip(refs[:count], refs[count : 2 * count], refs[2 * count :]):
        out[...] = (own.get()[...].astype(F32) + received[...].astype(F32)).astype(BF16)
        out.send()


def ordered(place):
    return [
        (4 * c + r, ((r ^ place[1]) * 2 + (c ^ place[0])).astype(jnp.int32))
        for c in range(2)
        for r in range(4)
    ]


def gathered(pieces, place, target, sems):
    copies = [
        pltpu.make_async_copy(pieces[i], target.at[to], sems.at[i]) for i, to in ordered(place)
    ]
    for copy in copies:
        copy.start()
    arrive(copies)


def finish_attn_kernel(place, *refs):
    pieces, refs = refs[:8], refs[8:]
    gq, gk, gv, go, bias_query, bias_value, bias_up, *vectors, block, sems = refs
    gathered(pieces, place, block, sems)
    for a, out in enumerate((gq, gk, gv)):
        rows = block[:, HALF * a : HALF * a + HALF].reshape(256, WIDE)
        out[0] = rows.astype(F32).T
        out.send()
    go[0] = block[:, 3 * HALF : 4 * HALF].reshape(256, WIDE).astype(F32)
    go.send()
    small = [block[i, 128:144].astype(F32) for i in range(8)]
    bias_query[...] = jnp.concatenate([v[0:1, 0:HALF] for v in small], 1)
    bias_value[...] = jnp.concatenate([v[0:1, HALF : 2 * HALF] for v in small], 1)
    for i in range(8):
        bias_up[:, 128 * i : 128 * i + 128] = small[i][0:1, 128:256]
    total = 0.5 * sum(small[1:], small[0])
    for i, out in enumerate(vectors):
        out[...] = total[i + 1 : i + 2]


def finish_up_kernel(place, *refs):
    pieces, refs = refs[:8], refs[8:]
    out, block, sems = refs
    gathered(pieces, place, block, sems)
    for i in range(8):
        out[0, :, 128 * i : 128 * i + 128] = block[i].astype(F32).T


def finish_down_kernel(place, *refs):
    pieces, refs = refs[:8], refs[8:]
    out, block, sems = refs
    gathered(pieces, place, block, sems)
    for i in range(8):
        out[0, 128 * i : 128 * i + 128] = block[i].astype(F32)


def finish_tokens_kernel(place, a, b, out):
    is_first = place[2] == 0

    @pl.when(is_first)
    def _():
        out[0, 0] = a[...].astype(out.buffer.dtype)
        out[0, 1] = b[...].astype(out.buffer.dtype)

    @pl.when(jnp.logical_not(is_first))
    def _():
        out[0, 0] = b[...].astype(out.buffer.dtype)
        out[0, 1] = a[...].astype(out.buffer.dtype)


RAW = ["a"] * 4
WHOLE = shape((SEQ, WIDE))
BLOCKS = shape((8, 128, WIDE))
HEAD_ROWS = shape((4, 4, 2, HALF, WIDE))
TOKEN = shape((SHARE, WIDE))
WIDE_TOKEN = shape((SHARE, WIDE), F32)
ONE = shape((SHARE, 1), F32)
PARTS = [("v", WIDE_TOKEN)] + [("v", TOKEN)] * 3
ROW = shape((1, WIDE))
FOUR = DMA((4,))
MASK = shape((1, SEQ), F32)
VECTORS = shape((8, WIDE), F32)

prep_attn = call(
    prep_attn_kernel,
    "pack_attention",
    ["s"]
    + [shape((1, WIDE, 256))] * 3
    + [shape((1, 256, WIDE))]
    + [shape((1, 256))] * 2
    + [ROW] * 7,
    [("h", shape((ATTN, WIDE)))] * 2,
    [scratch((3, 256, WIDE))],
)
pick = call(
    pick_kernel,
    "pick",
    ["s"] + [shape((ATTN, WIDE))] * 2,
    [("h", shape((ATTN, WIDE)))],
)
prep_feed = call(
    prep_feed_kernel,
    "pack_feed",
    ["s", "r", "r"],
    [("h", shape((2 * FEED, WIDE)))] * 2,
    [scratch((2, WIDE, 128)), DMA((4,))],
)
norm_one, norm_two = (
    call(
        partial(norm_kernel, first),
        name,
        ["v"] * 6,
        [("v", WIDE_TOKEN), ("v", TOKEN), ("h", TOKEN), ("h", ONE)],
        )
    for first, name in ((True, "norm_one"), (False, "norm_two"))
)
BACKS = [("h", WIDE_TOKEN), ("v", TOKEN), ("h", VECTORS)]
norm_two_both = call(
    norm_two_both_kernel, "norm_two_both", ["v"] * 7, [("v", TOKEN)] + BACKS
)
norm_two_back_sum = call(
    norm_two_back_sum_kernel,
    "norm_two_back_sum",
    ["v"] * 5 + [WIDE_TOKEN, TOKEN, ONE],
    BACKS + [("h", TOKEN)],
)
norm_one_back = call(
    norm_one_back_kernel,
    "norm_one_back",
    ["v"] * 5 + [WIDE_TOKEN, TOKEN, ONE],
    BACKS,
)
last_sum = call(
    last_sum_kernel, "last_sum", ["v"] * 4 + [WIDE_TOKEN], [("h", TOKEN)]
)
attn_forward = call(
    attn_kernel,
    "attention",
    RAW + ["v", "r", "a"],
    PARTS
    + [
        ("h", shape((SEQ, 768))),
        ("h", shape((HEADS, SEQ, SEQ))),
        ("h", shape((SEQ, 256))),
        ("h", WHOLE),
        ("h", HEAD_ROWS),
    ],
    [scratch((4, 16, WIDE)), DMA((9,)), FOUR],
)
attn_backward = call(
    attn_back_kernel,
    "attention_back",
    RAW + [HEAD_ROWS, shape((SEQ, 768)), shape((HEADS, SEQ, SEQ))],
    PARTS + [("h", shape((SEQ, 768))), ("h", WHOLE)],
    [FOUR],
)
attn_weights = call(
    attn_weights_kernel,
    "attention_weights",
    [shape((SEQ, 768)), shape((SEQ, 256)), WHOLE, WHOLE] + [VECTORS] * 3,
    [("h", shape((4, ATTN, WIDE)))] * 2,
)
feed_forward = call(
    feed_kernel,
    "feed",
    RAW + ["r", "r", "a", "r", "a"],
    PARTS + [("h", WHOLE)] * 3 + [("h", BLOCKS)] * 2,
    [scratch((4, 16, WIDE)), scratch((8, WIDE), F32), DMA((5,)), FOUR],
)
feed_backward = call(
    feed_back_kernel,
    "feed_back",
    RAW + [BLOCKS, WHOLE, BLOCKS],
    PARTS + [("h", WHOLE)] * 2,
    [FOUR],
)
feed_weights = call(
    feed_weights_kernel,
    "feed_weights",
    [WHOLE] * 4,
    [("h", shape((4, FEED, WIDE)))] * 4 + [("h", VECTORS)],
)
FEED_HALVES = ["s", shape((4, FEED, WIDE)), shape((4, FEED, WIDE)), "v", "v"]
core_sum_feed = call(
    core_sum_feed_kernel,
    "core_sum_feed",
    FEED_HALVES,
    [("h", shape((4, FEED, WIDE))), ("h", shape((4, FEED, WIDE)))],
)
split_attn, split_down = (
    call(
        split_kernel,
        "core_split",
        ["s", shape((4, rows, WIDE)), "v"],
        [("v", shape((rows, WIDE)))] * 4,
    )
    for rows in (ATTN, FEED)
)
core_sum_up = call(
    core_sum_kernel,
    "core_sum_up",
    [shape((4, FEED, WIDE)), "v"],
    [("h", shape((4, FEED, WIDE)))],
)
assemble = call(
    assemble_kernel,
    "assemble",
    ["s"] + ["v"] * 4,
    [("h", shape((4, FEED, WIDE)))],
)
core_sum_attn = call(
    core_sum_kernel,
    "core_sum_attention",
    [shape((4, ATTN, WIDE)), "v"],
    [("h", shape((4, ATTN, WIDE)))],
)
EIGHT = DMA((8,))
finish_attn = call(
    finish_attn_kernel,
    "finish_attention",
    ["s"] + ["a"] * 8,
    [("h", shape((1, WIDE, 256), F32))] * 3
    + [("h", shape((1, 256, WIDE), F32))]
    + [("h", shape((1, 256), F32))] * 2
    + [("h", shape((1, WIDE), F32))] * 7,
    [scratch((8, ATTN, WIDE)), EIGHT],
)
finish_up = call(
    finish_up_kernel,
    "finish_up",
    ["s"] + ["a"] * 8,
    [("h", shape((1, WIDE, WIDE), F32))],
    [scratch((8, FEED, WIDE)), EIGHT],
)
finish_down = call(
    finish_down_kernel,
    "finish_down",
    ["s"] + ["a"] * 8,
    [("h", shape((1, WIDE, WIDE), F32))],
    [scratch((8, FEED, WIDE)), EIGHT],
)
finish_tokens, finish_grads = (
    call(
        finish_tokens_kernel,
        name,
        ["s", "v", "v"],
        [("h", shape((1, 2, SHARE, WIDE), dtype))],
    )
    for name, dtype in (("finish_tokens", BF16), ("finish_grads", F32))
)


def mover(sizes, target, takes=None):
    replicas, sections, shards = sizes
    pairs = []
    for d in range(replicas):
        for s in range(sections):
            for z in range(shards):
                if takes is None or takes(d, s, z):
                    nd, ns, nz = target(d, s, z)
                    pairs.append(
                        ((d * sections + s) * shards + z, (nd * sections + ns) * shards + nz)
                    )

    def move(values):
        return lax.ppermute(values, AXES, pairs)

    return move


def solution(mesh):
    replicas, sections, shards = (mesh.shape[name] for name in AXES)
    sizes = (replicas, sections, shards)

    def block_of(d, s):
        return 2 * ((d >> 1) & 1) + s

    def quarter_of(d, s, z):
        return (block_of(d, s) + z) % 4

    swap_y = mover(sizes, lambda d, s, z: (d, s ^ 1, z))
    swap_x = mover(sizes, lambda d, s, z: (d ^ 2, s, z))
    swap_xy = mover(sizes, lambda d, s, z: (d ^ 2, s ^ 1, z))
    swap_core = mover(sizes, lambda d, s, z: (d ^ 1, s, z))
    swap_z = [mover(sizes, lambda d, s, z, r=r: (d, s, z ^ r)) for r in range(1, 4)]
    def into_place(d, s, z):
        x = (d >> 1) & 1
        micro = s ^ ((z - x) & 1)
        plane = 2 * micro + x
        block = (z - plane) % 4
        return (d & ~2) | ((block >> 1) << 1), block & 1, plane

    place_in = mover(sizes, into_place)
    place_out = [
        mover(
            sizes,
            lambda d, s, z, r=r: (
                (d & ~2) | ((z & 1) << 1),
                (z >> 1) ^ r,
                quarter_of(d, s, z),
            ),
        )
        for r in range(2)
    ]

    def gather(share):
        return (share, swap_y(share), swap_x(share), swap_xy(share))

    def scatter(parts):
        own, p1, p2, p3 = parts
        return (own, swap_y(p1), swap_x(p2), swap_xy(p3))

    def gather_direct(place, piece):
        return assemble(place, piece, *[move(piece) for move in swap_z])[0]

    def gather_mp(piece):
        return lax.all_gather(piece, "mp", axis=0)

    def scatter_mp(pieces):
        return lax.psum_scatter(pieces, "mp", scatter_dimension=0)

    def to_layers(first, second):
        is_first = (lax.axis_index("mp") >> 1) == 0
        return (
            place_out[0](jnp.where(is_first, first, second)),
            place_out[1](jnp.where(is_first, second, first)),
        )

    def per_device(
        inputs,
        cotangent,
        doc_ids,
        w_query,
        b_query,
        w_key,
        w_value,
        b_value,
        w_out,
        b_out,
        gain_one,
        shift_one,
        w_up,
        b_up,
        w_down,
        b_down,
        gain_two,
        shift_two,
    ):
        replica = lax.axis_index("dp")
        section = lax.axis_index("section")
        shard = lax.axis_index("mp")
        core = replica & 1
        block = block_of(replica, section)
        place = jnp.stack([core, block, section, shard]).astype(jnp.int32)

        attn_own, attn_peer = prep_attn(
            place,
            w_query,
            w_key,
            w_value,
            w_out,
            b_query,
            b_value,
            b_up,
            b_out,
            gain_one,
            shift_one,
            b_down,
            gain_two,
            shift_two,
        )
        attn_got = swap_y(attn_peer)
        which = section ^ ((shard - ((replica >> 1) & 1)) & 1)
        share_in = place_in(lax.dynamic_index_in_dim(inputs, which, 0, False))
        other_ids = swap_x(doc_ids)
        (attn_zero,) = pick(place, attn_own, attn_got, share_in, other_ids)
        whole_in = gather(share_in)
        feed_own, feed_peer = prep_feed(
            place, w_up, w_down, attn_zero, stamp(*whole_in[1:])
        )
        feed_got = swap_y(feed_peer)

        def of_layer(layer, own, got):
            return jnp.where(section == layer, own, got)

        attn_zero = gather_mp(attn_zero)
        attn_zero = (attn_zero, swap_core(attn_zero))
        feed_packs = [of_layer(layer, feed_own, feed_got) for layer in range(2)]
        up_zero = gather_mp(feed_packs[0][:FEED])
        down_zero = gather_direct(place, feed_packs[0][FEED:])
        attn_one = gather_mp(of_layer(1, attn_own, attn_got))
        up_one = gather_mp(feed_packs[1][:FEED])
        down_one = gather_mp(feed_packs[1][FEED:])

        mine = ((replica >> 1) & 1) == (shard & 1)
        ids = jnp.where(mine, doc_ids, other_ids)
        ids = lax.dynamic_index_in_dim(ids, shard >> 1, 0, False).reshape(4, SHARE)
        ids = jnp.concatenate(
            [
                lax.dynamic_index_in_dim(ids, ((block ^ r) + shard) % 4, 0, False)
                for r in range(4)
            ]
        )
        id_row = ids.astype(F32)[None, :]

        def attn_half(share, whole, weights, vec, *after):
            *parts, qkv, probs, mixed, whole, weights = attn_forward(*whole, id_row, *weights, *after)
            parts = scatter(parts)
            middle, low, normed, inverse = norm_one(*parts, share, vec)
            return middle, low, (whole, qkv, probs, mixed, normed, inverse, weights)

        def feed_half(middle, spread, weights, vec, *after):
            *parts, active, slope, spread, up, down = feed_forward(*spread, *weights, *after)
            return scatter(parts), (spread, active, slope, up, down)

        vec_zero = attn_zero[0][0, 128:144]
        middle, low, kept_attn_zero = attn_half(share_in, whole_in, attn_zero, vec_zero)
        spread = gather(low)
        up_zero = hold(up_zero, kept_attn_zero[4])
        down_zero = hold(down_zero, stamp(*spread[1:]))
        feed_zero = (attn_zero[0], up_zero, swap_core(up_zero), down_zero, swap_core(down_zero))
        parts, kept_feed_zero = feed_half(middle, spread, feed_zero, vec_zero)
        _, first, *kept_norm_zero = norm_two(*parts, middle, vec_zero)

        whole = gather(first)
        attn_one = hold(attn_one, kept_norm_zero[0])
        vec_one = attn_one[0, 128:144]
        attn_one = (attn_one, swap_core(attn_one))
        middle, low, kept_attn_one = attn_half(first, whole, attn_one, vec_one)
        spread = gather(low)
        up_one = hold(up_one, kept_attn_one[4])
        down_one = hold(down_one, stamp(*spread[1:]))
        feed_one = (attn_one[0], up_one, swap_core(up_one), down_one, swap_core(down_one))
        grad_which = which ^ zero_after(kept_attn_zero[1])
        share_grad = place_in(lax.dynamic_index_in_dim(cotangent, grad_which, 0, False))
        parts, kept_feed_one = feed_half(middle, spread, feed_one, vec_one)
        second, total, low, vec_two = norm_two_both(*parts, middle, share_grad, vec_one)

        def feed_half_back(low, kept, *after):
            spread, active, slope, up, down = kept
            grads = gather(low)
            *parts, d_hidden, grads = feed_backward(*grads, down, slope, up, *after)
            parts = scatter(parts)
            return parts, feed_weights(d_hidden, active, spread, grads), d_hidden

        def attn_half_back(grads, kept, *after):
            _, qkv, probs, _, _, _, weights = kept
            *parts, d_rows, grads = attn_backward(*grads, weights, qkv, probs, *after)
            return parts, d_rows, grads

        def feed_sum(total, halves, start, *after):
            up, up_other, down, down_other, _ = halves
            received = [swap_core(hold(other, start)) for other in (up_other, down_other)]
            return total(place, up, down, *received, *after)

        parts, halves, _ = feed_half_back(low, kept_feed_one)
        feed_bias = halves[4]
        outputs = to_layers(first, second)
        total, low, vec_first = norm_one_back(
            *parts, vec_one, total, kept_attn_one[4], kept_attn_one[5], halves[0], *outputs
        )
        (section_outputs,) = finish_tokens(place, *outputs)
        grads = gather(low)
        halves = feed_sum(core_sum_feed, halves, total)
        ready = stamp(*grads[1:], kept=[halves[0]])
        parts, d_rows, grads = attn_half_back(grads, kept_attn_one, ready)
        parts = scatter(parts)
        up_grad_one, down_grad_one = [scatter_mp(hold(part, ready)) for part in halves]
        own, other = attn_weights(
            d_rows, kept_attn_one[3], kept_attn_one[0], grads, vec_first, vec_two, feed_bias
        )
        total, low, vec_two, grad_one = norm_two_back_sum(
            *parts, vec_zero, total, *kept_norm_zero, own, section_outputs
        )
        (attn_grad_one,) = core_sum_attn(own, swap_core(hold(other, total)))
        parts, halves, d_hidden = feed_half_back(
            low, kept_feed_zero, attn_grad_one, up_grad_one
        )
        attn_grad_one = hold(attn_grad_one, d_hidden)
        total, low, vec_first = norm_one_back(
            *parts,
            vec_zero,
            total,
            kept_attn_zero[4],
            kept_attn_zero[5],
            halves[0],
            down_grad_one,
        )
        grads = gather(low)
        attn_grad_one = scatter_mp(attn_grad_one)
        up, up_other, down, down_other, feed_bias = halves
        (up,) = core_sum_up(up, swap_core(hold(up_other, total)))
        ready = stamp(*grads[1:], kept=[up])
        parts, d_rows, grads = attn_half_back(grads, kept_attn_zero, ready, attn_grad_one)
        up_grad_zero = scatter_mp(hold(up, ready))
        own, other = attn_weights(
            d_rows,
            kept_attn_zero[3],
            kept_attn_zero[0],
            grads,
            vec_first,
            vec_two,
            feed_bias,
        )
        attn_parts = split_attn(place, own, swap_core(other))
        down_parts = split_down(place, down, swap_core(hold(down_other, total)))
        parts = scatter(parts[:1] + [hold(part, own) for part in parts[1:]])

        def scatter_direct(parts, *after):
            moved = [move(hold(part, *after)) for move, part in zip(swap_z, parts[1:])]
            total = sum((part.astype(F32) for part in moved), parts[0].astype(F32))
            return total.astype(BF16), stamp(*moved)

        (grad_zero,) = last_sum(*parts, total)
        down_grad_zero, _ = scatter_direct(down_parts, up_grad_zero)
        attn_grad_zero, attn_there = scatter_direct(attn_parts, up_grad_zero)
        def exchange(zero, one, *after, last=False):
            if replicas > 4:
                groups = [[low + 4 * high for high in range(replicas // 4)] for low in range(4)]
                zero, one = lax.psum((zero, one), "dp", axis_index_groups=groups)
            mine = jnp.where(section == 0, zero, one)
            theirs = jnp.where(section == 0, one, zero)
            if after:
                mine, theirs = hold(mine, *after), hold(theirs, *after)
            pieces = [mine, swap_y(theirs), swap_x(mine), swap_xy(theirs)]
            own = hold(mine, stamp(pieces[1])) if last else mine
            return pieces + [swap_core(piece) for piece in [own] + pieces[1:]]

        ups = exchange(up_grad_zero, up_grad_one, grad_zero)
        (g_up,) = finish_up(place, *ups)
        downs = exchange(down_grad_zero, down_grad_one)
        (g_down,) = finish_down(place, *downs)
        attns = exchange(attn_grad_zero, attn_grad_one, last=True)
        g_query, g_key, g_value, g_out, g_b_query, g_b_value, g_b_up, *vectors = finish_attn(place, *attns)
        moved = to_layers(hold(grad_zero, attn_there), grad_one)
        (section_input_grads,) = finish_grads(place, *moved, g_query)
        return (
            section_outputs,
            section_input_grads,
            g_query,
            g_b_query,
            g_key,
            g_value,
            g_b_value,
            g_out,
            vectors[0],
            vectors[1],
            vectors[2],
            g_up,
            g_b_up,
            g_down,
            vectors[3],
            vectors[4],
            vectors[5],
        )

    vector = P("section", None)
    by_column = P("section", None, "mp")
    by_row = P("section", "mp", None)
    spread = P("section", "mp")
    tokens = P(None, ("dp", "mp"), None)
    layer_tokens = P("section", None, ("dp", "mp"), None)
    return jax.shard_map(
        per_device,
        mesh=mesh,
        in_specs=(
            tokens,
            tokens,
            P(None, "dp", None),
            by_column,
            spread,
            by_column,
            by_column,
            spread,
            by_row,
            vector,
            vector,
            vector,
            by_column,
            spread,
            by_row,
            vector,
            vector,
            vector,
        ),
        out_specs=(
            layer_tokens,
            layer_tokens,
            by_column,
            spread,
            by_column,
            by_column,
            spread,
            by_row,
            vector,
            vector,
            vector,
            by_column,
            spread,
            by_row,
            vector,
            vector,
            vector,
        ),
        check_vma=False,
    )
```

```python
from functools import partial

import jax
import jax.numpy as jnp
from jax import lax
from jax.experimental import pallas as pl
from jax.experimental.pallas import tpu as pltpu
from jax.sharding import PartitionSpec as P

HD = 64
SEQ = 512
SHARE = 128
WIDE = 1024
HEADS = 4
HALF = 32
ATTN = 144
FEED = 128
AXES = ("dp", "section", "mp")
EPSILON = 1e-05
NEGATIVE = -1e30
F32 = jnp.float32
BF16 = jnp.bfloat16
VMEM = pl.BlockSpec(memory_space=pltpu.VMEM)
ANY = pl.BlockSpec(memory_space=pl.ANY)
HBM = pl.BlockSpec(memory_space=pltpu.HBM)
SMEM = pl.BlockSpec(memory_space=pltpu.SMEM)


def dot_nt(left, right):
    return lax.dot_general(left, right, (((1,), (1,)), ((), ())), preferred_element_type=F32)


def dot_nn(left, right):
    return lax.dot_general(left, right, (((1,), (0,)), ((), ())), preferred_element_type=F32)


def dot_tn(left, right):
    return lax.dot_general(left, right, (((0,), (0,)), ((), ())), preferred_element_type=F32)


def shape(dims, dtype=BF16):
    return jax.ShapeDtypeStruct(dims, dtype)


DMA = pltpu.SemaphoreType.DMA


def scratch(dims, dtype=BF16):
    return pltpu.VMEM(dims, dtype)


def in_hbm(value):
    return pltpu.with_memory_space_constraint(value, pltpu.HBM)


class Arriving:
    def __init__(self, copies, target):
        self.copies, self.target = copies, target
        for copy in copies:
            copy.start()

    def get(self):
        for copy in self.copies:
            copy.wait()
        self.copies = []
        return self.target


class Leaving:
    def __init__(self, copies, buffer):
        self.copies, self.buffer, self.sent = copies, buffer, False

    def __setitem__(self, where, value):
        self.buffer[where] = value

    def __getitem__(self, where):
        return self.buffer[where]

    def send(self):
        for copy in self.copies:
            copy.start()
        self.sent = True


class Chunks:
    def __init__(self, rows):
        self.buffer = shape((4, rows, WIDE))
        cut = 80 if rows == ATTN else 64
        self.parts = [(z, start, end) for z in range(4) for start, end in ((0, cut), (cut, rows))]
        self.shapes = [shape((end - start, WIDE)) for _, start, end in self.parts]

    def views(self, buffer):
        return [buffer.at[z, start:end] for z, start, end in self.parts]


def call(kernel, name, ins, outs, scratches=(), limit=32):
    def arrays(item):
        return item.shapes if isinstance(item, Chunks) else [item]

    def buffer_of(item):
        held = item.buffer if isinstance(item, Chunks) else item
        return scratch(held.shape, held.dtype)

    loads = [i for i in ins if not isinstance(i, str)]
    stores = [o for where, o in outs if where == "h"]
    specs = {"v": VMEM, "s": SMEM, "r": HBM, "h": HBM, "a": ANY}
    in_specs, pinned = [], []
    for i in ins:
        count = 1 if isinstance(i, str) else len(arrays(i))
        in_specs += [specs[i] if isinstance(i, str) else HBM] * count
        pinned += [i == "r" or not isinstance(i, str)] * count
    out_specs, out_shapes = [], []
    for where, o in outs:
        for one in arrays(o):
            out_specs.append(specs[where])
            out_shapes.append(pltpu.HBM(one.shape, one.dtype) if where == "h" else one)
    n_loads = sum(len(arrays(i)) for i in loads)
    n_stores = sum(len(arrays(o)) for o in stores)

    def views(item, buffer):
        return item.views(buffer) if isinstance(item, Chunks) else [buffer]

    def body(after, *refs):
        refs = list(refs)
        in_refs = [refs.pop(0) for _ in in_specs]
        del refs[:after]
        out_refs = [refs.pop(0) for _ in out_specs]
        load_bufs = [refs.pop(0) for _ in loads]
        store_bufs = [refs.pop(0) for _ in stores]
        load_sems = refs.pop(0) if loads else None
        store_sems = refs.pop(0) if stores else None
        operands, results, n = [], [], 0
        for kind in ins:
            if isinstance(kind, str):
                operands.append(in_refs.pop(0))
                continue
            target, copies = load_bufs.pop(0), []
            for view in views(kind, target):
                copies.append(pltpu.make_async_copy(in_refs.pop(0), view, load_sems.at[n]))
                n += 1
            operands.append(Arriving(copies, target))
        n = 0
        for where, o in outs:
            if where == "v":
                results.append(out_refs.pop(0))
                continue
            buffer, copies = store_bufs.pop(0), []
            for view in views(o, buffer):
                copies.append(pltpu.make_async_copy(view, out_refs.pop(0), store_sems.at[n]))
                n += 1
            results.append(Leaving(copies, buffer))
        kernel(*operands, *results, *refs)
        for operand in operands:
            if isinstance(operand, Arriving):
                operand.get()
        leaving = [result for result in results if isinstance(result, Leaving)]
        for result in leaving:
            if not result.sent:
                result.send()
        for result in leaving:
            for copy in result.copies:
                copy.wait()

    def run(*operands):
        after = len(operands) - len(in_specs)
        operands = [
            in_hbm(operand) if pin else operand
            for pin, operand in zip(
                pinned + [o.size > 1 for o in operands[len(pinned) :]], operands
            )
        ]
        return pl.pallas_call(
            partial(body, after),
            name=name,
            in_specs=in_specs
            + [ANY if o.size > 1 else SMEM for o in operands[len(in_specs) :]],
            out_specs=tuple(out_specs),
            out_shape=tuple(out_shapes),
            scratch_shapes=[buffer_of(item) for item in loads + stores]
            + ([DMA((n_loads,))] if loads else [])
            + ([DMA((n_stores,))] if stores else [])
            + list(scratches),
            compiler_params=pltpu.CompilerParams(vmem_limit_bytes=limit << 20),
            cost_estimate=pl.CostEstimate(flops=0, bytes_accessed=0, transcendentals=0),
        )(*operands)

    return run


def hold(value, *after):
    return pl.pallas_call(
        lambda *refs: None,
        name="hold",
        in_specs=[HBM] + [ANY if o.size > 1 else SMEM for o in after],
        out_specs=HBM,
        out_shape=pltpu.HBM(value.shape, value.dtype),
        input_output_aliases={0: 0},
    )(in_hbm(value), *after)


def stamp(*values, kept=()):
    def kernel(*refs):
        refs[-1][0] = 0

    return pl.pallas_call(
        kernel,
        name="stamp",
        in_specs=[VMEM] * len(values) + [ANY] * len(kept),
        out_specs=SMEM,
        out_shape=shape((1,), jnp.int32),
        compiler_params=pltpu.CompilerParams(vmem_limit_bytes=16 << 20),
        cost_estimate=pl.CostEstimate(flops=0, bytes_accessed=0, transcendentals=0),
    )(*values, *[in_hbm(value) for value in kept])


def zero_after(after):
    def kernel(after, out):
        out[0] = 0

    return pl.pallas_call(
        kernel,
        name="zero",
        in_specs=[ANY],
        out_specs=SMEM,
        out_shape=shape((1,), jnp.int32),
    )(after)[0]


def at_rows(rows, values):
    place = lax.broadcasted_iota(jnp.int32, (rows, values[0].shape[1]), 0)
    block = jnp.zeros((rows, values[0].shape[1]), F32)
    for i, value in enumerate(values):
        block = jnp.where(place == i, value, block)
    return block


def columns(i, width=256):
    return pl.ds(pl.multiple_of(i * width, width), width)


def prep_attn_kernel(
    place, wq, wk, wv, wo, bq, bv, bu, v0, v1, v2, v3, v4, v5, own, peer, turned
):
    core, quarter = place[0], place[1]
    for a, w in enumerate((wq, wk, wv)):
        turned[a] = w.get()[0].T
    layer_rows = [v.get()[...].astype(F32) for v in (v0, v1, v2, v3, v4, v5)]
    wo, bq, bv, bu = wo.get(), bq.get(), bv.get(), bu.get()
    source = lax.broadcasted_iota(jnp.int32, (256, 128), 0)
    lane = lax.broadcasted_iota(jnp.int32, (256, 128), 1)
    for out, block in ((own, quarter), (peer, quarter ^ 1)):
        head = pl.multiple_of(block * HD + core * HALF, HALF)
        for a in range(3):
            out[HALF * a : HALF * a + HALF] = turned[a, pl.ds(head, HALF)]
        out[3 * HALF : 4 * HALF] = wo[0, pl.ds(head, HALF)]
        inner = lane & 63
        wanted = block * HD + (inner ^ (core * HALF))
        hit = source == wanted
        zero = jnp.zeros((256, 128), F32)
        one = jnp.ones((256, 128), F32)
        first = jnp.where(hit & (lane < 64), one, zero).astype(BF16)
        second = jnp.where(hit & (lane >= 64), one, zero).astype(BF16)
        bias = dot_nn(jnp.broadcast_to(bq[...], (16, 256)), first) + dot_nn(
            jnp.broadcast_to(bv[...], (16, 256)), second
        )
        rows = lax.broadcasted_iota(jnp.int32, (16, WIDE), 0)
        block_rows = jnp.zeros((16, WIDE), F32)
        for i, row in enumerate(layer_rows):
            block_rows = jnp.where(rows == i + 1, row, block_rows)
        out[128:144] = block_rows.astype(BF16)
        first_row = lax.broadcasted_iota(jnp.int32, (16, 128), 0) == 0
        out[128:144, 0:128] = jnp.where(first_row, bias, block_rows[:, 0:128]).astype(BF16)
        for h in range(2):
            unit = pl.multiple_of(block * 256 + (core ^ h) * 128, 128)
            lanes = slice(128 * (h + 1), 128 * (h + 2))
            piece = jnp.where(first_row, bu[:, pl.ds(unit, 128)].astype(F32), block_rows[:, lanes])
            out[128:144, lanes] = piece.astype(BF16)


def pick_kernel(place, own, got, out):
    own, got = own.get(), got.get()
    out[...] = jnp.where(jnp.full(own.shape, place[2]) == 0, own[...], got[...])


def prep_feed_kernel(place, up, down, own, peer, column, sems):
    core, quarter = place[0], place[1]
    copies = []
    outs = ((own, quarter), (peer, quarter ^ 1))
    for i, (out, block) in enumerate(outs):
        unit = pl.multiple_of(block * 256 + core * 128, 128)
        copies.append(
            pltpu.make_async_copy(up.at[0, :, pl.ds(unit, 128)], column.at[i], sems.at[2 * i])
        )
        copies.append(
            pltpu.make_async_copy(
                down.at[0, pl.ds(unit, 128)],
                out.buffer.at[FEED : 2 * FEED],
                sems.at[2 * i + 1],
            )
        )
    for copy in copies:
        copy.start()
    for i, (out, _) in enumerate(outs):
        copies[2 * i].wait()
        out[0:FEED] = column[i].T
        copies[2 * i + 1].wait()
        out.send()


def rows_of(ref, *which):
    block = ref[...].astype(F32)
    return [block[i : i + 1] for i in which]


def norm_forward(hidden, gain, offset):
    centre = jnp.mean(hidden, -1, keepdims=True)
    centred = hidden - centre
    variance = jnp.mean(centred * centred, -1, keepdims=True)
    inverse = lax.rsqrt(variance + EPSILON)
    normed = centred * inverse
    return (normed * gain + offset, normed, inverse)


def norm_backward(upstream, normed, inverse, gain):
    scaled = upstream * gain
    return inverse * (
        scaled
        - jnp.mean(scaled, -1, keepdims=True)
        - normed * jnp.mean(scaled * normed, -1, keepdims=True)
    )


def received(own, r1, r2, r3):
    return own[...] + r1[...].astype(F32) + r2[...].astype(F32) + r3[...].astype(F32)


def norm_kernel(first, own, r1, r2, r3, residual, vec, value, low, normed, inverse):
    bias, gain, offset = rows_of(vec, *((1, 2, 3) if first else (4, 5, 6)))
    hidden = residual[...].astype(F32) + received(own, r1, r2, r3) + bias
    result, flat, scale = norm_forward(hidden, gain, offset)
    low[...] = result.astype(BF16)
    value[...] = result
    normed[...] = flat.astype(BF16)
    inverse[...] = scale


def sums(*values):
    return at_rows(8, [jnp.sum(v, 0, keepdims=True) for v in values])


def norm_back(grad, gain, normed, inverse, total, low, vectors):
    flat = normed.get()[...].astype(F32)
    value = norm_backward(grad, flat, inverse.get()[...], gain)
    rounded = value.astype(BF16)
    low[...] = rounded
    total[...] = value
    total.send()
    vectors[...] = sums(rounded.astype(F32), grad * flat, grad)


def norm_two_both_kernel(own, r1, r2, r3, residual, upstream, vec, low, total, low_grad, vectors):
    bias, gain, offset = rows_of(vec, 4, 5, 6)
    hidden = residual[...].astype(F32) + received(own, r1, r2, r3) + bias
    result, flat, scale = norm_forward(hidden, gain, offset)
    low[...] = result.astype(BF16)
    grad = upstream[...].astype(F32)
    value = norm_backward(grad, flat, scale, gain)
    rounded = value.astype(BF16)
    low_grad[...] = rounded
    total[...] = value
    total.send()
    vectors[...] = sums(rounded.astype(F32), grad * flat, grad)


def norm_two_back_sum_kernel(
    own, r1, r2, r3, vec, before, normed, inverse, total, low, vectors, given
):
    (gain,) = rows_of(vec, 5)
    rounded = (before.get()[...] + received(own, r1, r2, r3)).astype(BF16)
    norm_back(rounded.astype(F32), gain, normed, inverse, total, low, vectors)
    given[...] = rounded


def norm_one_back_kernel(own, r1, r2, r3, vec, before, normed, inverse, total, low, vectors):
    (gain,) = rows_of(vec, 2)
    grad = before.get()[...] + received(own, r1, r2, r3)
    norm_back(grad, gain, normed, inverse, total, low, vectors)


def last_sum_kernel(own, r1, r2, r3, before, given):
    given[...] = (before.get()[...] + received(own, r1, r2, r3)).astype(BF16)


def load_attn(own, other, weight, sems):
    return [
        pltpu.make_async_copy(
            ref.at[:, HALF * a : HALF * a + HALF], weight.at[a, :, half], sems.at[4 * half + a]
        )
        for half, ref in enumerate((own, other))
        for a in range(4)
    ]


def join(target, pieces, sems):
    copies = [
        pltpu.make_async_copy(piece, target.at[SHARE * i : SHARE * i + SHARE], sems.at[i])
        for i, piece in enumerate(pieces)
    ]
    for copy in copies:
        copy.start()
    return copies


def arrive(copies):
    for copy in copies:
        copy.wait()


def spread_out(value, where, own, parts):
    own[:, where] = value[0:SHARE]
    for i, part in enumerate(parts):
        part[:, where] = value[SHARE * (i + 1) : SHARE * (i + 2)].astype(BF16)


def by_share(left, right, own, parts):
    for i in (3, 2, 1, 0):
        value = dot_nn(left[SHARE * i : SHARE * i + SHARE], right)
        if i:
            parts[i - 1][...] = value.astype(BF16)
        else:
            own[...] = value


def attn_kernel(
    x0, x1, x2, x3, id_row, a_own, a_other,
    own, p1, p2, p3, qkv, probs, mixed, x_out, weight_out,
    small, sems, x_sems,
):
    weight, x_all = weight_out.buffer, x_out.buffer
    copies = load_attn(a_own, a_other, weight, sems)
    copies.append(pltpu.make_async_copy(a_own.at[:, 128:144], small, sems.at[8]))
    for copy in copies:
        copy.start()
    arrive(join(x_all, (x0, x1, x2, x3), x_sems))
    x_out.send()
    arrive(copies)
    weight_out.send()
    ids = id_row[...]
    id_column = jnp.broadcast_to(ids, (128, SEQ)).T[:, 0:1]
    biases = [small[z].astype(F32)[0:1] for z in range(4)]
    bias_of = (
        jnp.concatenate([b[:, 0:64] for b in biases], 1),
        None,
        jnp.concatenate([b[:, 64:128] for b in biases], 1),
    )
    x = x_all[...]
    for a in range(3):
        rows = dot_nt(x, weight[a].reshape(256, WIDE))
        if bias_of[a] is not None:
            rows = rows + bias_of[a]
        qkv[:, 256 * a : 256 * a + 256] = rows.astype(BF16)
    qkv.send()
    for c in range(2):
        q_rows = slice(256 * c, 256 * c + 256)
        allowed = id_column[q_rows] == ids
        for h in range(HEADS):
            query = qkv[q_rows, HD * h : HD * h + HD]
            key = qkv[:, 256 + HD * h : 256 + HD * h + HD]
            value = qkv[:, 512 + HD * h : 512 + HD * h + HD]
            scores = jnp.where(allowed, dot_nt(query, key) * HD ** (-0.5), NEGATIVE)
            exponent = jnp.exp(scores - jnp.max(scores, -1, keepdims=True))
            low = (exponent / jnp.sum(exponent, -1, keepdims=True)).astype(BF16)
            probs[h, q_rows] = low
            mixed[q_rows, HD * h : HD * h + HD] = dot_nn(low, value).astype(BF16)
    probs.send()
    mixed.send()
    by_share(mixed, weight[3].reshape(256, WIDE), own, (p1, p2, p3))


def attn_back_kernel(
    g0, g1, g2, g3, weight, qkv, probs, own, p1, p2, p3, d_rows, g_out, x_sems
):
    g_all = g_out.buffer
    arrive(join(g_all, (g0, g1, g2, g3), x_sems))
    g_out.send()
    weight, qkv, probs = weight.get(), qkv.get(), probs.get()
    d_mixed = dot_nt(g_all[...], weight[3].reshape(256, WIDE)).astype(BF16)
    scale = HD ** (-0.5)
    for h in range(HEADS):
        query = qkv[:, HD * h : HD * h + HD]
        key = qkv[:, 256 + HD * h : 256 + HD * h + HD]
        value = qkv[:, 512 + HD * h : 512 + HD * h + HD]
        grad = d_mixed[:, HD * h : HD * h + HD]
        d_key = jnp.zeros((SEQ, HD), F32)
        d_value = jnp.zeros((SEQ, HD), F32)
        for c in range(2):
            q_rows = slice(256 * c, 256 * c + 256)
            low = probs[h, q_rows]
            p = low.astype(F32)
            d_probs = dot_nt(grad[q_rows], value)
            inner = jnp.sum(p * d_probs, -1, keepdims=True)
            d_scores = (p * (d_probs - inner)).astype(BF16)
            d_rows[q_rows, HD * h : HD * h + HD] = (dot_nn(d_scores, key) * scale).astype(BF16)
            d_key = d_key + dot_tn(d_scores, query[q_rows])
            d_value = d_value + dot_tn(low, grad[q_rows])
        d_rows[:, 256 + HD * h : 256 + HD * h + HD] = (d_key * scale).astype(BF16)
        d_rows[:, 512 + HD * h : 512 + HD * h + HD] = d_value.astype(BF16)
    d_rows.send()
    by_share(d_rows, weight[0:3].reshape(768, WIDE), own, (p1, p2, p3))


def attn_weights_kernel(
    d_rows, mixed, x_all, g_all, vec_one, vec_two, feed_bias, own, other
):
    operands = (d_rows, mixed, x_all, g_all, vec_one, vec_two, feed_bias)
    d_rows, mixed, x_all, g_all, vec_one, vec_two, feed_bias = (
        operand.get() for operand in operands
    )
    for a in range(4):
        if a < 3:
            value = dot_tn(d_rows[:, 256 * a : 256 * a + 256], x_all[...])
        else:
            value = dot_tn(mixed[...], g_all[...])
        value = value.astype(BF16).reshape(4, 2, HALF, WIDE)
        own[:, HALF * a : HALF * a + HALF] = value[:, 0]
        other[:, HALF * a : HALF * a + HALF] = value[:, 1]
    total = jnp.sum(d_rows[...].astype(F32), 0, keepdims=True)
    one, two = vec_one[...], vec_two[...]
    vectors = [one[i : i + 1] for i in range(3)] + [two[i : i + 1] for i in range(3)]
    block = at_rows(16, [jnp.zeros((1, WIDE), F32)] + vectors)
    first_row = lax.broadcasted_iota(jnp.int32, (16, 128), 0) == 0
    for half, out in ((1, other), (0, own)):
        for z in range(4):
            start = HD * z + HALF * half
            bias = jnp.concatenate(
                [
                    total[:, start : start + HALF],
                    total[:, 512 + start : 512 + start + HALF],
                    jnp.zeros((1, 64), F32),
                ],
                1,
            )
            out[z, 128:144] = block.astype(BF16)
            out[z, 128:144, 0:128] = jnp.where(first_row, bias, block[:, 0:128]).astype(BF16)
            unit = 512 * half + 128 * z
            piece = jnp.where(first_row, feed_bias[0:1, unit : unit + 128], block[:, 128:256])
            out[z, 128:144, 128:256] = piece.astype(BF16)
        out.send()


def load_feed(ups, downs, up, down, sems):
    copies = []
    for i, (refs, target) in enumerate(((ups, up), (downs, down))):
        for half in range(2):
            copies.append(
                pltpu.make_async_copy(
                    refs[half],
                    target.at[4 * half : 4 * half + 4],
                    sems.at[2 * i + half],
                )
            )
    return copies[:2], copies[2:]


def feed_kernel(
    x0, x1, x2, x3, a_own, up_own, up_other, down_own, down_other,
    own, p1, p2, p3, active, slope, x_out, up_out, down_out,
    small, bias, sems, x_sems,
):
    x_all, up, down = x_out.buffer, up_out.buffer, down_out.buffer
    ups, downs = load_feed((up_own, up_other), (down_own, down_other), up, down, sems)
    copies = [pltpu.make_async_copy(a_own.at[:, 128:144], small, sems.at[4])] + ups
    for copy in copies + downs:
        copy.start()
    arrive(join(x_all, (x0, x1, x2, x3), x_sems))
    x_out.send()
    arrive(copies)
    up_out.send()
    for half in range(2):
        for z in range(4):
            unit = 512 * half + 128 * z
            bias[0:8, unit : unit + 128] = jnp.broadcast_to(
                small[z, :, 128 * (half + 1) : 128 * (half + 2)].astype(F32)[0:1], (8, 128)
            )

    def units(i, carry):
        block = up[pl.ds(2 * i, 2)].reshape(256, WIDE)
        hidden = dot_nt(x_all[...], block) + bias[0:1, columns(i)]
        share = 0.5 * (1.0 + lax.erf(hidden * (0.5 ** 0.5)))
        density = jnp.exp(-0.5 * hidden * hidden) * 0.3989422804014327
        active[:, columns(i)] = (hidden * share).astype(BF16)
        slope[:, columns(i)] = (share + hidden * density).astype(BF16)
        return carry

    lax.fori_loop(0, 4, units, 0)
    active.send()
    slope.send()
    arrive(downs)
    down_out.send()

    def features(n, carry):
        block = down[:, :, columns(n)].reshape(WIDE, 256)
        spread_out(dot_nn(active[...], block), columns(n), own, (p1, p2, p3))
        return carry

    lax.fori_loop(0, 4, features, 0)


def feed_back_kernel(
    g0, g1, g2, g3, down, slope, up, own, p1, p2, p3, d_hidden, g_out, x_sems
):
    g_all = g_out.buffer
    arrive(join(g_all, (g0, g1, g2, g3), x_sems))
    g_out.send()
    down, slope = down.get(), slope.get()

    def units(i, carry):
        block = down[pl.ds(2 * i, 2)].reshape(256, WIDE)
        value = dot_nt(g_all[...], block) * slope[:, columns(i)].astype(F32)
        d_hidden[:, columns(i)] = value.astype(BF16)
        return carry

    lax.fori_loop(0, 4, units, 0)
    d_hidden.send()
    up = up.get()

    def features(n, carry):
        block = up[:, :, columns(n)].reshape(WIDE, 256)
        spread_out(dot_nn(d_hidden[...], block), columns(n), own, (p1, p2, p3))
        return carry

    lax.fori_loop(0, 4, features, 0)


def feed_weights_kernel(
    d_hidden, active, x_all, g_all, up_own, up_other, down_own, down_other, bias
):
    d_hidden, active, x_all, g_all = (v.get() for v in (d_hidden, active, x_all, g_all))
    for half, up, down in ((1, up_other, down_other), (0, up_own, down_own)):

        def pair(i, carry, half=half, up=up, down=down):
            where = columns(2 * half + i)
            value = dot_tn(d_hidden[:, where], x_all[...]).astype(BF16)
            up[pl.ds(2 * i, 2)] = value.reshape(2, 128, WIDE)
            value = dot_tn(active[:, where], g_all[...]).astype(BF16)
            down[pl.ds(2 * i, 2)] = value.reshape(2, 128, WIDE)
            return carry

        lax.fori_loop(0, 2, pair, 0)
        up.send()
        down.send()
    bias[...] = sums(d_hidden[...].astype(F32))


def assemble_kernel(place, x0, x1, x2, x3, out):
    for r, piece in enumerate((x0, x1, x2, x3)):
        out[place[3] ^ r] = piece[...]


def core_sum_feed_kernel(place, up, down, up_got, down_got, up_out, down_out):
    down_out[...] = (down.get()[...].astype(F32) + down_got[...].astype(F32)).astype(BF16)
    up_out[...] = (up.get()[...].astype(F32) + up_got[...].astype(F32)).astype(BF16)


def split_kernel(place, own, received, *outs):
    own = own.get()
    for r, out in enumerate(outs):
        z = place[3] ^ r
        out[...] = (own[z].astype(F32) + received[z].astype(F32)).astype(BF16)


def core_sum_kernel(*refs):
    count = len(refs) // 3
    for own, received, out in zip(refs[:count], refs[count : 2 * count], refs[2 * count :]):
        out[...] = (own.get()[...].astype(F32) + received[...].astype(F32)).astype(BF16)
        out.send()


def ordered(place):
    return [
        (4 * c + r, ((r ^ place[1]) * 2 + (c ^ place[0])).astype(jnp.int32))
        for c in range(2)
        for r in range(4)
    ]


def gathered(pieces, place, target, sems):
    copies = [
        pltpu.make_async_copy(pieces[i], target.at[to], sems.at[i]) for i, to in ordered(place)
    ]
    for copy in copies:
        copy.start()
    arrive(copies)


def finish_attn_kernel(place, *refs):
    pieces, refs = refs[:8], refs[8:]
    gq, gk, gv, go, bias_query, bias_value, bias_up, *vectors, block, sems = refs
    gathered(pieces, place, block, sems)
    for a, out in enumerate((gq, gk, gv)):
        rows = block[:, HALF * a : HALF * a + HALF].reshape(256, WIDE)
        out[0] = rows.astype(F32).T
        out.send()
    go[0] = block[:, 3 * HALF : 4 * HALF].reshape(256, WIDE).astype(F32)
    go.send()
    small = [block[i, 128:144].astype(F32) for i in range(8)]
    bias_query[...] = jnp.concatenate([v[0:1, 0:HALF] for v in small], 1)
    bias_value[...] = jnp.concatenate([v[0:1, HALF : 2 * HALF] for v in small], 1)
    for i in range(8):
        bias_up[:, 128 * i : 128 * i + 128] = small[i][0:1, 128:256]
    total = 0.5 * sum(small[1:], small[0])
    for i, out in enumerate(vectors):
        out[...] = total[i + 1 : i + 2]


def finish_up_kernel(place, *refs):
    pieces, refs = refs[:8], refs[8:]
    out, block, sems = refs
    gathered(pieces, place, block, sems)
    for i in range(8):
        out[0, :, 128 * i : 128 * i + 128] = block[i].astype(F32).T


def finish_down_kernel(place, *refs):
    pieces, refs = refs[:8], refs[8:]
    out, block, sems = refs
    gathered(pieces, place, block, sems)
    for i in range(8):
        out[0, 128 * i : 128 * i + 128] = block[i].astype(F32)


def finish_tokens_kernel(place, a, b, out):
    is_first = place[2] == 0

    @pl.when(is_first)
    def _():
        out[0, 0] = a[...].astype(out.buffer.dtype)
        out[0, 1] = b[...].astype(out.buffer.dtype)

    @pl.when(jnp.logical_not(is_first))
    def _():
        out[0, 0] = b[...].astype(out.buffer.dtype)
        out[0, 1] = a[...].astype(out.buffer.dtype)


RAW = ["a"] * 4
WHOLE = shape((SEQ, WIDE))
BLOCKS = shape((8, 128, WIDE))
HEAD_ROWS = shape((4, 4, 2, HALF, WIDE))
TOKEN = shape((SHARE, WIDE))
WIDE_TOKEN = shape((SHARE, WIDE), F32)
ONE = shape((SHARE, 1), F32)
PARTS = [("v", WIDE_TOKEN)] + [("v", TOKEN)] * 3
ROW = shape((1, WIDE))
FOUR = DMA((4,))
MASK = shape((1, SEQ), F32)
VECTORS = shape((8, WIDE), F32)

prep_attn = call(
    prep_attn_kernel,
    "pack_attention",
    ["s"]
    + [shape((1, WIDE, 256))] * 3
    + [shape((1, 256, WIDE))]
    + [shape((1, 256))] * 2
    + [ROW] * 7,
    [("h", shape((ATTN, WIDE)))] * 2,
    [scratch((3, 256, WIDE))],
)
pick = call(
    pick_kernel,
    "pick",
    ["s"] + [shape((ATTN, WIDE))] * 2,
    [("h", shape((ATTN, WIDE)))],
)
prep_feed = call(
    prep_feed_kernel,
    "pack_feed",
    ["s", "r", "r"],
    [("h", shape((2 * FEED, WIDE)))] * 2,
    [scratch((2, WIDE, 128)), DMA((4,))],
)
norm_one, norm_two = (
    call(
        partial(norm_kernel, first),
        name,
        ["v"] * 6,
        [("v", WIDE_TOKEN), ("v", TOKEN), ("h", TOKEN), ("h", ONE)],
        )
    for first, name in ((True, "norm_one"), (False, "norm_two"))
)
BACKS = [("h", WIDE_TOKEN), ("v", TOKEN), ("h", VECTORS)]
norm_two_both = call(
    norm_two_both_kernel, "norm_two_both", ["v"] * 7, [("v", TOKEN)] + BACKS
)
norm_two_back_sum = call(
    norm_two_back_sum_kernel,
    "norm_two_back_sum",
    ["v"] * 5 + [WIDE_TOKEN, TOKEN, ONE],
    BACKS + [("h", TOKEN)],
)
norm_one_back = call(
    norm_one_back_kernel,
    "norm_one_back",
    ["v"] * 5 + [WIDE_TOKEN, TOKEN, ONE],
    BACKS,
)
last_sum = call(
    last_sum_kernel, "last_sum", ["v"] * 4 + [WIDE_TOKEN], [("h", TOKEN)]
)
attn_forward = call(
    attn_kernel,
    "attention",
    RAW + ["v", "r", "a"],
    PARTS
    + [
        ("h", shape((SEQ, 768))),
        ("h", shape((HEADS, SEQ, SEQ))),
        ("h", shape((SEQ, 256))),
        ("h", WHOLE),
        ("h", HEAD_ROWS),
    ],
    [scratch((4, 16, WIDE)), DMA((9,)), FOUR],
)
attn_backward = call(
    attn_back_kernel,
    "attention_back",
    RAW + [HEAD_ROWS, shape((SEQ, 768)), shape((HEADS, SEQ, SEQ))],
    PARTS + [("h", shape((SEQ, 768))), ("h", WHOLE)],
    [FOUR],
)
attn_weights = call(
    attn_weights_kernel,
    "attention_weights",
    [shape((SEQ, 768)), shape((SEQ, 256)), WHOLE, WHOLE] + [VECTORS] * 3,
    [("h", shape((4, ATTN, WIDE)))] * 2,
)
feed_forward = call(
    feed_kernel,
    "feed",
    RAW + ["r", "r", "a", "r", "a"],
    PARTS + [("h", WHOLE)] * 3 + [("h", BLOCKS)] * 2,
    [scratch((4, 16, WIDE)), scratch((8, WIDE), F32), DMA((5,)), FOUR],
)
feed_backward = call(
    feed_back_kernel,
    "feed_back",
    RAW + [BLOCKS, WHOLE, BLOCKS],
    PARTS + [("h", WHOLE)] * 2,
    [FOUR],
)
feed_weights = call(
    feed_weights_kernel,
    "feed_weights",
    [WHOLE] * 4,
    [("h", shape((4, FEED, WIDE)))] * 4 + [("h", VECTORS)],
)
FEED_HALVES = ["s", shape((4, FEED, WIDE)), shape((4, FEED, WIDE)), "v", "v"]
core_sum_feed = call(
    core_sum_feed_kernel,
    "core_sum_feed",
    FEED_HALVES,
    [("h", shape((4, FEED, WIDE))), ("h", shape((4, FEED, WIDE)))],
)
split_attn, split_down = (
    call(
        split_kernel,
        "core_split",
        ["s", shape((4, rows, WIDE)), "v"],
        [("v", shape((rows, WIDE)))] * 4,
    )
    for rows in (ATTN, FEED)
)
core_sum_up = call(
    core_sum_kernel,
    "core_sum_up",
    [shape((4, FEED, WIDE)), "v"],
    [("h", shape((4, FEED, WIDE)))],
)
assemble = call(
    assemble_kernel,
    "assemble",
    ["s"] + ["v"] * 4,
    [("h", shape((4, FEED, WIDE)))],
)
core_sum_attn = call(
    core_sum_kernel,
    "core_sum_attention",
    [shape((4, ATTN, WIDE)), "v"],
    [("h", shape((4, ATTN, WIDE)))],
)
EIGHT = DMA((8,))
finish_attn = call(
    finish_attn_kernel,
    "finish_attention",
    ["s"] + ["a"] * 8,
    [("h", shape((1, WIDE, 256), F32))] * 3
    + [("h", shape((1, 256, WIDE), F32))]
    + [("h", shape((1, 256), F32))] * 2
    + [("h", shape((1, WIDE), F32))] * 7,
    [scratch((8, ATTN, WIDE)), EIGHT],
)
finish_up = call(
    finish_up_kernel,
    "finish_up",
    ["s"] + ["a"] * 8,
    [("h", shape((1, WIDE, WIDE), F32))],
    [scratch((8, FEED, WIDE)), EIGHT],
)
finish_down = call(
    finish_down_kernel,
    "finish_down",
    ["s"] + ["a"] * 8,
    [("h", shape((1, WIDE, WIDE), F32))],
    [scratch((8, FEED, WIDE)), EIGHT],
)
finish_tokens, finish_grads = (
    call(
        finish_tokens_kernel,
        name,
        ["s", "v", "v"],
        [("h", shape((1, 2, SHARE, WIDE), dtype))],
    )
    for name, dtype in (("finish_tokens", BF16), ("finish_grads", F32))
)


def mover(sizes, target, takes=None):
    replicas, sections, shards = sizes
    pairs = []
    for d in range(replicas):
        for s in range(sections):
            for z in range(shards):
                if takes is None or takes(d, s, z):
                    nd, ns, nz = target(d, s, z)
                    pairs.append(
                        ((d * sections + s) * shards + z, (nd * sections + ns) * shards + nz)
                    )

    def move(values):
        return lax.ppermute(values, AXES, pairs)

    return move


def solution(mesh):
    replicas, sections, shards = (mesh.shape[name] for name in AXES)
    sizes = (replicas, sections, shards)

    def block_of(d, s):
        return 2 * ((d >> 1) & 1) + s

    def quarter_of(d, s, z):
        return (block_of(d, s) + z) % 4

    swap_y = mover(sizes, lambda d, s, z: (d, s ^ 1, z))
    swap_x = mover(sizes, lambda d, s, z: (d ^ 2, s, z))
    swap_xy = mover(sizes, lambda d, s, z: (d ^ 2, s ^ 1, z))
    swap_core = mover(sizes, lambda d, s, z: (d ^ 1, s, z))
    swap_z = [mover(sizes, lambda d, s, z, r=r: (d, s, z ^ r)) for r in range(1, 4)]
    def into_place(d, s, z):
        x = (d >> 1) & 1
        micro = s ^ ((z - x) & 1)
        plane = 2 * micro + x
        block = (z - plane) % 4
        return (d & ~2) | ((block >> 1) << 1), block & 1, plane

    place_in = mover(sizes, into_place)
    place_out = [
        mover(
            sizes,
            lambda d, s, z, r=r: (
                (d & ~2) | ((z & 1) << 1),
                (z >> 1) ^ r,
                quarter_of(d, s, z),
            ),
        )
        for r in range(2)
    ]

    def gather(share):
        return (share, swap_y(share), swap_x(share), swap_xy(share))

    def scatter(parts):
        own, p1, p2, p3 = parts
        return (own, swap_y(p1), swap_x(p2), swap_xy(p3))

    def gather_direct(place, piece):
        return assemble(place, piece, *[move(piece) for move in swap_z])[0]

    def gather_mp(piece):
        return lax.all_gather(piece, "mp", axis=0)

    def scatter_mp(pieces):
        return lax.psum_scatter(pieces, "mp", scatter_dimension=0)

    def to_layers(first, second):
        is_first = (lax.axis_index("mp") >> 1) == 0
        return (
            place_out[0](jnp.where(is_first, first, second)),
            place_out[1](jnp.where(is_first, second, first)),
        )

    def per_device(
        inputs,
        cotangent,
        doc_ids,
        w_query,
        b_query,
        w_key,
        w_value,
        b_value,
        w_out,
        b_out,
        gain_one,
        shift_one,
        w_up,
        b_up,
        w_down,
        b_down,
        gain_two,
        shift_two,
    ):
        replica = lax.axis_index("dp")
        section = lax.axis_index("section")
        shard = lax.axis_index("mp")
        core = replica & 1
        block = block_of(replica, section)
        place = jnp.stack([core, block, section, shard]).astype(jnp.int32)

        attn_own, attn_peer = prep_attn(
            place,
            w_query,
            w_key,
            w_value,
            w_out,
            b_query,
            b_value,
            b_up,
            b_out,
            gain_one,
            shift_one,
            b_down,
            gain_two,
            shift_two,
        )
        attn_got = swap_y(attn_peer)
        which = section ^ ((shard - ((replica >> 1) & 1)) & 1)
        share_in = place_in(lax.dynamic_index_in_dim(inputs, which, 0, False))
        other_ids = swap_x(doc_ids)
        (attn_zero,) = pick(place, attn_own, attn_got, share_in, other_ids)
        whole_in = gather(share_in)
        feed_own, feed_peer = prep_feed(
            place, w_up, w_down, attn_zero, stamp(*whole_in[1:])
        )
        feed_got = swap_y(feed_peer)

        def of_layer(layer, own, got):
            return jnp.where(section == layer, own, got)

        attn_zero = gather_mp(attn_zero)
        attn_zero = (attn_zero, swap_core(attn_zero))
        feed_packs = [of_layer(layer, feed_own, feed_got) for layer in range(2)]
        up_zero = gather_mp(feed_packs[0][:FEED])
        down_zero = gather_direct(place, feed_packs[0][FEED:])
        attn_one = gather_mp(of_layer(1, attn_own, attn_got))
        up_one = gather_mp(feed_packs[1][:FEED])
        down_one = gather_mp(feed_packs[1][FEED:])

        mine = ((replica >> 1) & 1) == (shard & 1)
        ids = jnp.where(mine, doc_ids, other_ids)
        ids = lax.dynamic_index_in_dim(ids, shard >> 1, 0, False).reshape(4, SHARE)
        ids = jnp.concatenate(
            [
                lax.dynamic_index_in_dim(ids, ((block ^ r) + shard) % 4, 0, False)
                for r in range(4)
            ]
        )
        id_row = ids.astype(F32)[None, :]

        def attn_half(share, whole, weights, vec, *after):
            *parts, qkv, probs, mixed, whole, weights = attn_forward(*whole, id_row, *weights, *after)
            parts = scatter(parts)
            middle, low, normed, inverse = norm_one(*parts, share, vec)
            return middle, low, (whole, qkv, probs, mixed, normed, inverse, weights)

        def feed_half(middle, spread, weights, vec, *after):
            *parts, active, slope, spread, up, down = feed_forward(*spread, *weights, *after)
            return scatter(parts), (spread, active, slope, up, down)

        vec_zero = attn_zero[0][0, 128:144]
        middle, low, kept_attn_zero = attn_half(share_in, whole_in, attn_zero, vec_zero)
        spread = gather(low)
        up_zero = hold(up_zero, kept_attn_zero[4])
        down_zero = hold(down_zero, stamp(*spread[1:]))
        feed_zero = (attn_zero[0], up_zero, swap_core(up_zero), down_zero, swap_core(down_zero))
        parts, kept_feed_zero = feed_half(middle, spread, feed_zero, vec_zero)
        _, first, *kept_norm_zero = norm_two(*parts, middle, vec_zero)

        whole = gather(first)
        attn_one = hold(attn_one, kept_norm_zero[0])
        vec_one = attn_one[0, 128:144]
        attn_one = (attn_one, swap_core(attn_one))
        middle, low, kept_attn_one = attn_half(first, whole, attn_one, vec_one)
        spread = gather(low)
        up_one = hold(up_one, kept_attn_one[4])
        down_one = hold(down_one, stamp(*spread[1:]))
        feed_one = (attn_one[0], up_one, swap_core(up_one), down_one, swap_core(down_one))
        grad_which = which ^ zero_after(kept_attn_zero[1])
        share_grad = place_in(lax.dynamic_index_in_dim(cotangent, grad_which, 0, False))
        parts, kept_feed_one = feed_half(middle, spread, feed_one, vec_one)
        second, total, low, vec_two = norm_two_both(*parts, middle, share_grad, vec_one)

        def feed_half_back(low, kept, *after):
            spread, active, slope, up, down = kept
            grads = gather(low)
            *parts, d_hidden, grads = feed_backward(*grads, down, slope, up, *after)
            parts = scatter(parts)
            return parts, feed_weights(d_hidden, active, spread, grads), d_hidden

        def attn_half_back(grads, kept, *after):
            _, qkv, probs, _, _, _, weights = kept
            *parts, d_rows, grads = attn_backward(*grads, weights, qkv, probs, *after)
            return parts, d_rows, grads

        def feed_sum(total, halves, start, *after):
            up, up_other, down, down_other, _ = halves
            received = [swap_core(hold(other, start)) for other in (up_other, down_other)]
            return total(place, up, down, *received, *after)

        parts, halves, _ = feed_half_back(low, kept_feed_one)
        feed_bias = halves[4]
        outputs = to_layers(first, second)
        total, low, vec_first = norm_one_back(
            *parts, vec_one, total, kept_attn_one[4], kept_attn_one[5], halves[0], *outputs
        )
        (section_outputs,) = finish_tokens(place, *outputs)
        grads = gather(low)
        halves = feed_sum(core_sum_feed, halves, total)
        ready = stamp(*grads[1:], kept=[halves[0]])
        parts, d_rows, grads = attn_half_back(grads, kept_attn_one, ready)
        parts = scatter(parts)
        up_grad_one, down_grad_one = [scatter_mp(hold(part, ready)) for part in halves]
        own, other = attn_weights(
            d_rows, kept_attn_one[3], kept_attn_one[0], grads, vec_first, vec_two, feed_bias
        )
        total, low, vec_two, grad_one = norm_two_back_sum(
            *parts, vec_zero, total, *kept_norm_zero, own, section_outputs
        )
        (attn_grad_one,) = core_sum_attn(own, swap_core(hold(other, total)))
        parts, halves, d_hidden = feed_half_back(
            low, kept_feed_zero, attn_grad_one, up_grad_one
        )
        attn_grad_one = hold(attn_grad_one, d_hidden)
        total, low, vec_first = norm_one_back(
            *parts,
            vec_zero,
            total,
            kept_attn_zero[4],
            kept_attn_zero[5],
            halves[0],
            down_grad_one,
        )
        grads = gather(low)
        attn_grad_one = scatter_mp(attn_grad_one)
        up, up_other, down, down_other, feed_bias = halves
        (up,) = core_sum_up(up, swap_core(hold(up_other, total)))
        ready = stamp(*grads[1:], kept=[up])
        parts, d_rows, grads = attn_half_back(grads, kept_attn_zero, ready, attn_grad_one)
        up_grad_zero = scatter_mp(hold(up, ready))
        own, other = attn_weights(
            d_rows,
            kept_attn_zero[3],
            kept_attn_zero[0],
            grads,
            vec_first,
            vec_two,
            feed_bias,
        )
        attn_parts = split_attn(place, own, swap_core(other))
        down_parts = split_down(place, down, swap_core(hold(down_other, total)))
        parts = scatter(parts[:1] + [hold(part, own) for part in parts[1:]])

        def scatter_direct(parts, *after):
            moved = [move(hold(part, *after)) for move, part in zip(swap_z, parts[1:])]
            total = sum((part.astype(F32) for part in moved), parts[0].astype(F32))
            return total.astype(BF16), stamp(*moved)

        (grad_zero,) = last_sum(*parts, total)
        down_grad_zero, _ = scatter_direct(down_parts, up_grad_zero)
        attn_grad_zero, attn_there = scatter_direct(attn_parts, up_grad_zero)
        def exchange(zero, one, *after, last=False):
            if replicas > 4:
                groups = [[low + 4 * high for high in range(replicas // 4)] for low in range(4)]
                zero, one = lax.psum((zero, one), "dp", axis_index_groups=groups)
            mine = jnp.where(section == 0, zero, one)
            theirs = jnp.where(section == 0, one, zero)
            if after:
                mine, theirs = hold(mine, *after), hold(theirs, *after)
            pieces = [mine, swap_y(theirs), swap_x(mine), swap_xy(theirs)]
            own = hold(mine, stamp(pieces[1])) if last else mine
            return pieces + [swap_core(piece) for piece in [own] + pieces[1:]]

        ups = exchange(up_grad_zero, up_grad_one, grad_zero)
        (g_up,) = finish_up(place, *ups)
        downs = exchange(down_grad_zero, down_grad_one)
        (g_down,) = finish_down(place, *downs)
        attns = exchange(attn_grad_zero, attn_grad_one, last=True)
        moved = to_layers(hold(grad_zero, attn_there), grad_one)
        (section_input_grads,) = finish_grads(place, *moved)
        g_query, g_key, g_value, g_out, g_b_query, g_b_value, g_b_up, *vectors = finish_attn(
            place, *attns, section_input_grads
        )
        return (
            section_outputs,
            section_input_grads,
            g_query,
            g_b_query,
            g_key,
            g_value,
            g_b_value,
            g_out,
            vectors[0],
            vectors[1],
            vectors[2],
            g_up,
            g_b_up,
            g_down,
            vectors[3],
            vectors[4],
            vectors[5],
        )

    vector = P("section", None)
    by_column = P("section", None, "mp")
    by_row = P("section", "mp", None)
    spread = P("section", "mp")
    tokens = P(None, ("dp", "mp"), None)
    layer_tokens = P("section", None, ("dp", "mp"), None)
    return jax.shard_map(
        per_device,
        mesh=mesh,
        in_specs=(
            tokens,
            tokens,
            P(None, "dp", None),
            by_column,
            spread,
            by_column,
            by_column,
            spread,
            by_row,
            vector,
            vector,
            vector,
            by_column,
            spread,
            by_row,
            vector,
            vector,
            vector,
        ),
        out_specs=(
            layer_tokens,
            layer_tokens,
            by_column,
            spread,
            by_column,
            by_column,
            spread,
            by_row,
            vector,
            vector,
            vector,
            by_column,
            spread,
            by_row,
            vector,
            vector,
            vector,
        ),
        check_vma=False,
    )
```
